32 devices in a mesh: dp: 8 (over z, core), fsdp: 4 (over y, x).
Axes of the slice: x: 2, y: 2, z: 4, core: 2. Of those that a mesh axis runs over, the one named last changes fastest.
Arguments:
- tokens: bfloat16 [4096, 768], P(('dp', 'fsdp')), may hold values from -6 to 6
- lengths: int32 [32, 4], P(('dp', 'fsdp')), may hold values from 0 to 128, as said below
- ln_attn_gain: bfloat16 [768], P(('dp', 'fsdp')), may hold values from 0.25 to 1.75
- ln_attn_bias: bfloat16 [768], P(('dp', 'fsdp')), may hold values from -3 to 3
- ln_mlp_gain: bfloat16 [768], P(('dp', 'fsdp')), may hold values from 0.25 to 1.75
- ln_mlp_bias: bfloat16 [768], P(('dp', 'fsdp')), may hold values from -3 to 3
- w_qkv: bfloat16 [768, 2304], P(('dp', 'fsdp')), may hold values from -0.21875 to 0.21875
- b_qkv: bfloat16 [2304], P(('dp', 'fsdp')), may hold values from -3 to 3
- w_out: bfloat16 [768, 768], P(('dp', 'fsdp')), may hold values from -0.875 to 0.875
- b_out: bfloat16 [768], P(('dp', 'fsdp')), may hold values from -3 to 3
- w_fc1: bfloat16 [768, 3072], P(('dp', 'fsdp')), may hold values from -0.21875 to 0.21875
- b_fc1: bfloat16 [3072], P(('dp', 'fsdp')), may hold values from -3 to 3
- w_fc2: bfloat16 [3072, 768], P(('dp', 'fsdp')), may hold values from -0.21875 to 0.21875
- b_fc2: bfloat16 [768], P(('dp', 'fsdp')), may hold values from -3 to 3
- cotangent: bfloat16 [4096, 768], P(('dp', 'fsdp')), may hold values from -6 to 6
Outputs:
- output: bfloat16 [4096, 768], P(('dp', 'fsdp'))
- grad_tokens: float32 [4096, 768], P(('dp', 'fsdp'))
- grad_ln_attn_gain: float32 [768], P(('dp', 'fsdp'))
- grad_ln_attn_bias: float32 [768], P(('dp', 'fsdp'))
- grad_ln_mlp_gain: float32 [768], P(('dp', 'fsdp'))
- grad_ln_mlp_bias: float32 [768], P(('dp', 'fsdp'))
- grad_w_qkv: float32 [768, 2304], P(('dp', 'fsdp'))
- grad_b_qkv: float32 [2304], P(('dp', 'fsdp'))
- grad_w_out: float32 [768, 768], P(('dp', 'fsdp'))
- grad_b_out: float32 [768], P(('dp', 'fsdp'))
- grad_w_fc1: float32 [768, 3072], P(('dp', 'fsdp'))
- grad_b_fc1: float32 [3072], P(('dp', 'fsdp'))
- grad_w_fc2: float32 [3072, 768], P(('dp', 'fsdp'))
- grad_b_fc2: float32 [768], P(('dp', 'fsdp'))
The draws below stay inside these ranges and needn't reach their ends.
Inputs may be any that keep to these rules, and one draw needn't show every extreme that they name: `lengths`: row d lists the sequences packed from the first row of device d in slot order, 0 for an unused slot; each row sums to at most 128; in every draw one device holds a single sequence of 128 tokens.
All inputs are finite; a program needn't handle non-finite values.
Results may differ from the reference program's by a relative error of at most 0.0092.
Values may be sent and summed in bfloat16 or wider, within the bound.
No kernel may reach another device: no remote copies, remote signals or barrier semaphores. Data moves between devices by JAX's collectives and lax.ppermute only.
A program may use at most 192 MiB of HBM per device.

```python
import jax
import jax.numpy as jnp
from jax import lax

D = 768
HEADS = 12
HEAD = 64
FF = 3072
ROT = 16
SEQ_SLOTS = 4
ROWS_DEV = 128
TOKENS = 4096
DEVICES = 32


def draw_lengths(key, part):
    key = jax.random.fold_in(key, 7)
    key_total, key_cuts, key_full = jax.random.split(key, 3)
    totals = jax.random.randint(key_total, (DEVICES,), ROWS_DEV // 4, ROWS_DEV + 1).astype(jnp.int32)
    cuts = jax.random.randint(key_cuts, (DEVICES, SEQ_SLOTS - 1), 0, ROWS_DEV + 1).astype(jnp.int32)
    cuts = jnp.sort(jnp.minimum(cuts, totals[:, None]), axis=1)
    bounds = jnp.concatenate([jnp.zeros((DEVICES, 1), jnp.int32), cuts, totals[:, None]], axis=1)
    seq_lengths = bounds[:, 1:] - bounds[:, :-1]
    chosen = jax.random.randint(key_full, (), 0, DEVICES)
    full_row = jnp.where(jnp.arange(SEQ_SLOTS) == 0, ROWS_DEV, 0).astype(jnp.int32)
    device_index = jnp.arange(DEVICES)
    seq_lengths = jnp.where((device_index == chosen)[:, None], full_row[None, :], seq_lengths)
    return seq_lengths.astype(jnp.int32)


def with_spikes(drawn, rng, source, target, parts, factor):
    owner, partner = [(jnp.arange(drawn.shape[axis_at]) // (drawn.shape[axis_at] // parts)).reshape([-1 if axis == axis_at else 1 for axis in range(drawn.ndim)]) for axis_at in (source, target)]
    chosen = jax.random.permutation(rng, parts)[partner]
    strong = (owner == chosen) | (owner == (partner + parts // 2) % parts)
    return jnp.where(strong, factor * drawn, drawn)


def levels(key, shape, shards, low, top_value):
    def one(dim, shards_of):
        heights = jax.random.uniform(jax.random.fold_in(jax.random.fold_in(key, 6), dim), (shards_of,), jnp.float32, low / len(shards), top_value / len(shards))
        return jnp.repeat(jnp.exp(heights), shape[dim] // shards_of).reshape((-1,) + (1,) * (len(shape) - dim - 1))

    level = one(*shards[0])
    for cut in shards[1:]:
        level = level * one(*cut)
    return level


def gaussian(own_key, dims, deviation, most, cuts=(), kind=jnp.bfloat16):
    array = jax.random.normal(own_key, dims, jnp.float32) * deviation
    if len(cuts) > 0:
        array = levels(own_key, dims, cuts, -0.22, 0.18) * array
    return jnp.clip(array, min=-most, max=most).astype(kind)


def heavy_noise(own_key, extent, width, reach, cuts, heavy, kind=jnp.bfloat16):
    values = width * jax.random.normal(own_key, extent, jnp.float32)
    if cuts:
        values = values * levels(own_key, extent, cuts, -0.22, 0.18)
    return jnp.clip(with_spikes(values, jax.random.fold_in(own_key, 3), *heavy), -reach, reach).astype(kind)


def setup_inputs(seed: int = 0) -> dict:
    key_of = jax.random.split(jax.random.key(seed), 16)
    return {
        "tokens": heavy_noise(key_of[0], (TOKENS, D), 1.0, 6.0, ((0, 32),), (0, 1, 32, 2.75)),
        "lengths": draw_lengths(jax.random.fold_in(key_of[15], 71), 0),
        "ln_attn_gain": jnp.clip(1.0 + 0.15 * jax.random.normal(key_of[2], (D,), jnp.float32), 0.25, 1.75).astype(jnp.bfloat16),
        "ln_attn_bias": gaussian(key_of[3], (D,), 0.3, 3.0, ((0, 32),)),
        "ln_mlp_gain": jnp.clip(1.0 + 0.15 * jax.random.normal(key_of[4], (D,), jnp.float32), 0.25, 1.75).astype(jnp.bfloat16),
        "ln_mlp_bias": gaussian(key_of[5], (D,), 0.3, 3.0, ((0, 32),)),
        "w_qkv": gaussian(key_of[6], (D, 3 * D), D ** -0.5, 0.21875, ((0, 32),)),
        "b_qkv": gaussian(key_of[7], (3 * D,), 0.5, 3.0, ((0, 32),)),
        "w_out": gaussian(key_of[8], (D, D), (D // 16) ** -0.5, 0.875, ((0, 32),)),
        "b_out": gaussian(key_of[9], (D,), 0.5, 3.0, ((0, 32),)),
        "w_fc1": gaussian(key_of[10], (D, FF), D ** -0.5, 0.21875, ((0, 32),)),
        "b_fc1": gaussian(key_of[11], (FF,), 0.5, 3.0, ((0, 32),)),
        "w_fc2": gaussian(key_of[12], (FF, D), (FF // 4) ** -0.5, 0.21875, ((0, 32),)),
        "b_fc2": gaussian(key_of[13], (D,), 0.5, 3.0, ((0, 32),)),
        "cotangent": heavy_noise(key_of[14], (TOKENS, D), 1.0, 6.0, ((0, 32),), (0, 1, 32, 2.75)),
    }


@jax.custom_vjp
def low(v):
    return lax.optimization_barrier(v.astype(jnp.bfloat16)).astype(jnp.float32)

@jax.custom_vjp
def low_back(v):
    return v

def low_keep(v):
    return (low(v), None)

def low_pass(kept, grad):
    return (grad,)

def back_keep(v):
    return (v, None)

def back_low(kept, grad):
    return (low(grad),)
low.defvjp(low_keep, low_pass)
low_back.defvjp(back_keep, back_low)
epsilon = 1e-05
highest = lax.Precision.HIGHEST
neg_large = -1e+30

def layout(seq_lengths):
    row_index = jnp.arange(ROWS_DEV, dtype=jnp.int32)
    seq_lengths = seq_lengths.astype(jnp.int32)
    ends = jnp.cumsum(seq_lengths).astype(jnp.int32)
    starts = ends - seq_lengths
    segment = lax.optimization_barrier(jnp.sum((row_index[:, None] >= ends[None, :]).astype(jnp.int32), axis=1)).astype(jnp.int32)
    live_rows = row_index < ends[-1]
    unique_seg = jnp.where(live_rows, segment, SEQ_SLOTS + row_index)
    slot_index = jnp.arange(SEQ_SLOTS, dtype=jnp.int32)
    first_row = lax.optimization_barrier(jnp.sum(jnp.where(segment[:, None] == slot_index[None, :], starts[None, :], 0), axis=1)).astype(jnp.int32)
    position = jnp.where(live_rows, row_index - first_row, 0)
    attn_mask = (unique_seg[:, None] == unique_seg[None, :]) & (row_index[None, :] <= row_index[:, None])
    half_rot = ROT // 2
    inverse_freq = 10000.0 ** (-(2.0 * jnp.arange(half_rot, dtype=jnp.float32)) / ROT)
    angle = position.astype(jnp.float32)[:, None] * inverse_freq[None, :]
    return (live_rows.astype(jnp.float32), attn_mask, jnp.cos(angle)[:, None, :], jnp.sin(angle)[:, None, :])

def layer_normalize(values_in, gain_vector, shift_vector):
    center = lax.optimization_barrier(jnp.mean(values_in, axis=-1, keepdims=True))
    mean_removed_input = values_in - center
    variance = lax.optimization_barrier(jnp.mean(mean_removed_input * mean_removed_input, axis=-1, keepdims=True))
    return mean_removed_input * lax.rsqrt(variance + epsilon) * gain_vector + shift_vector

def rotate(part, cosine, sine):
    half_rot = ROT // 2
    first = part[..., :half_rot]
    second = part[..., half_rot:ROT]
    return jnp.concatenate([first * cosine - second * sine, second * cosine + first * sine, part[..., ROT:]], axis=-1)

def layer(resid, params, live_rows, attn_mask, cosine, sine):
    gain_one, bias_one, gain_two, bias_two, mat_qkv, vec_qkv, mat_out, vec_out, mat_up, vec_up, mat_down, vec_down = params
    row_count = resid.shape[0]
    h_one = low(layer_normalize(resid, gain_one, bias_one))
    h_two = low(layer_normalize(resid, gain_two, bias_two))
    qkv = low_back(jnp.dot(h_one, mat_qkv, precision=highest) + vec_qkv)
    query_rows = qkv[:, :D].reshape(row_count, HEADS, HEAD)
    key_rows = qkv[:, D:2 * D].reshape(row_count, HEADS, HEAD)
    value_rows = qkv[:, 2 * D:].reshape(row_count, HEADS, HEAD)
    q_low = low(rotate(query_rows, cosine, sine))
    k_low = low(rotate(key_rows, cosine, sine))
    v_low = low(value_rows)
    scores = low_back(jnp.einsum('qhd,khd->hqk', q_low, k_low, precision=highest) * 0.125)
    scores = jnp.where(attn_mask[None], scores, neg_large)
    probs = low(jax.nn.softmax(scores, axis=-1))
    mixed = jnp.einsum('hqk,khd->qhd', probs, v_low, precision=highest).reshape(row_count, D)
    mixed = low(low_back(mixed))
    attn_branch = jnp.dot(mixed, mat_out, precision=highest) + vec_out
    up_rows = low_back(jnp.dot(h_two, mat_up, precision=highest) + vec_up)
    act_low = low(jax.nn.gelu(up_rows, approximate=False))
    mlp_branch = jnp.dot(act_low, mat_down, precision=highest) + vec_down
    return live_rows[:, None] * (resid + attn_branch + mlp_branch)

def reference(tokens, lengths, ln_attn_gain, ln_attn_bias, ln_mlp_gain, ln_mlp_bias, w_qkv, b_qkv, w_out, b_out, w_fc1, b_fc1, w_fc2, b_fc2, cotangent):
    params = tuple((item.astype(jnp.float32) for item in (ln_attn_gain, ln_attn_bias, ln_mlp_gain, ln_mlp_bias, w_qkv, b_qkv, w_out, b_out, w_fc1, b_fc1, w_fc2, b_fc2)))
    row_groups = tokens.astype(jnp.float32).reshape(DEVICES, ROWS_DEV, D)
    grad_groups = cotangent.astype(jnp.float32).reshape(DEVICES, ROWS_DEV, D)

    def step(carry, item):
        rows_in, grad_in, seq_lengths = item
        live_rows, attn_mask, cosine, sine = layout(seq_lengths)

        def forward(resid, weights):
            return layer(resid, weights, live_rows, attn_mask, cosine, sine)
        result, pull = jax.vjp(forward, rows_in, params)
        grad_rows, grad_params = pull(grad_in)
        summed = tuple((total + part for total, part in zip(carry, grad_params)))
        return (summed, (result.astype(jnp.bfloat16), grad_rows))
    zeros = tuple((jnp.zeros_like(item) for item in params))
    grads, (outputs, grad_rows) = lax.scan(step, zeros, (row_groups, grad_groups, lengths))
    return (outputs.reshape(TOKENS, D), grad_rows.reshape(TOKENS, D), grads[0], grads[1], grads[2], grads[3], grads[4], grads[5], grads[6], grads[7], grads[8], grads[9], grads[10], grads[11])
```

```python
import math

import jax
import jax.numpy as jnp
from jax import lax
from jax.sharding import Mesh
from jax.sharding import PartitionSpec as P

HEADS = 12
HEAD = 64
ROT = 16
TP = 4
BF = jnp.bfloat16
F32 = jnp.float32

epsilon = 1e-05
neg_large = -1e30
inv_sqrt_two = 1.0 / math.sqrt(2.0)
inv_sqrt_tau = 1.0 / math.sqrt(2.0 * math.pi)


def xor_pairs(count, bit):
    return [(i, i ^ bit) for i in range(count)]


def pick(array, index, axis=0):
    return lax.dynamic_index_in_dim(array, index, axis, keepdims=False)


def unxor(slots, rank):
    bit = 1
    while bit < len(slots):
        flip = (rank & bit) != 0
        slots = [jnp.where(flip, slots[k ^ bit], slots[k]) for k in range(len(slots))]
        bit *= 2
    return slots


def gather_t(block, rank):
    one = lax.ppermute(block, "t", xor_pairs(TP, 1))
    two = lax.ppermute(block, "t", xor_pairs(TP, 2))
    near = lax.ppermute(block, "t", [(1, 2), (2, 1)])
    far = lax.ppermute(two, "t", [(2, 3), (1, 0)])
    middle = (rank == 1) | (rank == 2)
    return [block, one, two, jnp.where(middle, near, far)]


def scatter_t(slots):
    low = [slot.astype(BF) for slot in slots]
    one = lax.ppermute(low[1], "t", xor_pairs(TP, 1))
    near = lax.ppermute(low[3], "t", [(1, 2), (2, 1)])
    relay = lax.ppermute(low[3], "t", [(0, 1), (3, 2)])
    two = lax.ppermute((slots[2] + relay.astype(F32)).astype(BF), "t", xor_pairs(TP, 2))
    return slots[0] + one.astype(F32) + near.astype(F32) + two.astype(F32)


def exchange_t(pieces):
    return [pieces[0]] + [
        lax.ppermute(pieces[k], "t", xor_pairs(TP, k)) for k in range(1, TP)
    ]


def gather_q(block, rank, sizes):
    if sizes != (2, 4):
        return lax.all_gather(block, ("dq", "fsdp"), axis=0, tiled=False)
    half = block.shape[0] // 2
    one = lax.ppermute(block, "fsdp", xor_pairs(4, 1))
    two = lax.ppermute(block, "fsdp", xor_pairs(4, 2))
    upper = lax.ppermute(one[:half], "fsdp", xor_pairs(4, 2))
    lower = lax.ppermute(two[half:], "fsdp", xor_pairs(4, 1))
    three = jnp.concatenate([upper, lower], axis=0)
    mine = [block, one, two, three]
    other = [lax.ppermute(part, "dq", xor_pairs(2, 1)) for part in mine]
    return jnp.stack(unxor(mine + other, rank))


def scatter_q(blocks, rank, sizes):
    if sizes != (2, 4):
        return lax.psum_scatter(
            blocks.astype(BF), ("dq", "fsdp"), scatter_dimension=0, tiled=False
        ).astype(F32)
    core, spot = rank // 4, rank % 4
    halves = blocks.reshape((2, 4) + blocks.shape[1:])
    keep = pick(halves, core)
    send = pick(halves, 1 - core).astype(BF)
    pair = keep + lax.ppermute(send, "dq", xor_pairs(2, 1)).astype(F32)
    mine, one, two, three = [pick(pair, spot ^ k) for k in range(4)]
    half = mine.shape[0] // 2
    three = three.astype(BF)
    upper = lax.ppermute(three[:half], "fsdp", xor_pairs(4, 1))
    lower = lax.ppermute(three[half:], "fsdp", xor_pairs(4, 2))
    two = jnp.concatenate([two[:half] + upper.astype(F32), two[half:]], axis=0)
    one = jnp.concatenate([one[:half], one[half:] + lower.astype(F32)], axis=0)
    one = lax.ppermute(one.astype(BF), "fsdp", xor_pairs(4, 1))
    two = lax.ppermute(two.astype(BF), "fsdp", xor_pairs(4, 2))
    return mine + one.astype(F32) + two.astype(F32)


def layout(seq_lengths, row_count):
    row_index = jnp.arange(row_count, dtype=jnp.int32)
    slot_count = seq_lengths.shape[0]
    ends = jnp.cumsum(seq_lengths)
    starts = ends - seq_lengths
    segment = jnp.sum((row_index[:, None] >= ends[None, :]).astype(jnp.int32), axis=1)
    live_rows = row_index < ends[-1]
    unique_seg = jnp.where(live_rows, segment, slot_count + row_index)
    slot_index = jnp.arange(slot_count, dtype=jnp.int32)
    first_row = jnp.sum(
        jnp.where(segment[:, None] == slot_index[None, :], starts[None, :], 0), axis=1
    )
    position = jnp.where(live_rows, row_index - first_row, 0)
    attn_mask = (unique_seg[:, None] == unique_seg[None, :]) & (
        row_index[None, :] <= row_index[:, None]
    )
    half_rot = ROT // 2
    inverse_freq = 10000.0 ** (-(2.0 * jnp.arange(half_rot, dtype=jnp.float32)) / ROT)
    angle = position.astype(jnp.float32)[:, None] * inverse_freq[None, :]
    return (
        live_rows.astype(jnp.float32),
        attn_mask,
        jnp.cos(angle)[:, None, :],
        jnp.sin(angle)[:, None, :],
    )


def rotate(part, cosine, sine):
    half_rot = ROT // 2
    first = part[..., :half_rot]
    second = part[..., half_rot:ROT]
    return jnp.concatenate(
        [first * cosine - second * sine, second * cosine + first * sine, part[..., ROT:]], axis=-1
    )


def contract(left, right, left_dim, right_dim):
    return lax.dot_general(
        left, right, (((left_dim,), (right_dim,)), ((), ())), preferred_element_type=F32
    )


def local(
    sizes,
    tokens,
    lengths,
    ln_attn_gain,
    ln_attn_bias,
    ln_mlp_gain,
    ln_mlp_bias,
    w_qkv,
    b_qkv,
    w_out,
    b_out,
    w_fc1,
    b_fc1,
    w_fc2,
    b_fc2,
    cotangent,
):
    t = lax.axis_index("t")
    q = lax.axis_index("dq") * sizes[1] + lax.axis_index("fsdp")
    qs = sizes[0] * sizes[1]
    rows, width = tokens.shape
    shard = w_qkv.shape[0]
    part = width // TP
    hidden = w_fc1.shape[1] // TP
    units = w_fc2.shape[0]
    heads = HEADS // TP

    vectors = jnp.concatenate(
        [
            item.reshape(shard, -1)
            for item in (
                ln_attn_gain, ln_attn_bias, ln_mlp_gain, ln_mlp_bias, b_qkv, b_out, b_fc1, b_fc2
            )
        ],
        axis=1,
    )
    n_vec = vectors.shape[1]
    low_lengths = jnp.broadcast_to(lengths.astype(BF), (shard, lengths.shape[1]))
    small = jnp.concatenate([vectors, low_lengths], axis=1)
    qkv_parts = w_qkv.reshape(shard, 3, TP, part)
    fc1_parts = w_fc1.reshape(shard, TP, hidden)
    pieces = [
        jnp.concatenate(
            [
                pick(qkv_parts, t ^ k, 2).reshape(shard, 3 * part),
                small,
                pick(fc1_parts, t ^ k, 1),
            ],
            axis=1,
        )
        for k in range(TP)
    ]
    pieces = exchange_t(pieces)
    at = 3 * part
    group_lengths = [piece[0, at + n_vec : at + n_vec + 4].astype(jnp.int32) for piece in pieces]
    mine = jnp.stack(unxor(pieces, t))
    columns = gather_q(mine, q, sizes)
    columns = columns.transpose(1, 0, 2, 3).reshape(width, -1)
    mat_qkv = columns[:, : 3 * part]
    vecs = columns[:, at : at + n_vec].astype(F32)
    mat_up = columns[:, at + small.shape[1] :]
    tail = gather_q(jnp.concatenate([w_fc2, w_out], axis=0), q, sizes)
    mat_down = tail[:, :units].reshape(qs * units, width)
    mat_out = tail[:, units:].reshape(part, width)

    vecs_t = vecs.T
    gain_one, bias_one, gain_two, bias_two = vecs_t[0], vecs_t[1], vecs_t[2], vecs_t[3]
    all_b_qkv = vecs[:, 4:7].reshape(3, TP, part)
    vec_qkv = pick(all_b_qkv, t, 1).reshape(3 * part)
    vec_out = vecs_t[7]
    vec_up = pick(vecs[:, 8:12].reshape(TP, hidden), t)
    vec_down = vecs_t[12]

    token_slots = gather_t(tokens, t)
    upstream_slots = gather_t(cotangent, t)
    layouts = [layout(item, rows) for item in group_lengths]
    live = jnp.concatenate([item[0] for item in layouts])[:, None]
    attn_mask = jnp.stack([item[1] for item in layouts])[:, None]
    cosine = jnp.concatenate([item[2] for item in layouts])
    sine = jnp.concatenate([item[3] for item in layouts])
    resid = jnp.concatenate(token_slots).astype(F32)
    upstream_low = jnp.concatenate(upstream_slots) * live.astype(BF)

    center = jnp.mean(resid, axis=-1, keepdims=True)
    removed = resid - center
    rstd = lax.rsqrt(jnp.mean(removed * removed, axis=-1, keepdims=True) + epsilon)
    xhat = removed * rstd
    low_one = (xhat * gain_one + bias_one).astype(BF)
    low_two = (xhat * gain_two + bias_two).astype(BF)

    up_rows = contract(low_two, mat_up, 1, 0) + vec_up
    phi = 0.5 * (1.0 + lax.erf(up_rows * inv_sqrt_two))
    act_low = (up_rows * phi).astype(BF)
    slope = phi + up_rows * jnp.exp(-0.5 * up_rows * up_rows) * inv_sqrt_tau
    mlp_share = contract(act_low, mat_down, 1, 0)
    grad_down = contract(act_low, upstream_low, 0, 0)
    d_up_low = (contract(upstream_low, mat_down, 1, 1) * slope).astype(BF)
    grad_up = contract(low_two, d_up_low, 0, 0)
    grad_up_bias = jnp.sum(d_up_low.astype(F32), axis=0)
    d_h2 = contract(d_up_low, mat_up, 1, 1)

    count = TP * rows
    qkv = (contract(low_one, mat_qkv, 1, 0) + vec_qkv).reshape(count, 3, heads, HEAD)
    q_low = rotate(qkv[:, 0], cosine, sine).astype(BF).reshape(TP, rows, heads, HEAD)
    k_low = rotate(qkv[:, 1], cosine, sine).astype(BF).reshape(TP, rows, heads, HEAD)
    v_low = qkv[:, 2].astype(BF).reshape(TP, rows, heads, HEAD)
    scores = jnp.einsum("gqhd,gkhd->ghqk", q_low, k_low, preferred_element_type=F32) * 0.125
    scores = jnp.where(attn_mask, scores, neg_large)
    exponent = jnp.exp(scores - jnp.max(scores, axis=-1, keepdims=True))
    probs = exponent / jnp.sum(exponent, axis=-1, keepdims=True)
    probs_low = probs.astype(BF)
    mixed = jnp.einsum("ghqk,gkhd->gqhd", probs_low, v_low, preferred_element_type=F32)
    mixed_low = mixed.reshape(count, part).astype(BF)
    out_share = (mlp_share + contract(mixed_low, mat_out, 1, 0)).reshape(TP, rows, width)
    out_sum = scatter_t([out_share[k] for k in range(TP)])
    output = live[:rows] * (resid[:rows] + out_sum + vec_out + vec_down)

    grad_out = contract(mixed_low, upstream_low, 0, 0)
    d_mixed = contract(upstream_low, mat_out, 1, 1).astype(BF).reshape(TP, rows, heads, HEAD)
    d_probs = jnp.einsum("gqhd,gkhd->ghqk", d_mixed, v_low, preferred_element_type=F32)
    d_values = jnp.einsum("ghqk,gqhd->gkhd", probs_low, d_mixed, preferred_element_type=F32)
    delta = jnp.sum(probs * d_probs, axis=-1, keepdims=True)
    d_scores = (probs * (d_probs - delta)).astype(BF)
    d_query = jnp.einsum("ghqk,gkhd->gqhd", d_scores, k_low, preferred_element_type=F32) * 0.125
    d_keys = jnp.einsum("ghqk,gqhd->gkhd", d_scores, q_low, preferred_element_type=F32) * 0.125
    d_query = rotate(d_query.reshape(count, heads, HEAD), cosine, -sine).reshape(count, part)
    d_keys = rotate(d_keys.reshape(count, heads, HEAD), cosine, -sine).reshape(count, part)
    d_qkv = jnp.concatenate([d_query, d_keys, d_values.reshape(count, part)], axis=1).astype(BF)
    grad_qkv = contract(low_one, d_qkv, 0, 0)
    grad_qkv_bias = jnp.sum(d_qkv.astype(F32), axis=0)
    d_h1 = contract(d_qkv, mat_qkv, 1, 1)

    e_share = (d_h1 * gain_one + d_h2 * gain_two).reshape(TP, rows, width)
    e_sum = scatter_t([e_share[k] for k in range(TP)])
    own_xhat = xhat[:rows]
    dx = rstd[:rows] * (
        e_sum
        - jnp.mean(e_sum, axis=-1, keepdims=True)
        - own_xhat * jnp.mean(e_sum * own_xhat, axis=-1, keepdims=True)
    )
    own_upstream = upstream_low[:rows].astype(F32)
    grad_tokens = own_upstream + dx

    zero_qkv = jnp.zeros((3, TP, part), F32)
    full_b_qkv = lax.dynamic_update_index_in_dim(
        zero_qkv, grad_qkv_bias.reshape(3, 1, part), t, 1
    ).reshape(width, 3)
    zero_up = jnp.zeros((TP, hidden), F32)
    full_b_up = lax.dynamic_update_index_in_dim(zero_up, grad_up_bias[None], t, 0).reshape(width, 4)
    lanes = jnp.stack(
        [
            jnp.sum(d_h1 * xhat, axis=0),
            jnp.sum(d_h1, axis=0),
            jnp.sum(d_h2 * xhat, axis=0),
            jnp.sum(d_h2, axis=0),
            jnp.sum(own_upstream, axis=0),
        ],
        axis=1,
    )
    vec_grads = jnp.concatenate([lanes, full_b_qkv, full_b_up], axis=1)

    tail_grads = jnp.concatenate(
        [grad_down.reshape(qs, units, width), grad_out.reshape(qs, shard, width)], axis=1
    )
    tail_sum = scatter_q(tail_grads, q, sizes)
    shard_down, shard_out = tail_sum[:units], tail_sum[units:]
    column_grads = jnp.concatenate([grad_qkv, vec_grads, grad_up], axis=1)
    column_grads = column_grads.reshape(TP, qs, shard, -1).transpose(1, 0, 2, 3)
    column_sum = scatter_q(column_grads, q, sizes)
    low_sum = column_sum.astype(BF)
    got = exchange_t([pick(low_sum, t ^ k) for k in range(TP)])
    got = [pick(column_sum, t)] + [item.astype(F32) for item in got[1:]]
    vec_sum = sum(item[:, at : at + 12] for item in got)
    got = jnp.stack(unxor(got, t))
    shard_qkv = (
        got[:, :, : 3 * part].reshape(TP, shard, 3, part).transpose(1, 2, 0, 3).reshape(shard, -1)
    )
    shard_up = got[:, :, at + 12 :].transpose(1, 0, 2).reshape(shard, -1)
    shard_branch_bias = vec_sum[:, 4]
    return (
        output.astype(BF),
        grad_tokens,
        vec_sum[:, 0],
        vec_sum[:, 1],
        vec_sum[:, 2],
        vec_sum[:, 3],
        shard_qkv,
        vec_sum[:, 5:8].reshape(-1),
        shard_out,
        shard_branch_bias,
        shard_up,
        vec_sum[:, 8:12].reshape(-1),
        shard_down,
        shard_branch_bias,
    )


def solution(mesh):
    nd, nf = mesh.shape["dp"], mesh.shape["fsdp"]
    sizes = (nd // TP, nf)
    inner = Mesh(mesh.devices.reshape((TP,) + sizes), ("t", "dq", "fsdp"))
    axes = ("t", "dq", "fsdp")
    matrix, vector = P(axes, None), P(axes)
    return jax.shard_map(
        lambda *args: local(sizes, *args),
        mesh=inner,
        in_specs=(
            matrix, matrix, vector, vector, vector, vector, matrix, vector,
            matrix, vector, matrix, vector, matrix, vector, matrix,
        ),
        out_specs=(
            matrix, matrix, vector, vector, vector, vector, matrix, vector,
            matrix, vector, matrix, vector, matrix, vector,
        ),
        check_vma=False,
    )
```

```python
import math

import jax
import jax.numpy as jnp
from jax import lax
from jax.experimental import pallas as pl
from jax.experimental.pallas import tpu as pltpu
from jax.sharding import Mesh
from jax.sharding import PartitionSpec as P

HEADS = 12
HEAD = 64
ROT = 16
TP = 4
BF = jnp.bfloat16
F32 = jnp.float32

epsilon = 1e-05
neg_large = -1e30
inv_sqrt_two = 1.0 / math.sqrt(2.0)
inv_sqrt_tau = 1.0 / math.sqrt(2.0 * math.pi)


def xor_pairs(count, bit):
    return [(i, i ^ bit) for i in range(count)]


def pick(array, index, axis=0):
    return lax.dynamic_index_in_dim(array, index, axis, keepdims=False)


def unxor(slots, rank):
    bit = 1
    while bit < len(slots):
        flip = (rank & bit) != 0
        slots = [jnp.where(flip, slots[k ^ bit], slots[k]) for k in range(len(slots))]
        bit *= 2
    return slots


def gather_t(block, rank):
    one = lax.ppermute(block, "t", xor_pairs(TP, 1))
    two = lax.ppermute(block, "t", xor_pairs(TP, 2))
    near = lax.ppermute(block, "t", [(1, 2), (2, 1)])
    far = lax.ppermute(two, "t", [(2, 3), (1, 0)])
    middle = (rank == 1) | (rank == 2)
    return [block, one, two, jnp.where(middle, near, far)]


def scatter_t(slots):
    low = [slot.astype(BF) for slot in slots]
    one = lax.ppermute(low[1], "t", xor_pairs(TP, 1))
    near = lax.ppermute(low[3], "t", [(1, 2), (2, 1)])
    relay = lax.ppermute(low[3], "t", [(0, 1), (3, 2)])
    two = lax.ppermute((slots[2] + relay.astype(F32)).astype(BF), "t", xor_pairs(TP, 2))
    return slots[0] + one.astype(F32) + near.astype(F32) + two.astype(F32)


def exchange_t(pieces):
    return [pieces[0]] + [
        lax.ppermute(pieces[k], "t", xor_pairs(TP, k)) for k in range(1, TP)
    ]


def gather_q(block, rank, sizes):
    if sizes != (2, 4):
        return lax.all_gather(block, ("dq", "fsdp"), axis=0, tiled=False)
    half = block.shape[0] // 2
    one = lax.ppermute(block, "fsdp", xor_pairs(4, 1))
    two = lax.ppermute(block, "fsdp", xor_pairs(4, 2))
    upper = lax.ppermute(one[:half], "fsdp", xor_pairs(4, 2))
    lower = lax.ppermute(two[half:], "fsdp", xor_pairs(4, 1))
    three = jnp.concatenate([upper, lower], axis=0)
    mine = [block, one, two, three]
    other = [lax.ppermute(part, "dq", xor_pairs(2, 1)) for part in mine]
    return jnp.stack(unxor(mine + other, rank))


def scatter_q(blocks, rank, sizes):
    if sizes != (2, 4):
        return lax.psum_scatter(
            blocks.astype(BF), ("dq", "fsdp"), scatter_dimension=0, tiled=False
        ).astype(F32)
    core, spot = rank // 4, rank % 4
    halves = blocks.reshape((2, 4) + blocks.shape[1:])
    keep = pick(halves, core)
    send = pick(halves, 1 - core).astype(BF)
    pair = keep + lax.ppermute(send, "dq", xor_pairs(2, 1)).astype(F32)
    mine, one, two, three = [pick(pair, spot ^ k) for k in range(4)]
    half = mine.shape[0] // 2
    three = three.astype(BF)
    upper = lax.ppermute(three[:half], "fsdp", xor_pairs(4, 1))
    lower = lax.ppermute(three[half:], "fsdp", xor_pairs(4, 2))
    two = jnp.concatenate([two[:half] + upper.astype(F32), two[half:]], axis=0)
    one = jnp.concatenate([one[:half], one[half:] + lower.astype(F32)], axis=0)
    one = lax.ppermute(one.astype(BF), "fsdp", xor_pairs(4, 1))
    two = lax.ppermute(two.astype(BF), "fsdp", xor_pairs(4, 2))
    return mine + one.astype(F32) + two.astype(F32)


def layout(seq_lengths, row_count):
    row_index = jnp.arange(row_count, dtype=jnp.int32)
    slot_count = seq_lengths.shape[0]
    ends = jnp.cumsum(seq_lengths)
    starts = ends - seq_lengths
    segment = jnp.sum((row_index[:, None] >= ends[None, :]).astype(jnp.int32), axis=1)
    live_rows = row_index < ends[-1]
    unique_seg = jnp.where(live_rows, segment, slot_count + row_index)
    slot_index = jnp.arange(slot_count, dtype=jnp.int32)
    first_row = jnp.sum(
        jnp.where(segment[:, None] == slot_index[None, :], starts[None, :], 0), axis=1
    )
    position = jnp.where(live_rows, row_index - first_row, 0)
    attn_mask = (unique_seg[:, None] == unique_seg[None, :]) & (
        row_index[None, :] <= row_index[:, None]
    )
    half_rot = ROT // 2
    inverse_freq = 10000.0 ** (-(2.0 * jnp.arange(half_rot, dtype=jnp.float32)) / ROT)
    angle = position.astype(jnp.float32)[:, None] * inverse_freq[None, :]
    return (
        live_rows.astype(jnp.float32),
        attn_mask,
        jnp.cos(angle)[:, None, :],
        jnp.sin(angle)[:, None, :],
    )


def rotate(part, cosine, sine):
    half_rot = ROT // 2
    first = part[..., :half_rot]
    second = part[..., half_rot:ROT]
    return jnp.concatenate(
        [first * cosine - second * sine, second * cosine + first * sine, part[..., ROT:]], axis=-1
    )


def contract(left, right, left_dim, right_dim):
    return lax.dot_general(
        left, right, (((left_dim,), (right_dim,)), ((), ())), preferred_element_type=F32
    )


ROWS = 128
COUNT = TP * ROWS
WIDTH = 768
SHARD = 24
LANES = 1408
QKV_AT = 768
VEC_AT = 1344
G_HEADS = HEADS // TP
QUARTER = WIDTH // TP
PARAMS = pltpu.CompilerParams(vmem_limit_bytes=48 * 1024 * 1024)


def iota(shape, axis):
    return lax.broadcasted_iota(jnp.int32, shape, axis)


def split(number, by):
    quotient = jnp.floor((number.astype(F32) + 0.5) * (1.0 / by)).astype(jnp.int32)
    return quotient, number - quotient * by


def hot(condition):
    return jnp.where(condition, 1.0, 0.0).astype(BF)


def owner_of_block(block, t, q):
    return ((block & 3) ^ t) * 8 + ((block >> 2) ^ q)


def feature_order(t, q):
    block, row = split(iota((1, WIDTH), 1), SHARD)
    return hot(iota((WIDTH, 1), 0) == owner_of_block(block, t, q) * SHARD + row)


def head_order(q):
    lane = iota((1, 256), 1)
    row = lane & 31
    place = ((lane >> 5) ^ q) * SHARD + row
    place = jnp.where(row < SHARD, place, -1)
    return hot(iota((QUARTER, 1), 0) == place)


def vector_rows():
    at = iota((160, 1), 0)
    return hot(iota((1, WIDTH), 1) == (at & 31) * SHARD + (at >> 5))


def dot(left, right, left_dim=1, right_dim=0):
    return lax.dot_general(
        left, right, (((left_dim,), (right_dim,)), ((), ())), preferred_element_type=F32
    )


def placing(number, length, owners):
    owner, element = split(number, length)
    return jnp.where(owners == owner, 1.0, 0.0), hot(iota((length, 1), 0) == element)


def all_places(t, q):
    block = iota((32, 1), 0)
    owners = owner_of_block(block, t, q)
    lane = iota((1, WIDTH), 1)
    third, rest = split(iota((1, 3 * QUARTER), 1), QUARTER)
    return (
        placing(lane, SHARD, block),
        placing(lane, SHARD, owners),
        placing(third * WIDTH + t * QUARTER + rest, 3 * SHARD, owners),
        placing(lane + t * WIDTH, 4 * SHARD, owners),
    )


def spread(values, places):
    mask, element = places
    return jnp.sum(dot(values.astype(BF), element) * mask, axis=0, keepdims=True)


def collect(row, places):
    mask, element = places
    return dot((mask * row).astype(BF), element, 1, 1)


def prepare_kernel(place, w_qkv, w_fc1, vector, *pieces):
    t = place[0]
    row = iota((SHARD, 64), 0)
    packed = jnp.zeros((SHARD, 64), F32)
    for i in range(5):
        packed = jnp.where(row == i, vector[:, 64 * i : 64 * i + 64], packed)
    packed = packed.astype(BF)
    for rank in range(TP):

        @pl.when(t == rank)
        def _(rank=rank):
            for k in range(TP):
                r = rank ^ k
                at = QUARTER * r
                pieces[k][:, :] = jnp.concatenate(
                    [
                        w_fc1[:, WIDTH * r : WIDTH * (r + 1)],
                        w_qkv[:, at : at + QUARTER],
                        w_qkv[:, WIDTH + at : WIDTH + at + QUARTER],
                        w_qkv[:, 2 * WIDTH + at : 2 * WIDTH + at + QUARTER],
                        packed,
                    ],
                    axis=1,
                )


def normalize_kernel(place, *refs):
    *slots, xhat, order = refs
    order[:, :] = feature_order(place[0], place[1])
    for k in range(TP):
        rows = dot(slots[k][:, :], order[:, :])
        removed = rows - jnp.mean(rows, axis=-1, keepdims=True)
        variance = jnp.mean(removed * removed, axis=-1, keepdims=True)
        xhat[ROWS * k : ROWS * (k + 1), :] = removed * lax.rsqrt(variance + epsilon)


def frequency_lanes():
    member = iota((1, 128), 1) & 7
    lanes = jnp.zeros((1, 128), F32)
    for i in range(ROT // 2):
        lanes = jnp.where(member == i, 10000.0 ** (-2.0 * i / ROT), lanes)
    return lanes


def turn(values, cosine, sine):
    member = iota((1, 384), 1) & 63
    ahead = pltpu.roll(values, 384 - ROT // 2, 1)
    behind = pltpu.roll(values, ROT // 2, 1)
    partner = jnp.where(member < ROT // 2, ahead, behind)
    return values * jnp.concatenate([cosine] * 3, axis=1) + partner * jnp.concatenate(
        [sine] * 3, axis=1
    )


def gathered_blocks(refs, rows):
    for core in range(2):
        own, pair, third = refs[3 * core : 3 * core + 3]
        yield 4 * core, own, 0
        yield 4 * core + 1, pair, 0
        yield 4 * core + 2, pair, rows
        yield 4 * core + 3, third, 0


def forward_kernel(place, xhat, *refs):
    columns, tails, cots = refs[:6], refs[6:12], refs[12:16]
    (
        mat, h_one, h_two, d_up, q_low, k_low, v_low, probs, d_mixed, gains, cosine, sine,
        out_zero, out_one, out_two, out_three, tail_keep, tail_send,
        down, out_mat, upstream, mixed, grad_down,
    ) = refs[16:]
    t, q = place[0], place[1]
    for kq, ref, at in gathered_blocks(columns, 96):
        mat[96 * kq : 96 * kq + 96, :] = ref[at : at + 96, :]
    for kq, ref, at in gathered_blocks(tails, 128):
        first = pl.multiple_of((q ^ kq) * 96, 32)
        down[pl.ds(first, 96), :] = ref[at : at + 96, :]
        out_mat[32 * kq : 32 * kq + 32, :] = ref[at + 96 : at + 128, :]

    slots, plain, of_qkv, of_up = all_places(t, q)
    packed = dot(vector_rows(), mat[:, VEC_AT:])
    vectors = jnp.concatenate([packed[32 * i : 32 * i + 32] for i in range(5)], axis=1)
    gain_one, bias_one, gain_two, bias_two = [
        spread(vectors[:, SHARD * i : SHARD * i + SHARD], slots) for i in range(4)
    ]
    vec_qkv = spread(vectors[:, 96:168], of_qkv)
    vec_up = spread(vectors[:, 192:288], of_up)
    vec_out = spread(vectors[:, 168:192], plain) + spread(vectors[:, 288:312], plain)
    gains[:, :] = jnp.concatenate([gain_one, gain_two, vec_out, jnp.zeros((5, WIDTH), F32)], axis=0)

    column = iota((1, ROWS), 1).astype(F32)
    line = iota((ROWS, 1), 0).astype(F32)
    masks = []
    for k in range(TP):
        end = jnp.zeros((1, 1), F32)
        segment_line, segment_column = jnp.zeros((ROWS, 1), F32), jnp.zeros((1, ROWS), F32)
        first_line = jnp.zeros((ROWS, 1), F32)
        for s in range(4):
            size = vectors[k : k + 1, 312 + s : 313 + s]
            end = end + size
            first_line = first_line + jnp.where(line >= end, size, 0.0)
            segment_line = segment_line + jnp.where(line >= end, 1.0, 0.0)
            segment_column = segment_column + jnp.where(column >= end, 1.0, 0.0)
        live = line < end
        masks.append(
            (line == column) | (live & (segment_line == segment_column) & (column <= line))
        )
        angle = jnp.where(live, line - first_line, 0.0) * frequency_lanes()
        member = iota((1, 128), 1) & 63
        at = slice(ROWS * k, ROWS * (k + 1))
        cosine[at, :] = jnp.where(member < ROT, jnp.cos(angle), 1.0)
        sine[at, :] = jnp.where(member < ROT, jnp.sin(angle), 0.0) * jnp.where(
            member < ROT // 2, -1.0, 1.0
        )
        upstream[at, :] = (cots[k][:, :].astype(F32) * jnp.where(live, 1.0, 0.0)).astype(BF)

    h_two[:, :] = (xhat[:, :] * gain_two + bias_two).astype(BF)
    up = dot(h_two[:, :], mat[:, :WIDTH]) + vec_up
    phi = 0.5 * (1.0 + lax.erf(up * inv_sqrt_two))
    act = (up * phi).astype(BF)
    slope = phi + up * jnp.exp(-0.5 * up * up) * inv_sqrt_tau
    share = dot(act, down[:, :])
    grad_down[:, :] = dot(act, upstream[:, :], 0, 0)
    d_up[:, :] = (dot(upstream[:, :], down[:, :], 1, 1) * slope).astype(BF)

    h_one[:, :] = (xhat[:, :] * gain_one + bias_one).astype(BF)
    qkv = dot(h_one[:, :], mat[:, QKV_AT:VEC_AT]) + vec_qkv
    turned = turn(qkv[:, : 2 * QUARTER], cosine[:, :], sine[:, :])
    q_low[:, :] = turned[:, :QUARTER].astype(BF)
    k_low[:, :] = turned[:, QUARTER:].astype(BF)
    v_low[:, :] = qkv[:, 2 * QUARTER :].astype(BF)
    for k in range(TP):
        at = slice(ROWS * k, ROWS * (k + 1))
        for head in range(G_HEADS):
            lanes = slice(HEAD * head, HEAD * (head + 1))
            scores = dot(q_low[at, lanes], k_low[at, lanes], 1, 1) * 0.125
            scores = jnp.where(masks[k], scores, neg_large)
            exponent = jnp.exp(scores - jnp.max(scores, axis=-1, keepdims=True))
            chances = exponent / jnp.sum(exponent, axis=-1, keepdims=True)
            probs[G_HEADS * k + head] = chances
            mixed[at, lanes] = dot(chances.astype(BF), v_low[at, lanes]).astype(BF)
    order = head_order(q)
    mixed_slots = dot(mixed[:, :], order).astype(BF)
    share = share + dot(mixed_slots, out_mat[:, :])
    out_zero[:, :] = share[:ROWS]
    out_one[:, :] = share[ROWS : 2 * ROWS].astype(BF)
    out_two[:, :] = share[2 * ROWS : 3 * ROWS]
    out_three[:, :] = share[3 * ROWS :].astype(BF)
    d_slots = dot(upstream[:, :], out_mat[:, :], 1, 1).astype(BF)
    d_mixed[:, :] = dot(d_slots, order, 1, 1).astype(BF)
    grad_out = dot(mixed_slots, upstream[:, :], 0, 0)
    for kq in range(8):
        target = tail_keep if kq < 4 else tail_send
        at = 128 * (kq % 4)
        first = pl.multiple_of((q ^ kq) * 96, 32)
        target[at : at + 96, :] = grad_down[pl.ds(first, 96), :].astype(target.dtype)
        target[at + 96 : at + 128, :] = grad_out[32 * kq : 32 * kq + 32].astype(target.dtype)


def backward_kernel(
    place, xhat, order, mat, h_one, h_two, d_up, q_low, k_low, v_low, probs, d_mixed, gains, cosine,
    sine, cot, live, e_zero, e_one, e_two, e_three, col_keep, col_send, d_turned, d_qkv,
):
    t, q = place[0], place[1]
    for k in range(TP):
        at = slice(ROWS * k, ROWS * (k + 1))
        for head in range(G_HEADS):
            lanes = slice(HEAD * head, HEAD * (head + 1))
            chances = probs[G_HEADS * k + head]
            d_out = d_mixed[at, lanes]
            d_probs = dot(d_out, v_low[at, lanes], 1, 1)
            delta = jnp.sum(chances * d_probs, axis=-1, keepdims=True)
            d_scores = (chances * (d_probs - delta)).astype(BF)
            d_turned[at, lanes] = dot(d_scores, k_low[at, lanes]) * 0.125
            d_turned[at, QUARTER + HEAD * head : QUARTER + HEAD * (head + 1)] = (
                dot(d_scores, q_low[at, lanes], 0, 0) * 0.125
            )
            d_qkv[at, 2 * QUARTER + HEAD * head : 2 * QUARTER + HEAD * (head + 1)] = dot(
                chances.astype(BF), d_out, 0, 0
            ).astype(BF)
    d_qkv[:, : 2 * QUARTER] = turn(d_turned[:, :], cosine[:, :], -sine[:, :]).astype(BF)

    d_one = dot(d_qkv[:, :], mat[:, QKV_AT:VEC_AT], 1, 1)
    d_two = dot(d_up[:, :], mat[:, :WIDTH], 1, 1)
    share = (d_one * gains[0:1, :] + d_two * gains[1:2, :]).astype(BF)
    share = dot(share, order[:, :], 1, 1)
    e_zero[:, :] = share[:ROWS]
    e_one[:, :] = share[ROWS : 2 * ROWS].astype(BF)
    e_two[:, :] = share[2 * ROWS : 3 * ROWS]
    e_three[:, :] = share[3 * ROWS :].astype(BF)

    slots, plain, of_qkv, of_up = all_places(t, q)

    def total(rows):
        return jnp.sum(rows, axis=0, keepdims=True)

    vectors = jnp.concatenate(
        [
            collect(total(d_one * xhat[:, :]), slots),
            collect(total(d_one), slots),
            collect(total(d_two * xhat[:, :]), slots),
            collect(total(d_two), slots),
            collect(total(cot[:, :].astype(F32) * live[:, :]), plain),
            collect(total(d_qkv[:, :].astype(F32)), of_qkv),
            collect(total(d_up[:, :].astype(F32)), of_up),
            jnp.zeros((32, 32), F32),
        ],
        axis=1,
    ).astype(BF)
    packed = jnp.concatenate([vectors[:, 64 * i : 64 * i + 64] for i in range(5)], axis=0)
    grads = jnp.concatenate(
        [
            dot(h_two[:, :], d_up[:, :], 0, 0),
            dot(h_one[:, :], d_qkv[:, :], 0, 0),
            dot(vector_rows(), packed, 0, 0),
        ],
        axis=1,
    )
    col_keep[:, :] = grads[:384]
    col_send[:, :] = grads[384:].astype(BF)


def columns_kernel(place, zero, one, two, three, qkv, up, *vectors):
    t = place[0]
    parts = [zero[:, :]] + [ref[:, :].astype(F32) for ref in (one, two, three)]
    for rank in range(TP):

        @pl.when(t == rank)
        def _(rank=rank):
            by_rank = [parts[rank ^ s] for s in range(TP)]
            up[:, :] = jnp.concatenate([item[:, :WIDTH] for item in by_rank], axis=1)
            qkv[:, :] = jnp.concatenate(
                [
                    item[:, QKV_AT + QUARTER * i : QKV_AT + QUARTER * (i + 1)]
                    for i in range(3)
                    for item in by_rank
                ],
                axis=1,
            )

    packed = sum(item[:8, VEC_AT:] for item in parts)
    row = jnp.concatenate([packed[i : i + 1] for i in range(5)], axis=1)
    at = 0
    for ref in vectors:
        size = ref.shape[1]
        ref[:, :] = row[:, at : at + size]
        at += size


def output_kernel(zero, one, two, three, tokens, live, gains, output):
    share = zero[:, :] + one[:, :].astype(F32) + two[:, :].astype(F32) + three[:, :].astype(F32)
    output[:, :] = (live[:, :] * (tokens[:, :].astype(F32) + share + gains[2:3, :])).astype(BF)


def input_kernel(zero, one, two, three, tokens, cot, live, grad):
    e = zero[:, :] + one[:, :].astype(F32) + two[:, :].astype(F32) + three[:, :].astype(F32)
    rows = tokens[:, :].astype(F32)
    removed = rows - jnp.mean(rows, axis=-1, keepdims=True)
    rstd = lax.rsqrt(jnp.mean(removed * removed, axis=-1, keepdims=True) + epsilon)
    xhat = removed * rstd
    dx = rstd * (
        e - jnp.mean(e, axis=-1, keepdims=True) - xhat * jnp.mean(e * xhat, axis=-1, keepdims=True)
    )
    grad[:, :] = cot[:, :].astype(F32) * live[:, :] + dx


def call(kernel, name, outs, *args, scratch=()):
    space = [pl.BlockSpec(memory_space=pltpu.VMEM)] * len(args)
    if args[0].dtype == jnp.int32:
        space[0] = pl.BlockSpec(memory_space=pltpu.SMEM)
    shapes = [jax.ShapeDtypeStruct(shape, kind) for shape, kind in outs]
    return pl.pallas_call(
        kernel,
        name=name,
        out_shape=shapes,
        in_specs=space,
        out_specs=[pl.BlockSpec(memory_space=pltpu.VMEM)] * len(shapes),
        scratch_shapes=[pltpu.VMEM(shape, kind) for shape, kind in scratch],
        compiler_params=PARAMS,
    )(*args)


def gather_plane(block):
    half = block.shape[0] // 2
    one = lax.ppermute(block, "fsdp", xor_pairs(4, 1))
    two = lax.ppermute(block, "fsdp", xor_pairs(4, 2))
    upper = lax.ppermute(one[:half], "fsdp", xor_pairs(4, 2))
    lower = lax.ppermute(two[half:], "fsdp", xor_pairs(4, 1))
    mine = [block, jnp.concatenate([one, two], axis=0), jnp.concatenate([upper, lower], axis=0)]
    return mine + [lax.ppermute(part, "dq", xor_pairs(2, 1)) for part in mine]


def scatter_plane(keep, send):
    rows = keep.shape[0] // 4
    half = rows // 2
    pair = keep + lax.ppermute(send, "dq", xor_pairs(2, 1)).astype(F32)
    mine, one, two, three = [pair[rows * k : rows * (k + 1)] for k in range(4)]
    three = three.astype(BF)
    upper = lax.ppermute(three[:half], "fsdp", xor_pairs(4, 1))
    lower = lax.ppermute(three[half:], "fsdp", xor_pairs(4, 2))
    two = jnp.concatenate([two[:half] + upper.astype(F32), two[half:]], axis=0)
    one = jnp.concatenate([one[:half], one[half:] + lower.astype(F32)], axis=0)
    one = lax.ppermute(one.astype(BF), "fsdp", xor_pairs(4, 1))
    two = lax.ppermute(two.astype(BF), "fsdp", xor_pairs(4, 2))
    return mine + one.astype(F32) + two.astype(F32)


def gather_rows(block):
    one = lax.ppermute(block, "t", xor_pairs(TP, 1))
    two = lax.ppermute(block, "t", xor_pairs(TP, 2))
    near = lax.ppermute(block, "t", [(1, 2), (2, 1)])
    far = lax.ppermute(two, "t", [(2, 3), (1, 0)])
    return [block, one, two, near + far]


def scatter_rows(one, two, three):
    relay = lax.ppermute(three, "t", [(0, 1), (3, 2)])
    near = lax.ppermute(three, "t", [(1, 2), (2, 1)])
    one = lax.ppermute(one, "t", xor_pairs(TP, 1))
    two = lax.ppermute((two + relay.astype(F32)).astype(BF), "t", xor_pairs(TP, 2))
    return one, two, near


def plane_local(
    tokens, lengths, ln_attn_gain, ln_attn_bias, ln_mlp_gain, ln_mlp_bias, w_qkv, b_qkv,
    w_out, b_out, w_fc1, b_fc1, w_fc2, b_fc2, cotangent,
):
    t = lax.axis_index("t")
    q = lax.axis_index("dq") * 4 + lax.axis_index("fsdp")
    place = jnp.stack([t, q]).astype(jnp.int32)
    live = jnp.where(iota((ROWS, 1), 0) < jnp.sum(lengths), 1.0, 0.0)
    vector = jnp.concatenate(
        [
            ln_attn_gain, ln_attn_bias, ln_mlp_gain, ln_mlp_bias, b_qkv, b_out, b_fc1, b_fc2,
            lengths[0].astype(BF), jnp.zeros((68,), BF),
        ]
    )
    pieces = call(
        prepare_kernel, "prepare", [((SHARD, LANES), BF)] * TP, place, w_qkv, w_fc1,
        vector.astype(F32)[None],
    )
    tail = gather_plane(jnp.concatenate([w_fc2, w_out, jnp.zeros((8, WIDTH), BF)], axis=0))
    columns = gather_plane(jnp.concatenate(exchange_t(pieces), axis=0))
    token_slots = gather_rows(tokens)
    cot_slots = gather_rows(cotangent)
    wide = (COUNT, WIDTH)
    xhat, order = call(
        normalize_kernel, "normalize", [(wide, F32), ((WIDTH, WIDTH), BF)], place, *token_slots
    )
    third = (COUNT, QUARTER)
    block = (ROWS, WIDTH)
    (
        mat, h_one, h_two, d_up, q_low, k_low, v_low, probs, d_mixed, gains, cosine, sine,
        out_zero, out_one, out_two, out_three, tail_keep, tail_send,
    ) = call(
        forward_kernel,
        "forward",
        [
            ((WIDTH, LANES), BF), (wide, BF), (wide, BF), (wide, BF), (third, BF), (third, BF),
            (third, BF), ((HEADS, ROWS, ROWS), F32), (third, BF), ((8, WIDTH), F32),
            ((COUNT, 128), F32), ((COUNT, 128), F32),
            (block, F32), (block, BF), (block, F32), (block, BF), (wide, F32), (wide, BF),
        ],
        place, xhat, *columns, *tail, *cot_slots,
        scratch=[
            ((WIDTH, WIDTH), BF), ((256, WIDTH), BF), (wide, BF), (third, BF),
            ((WIDTH, WIDTH), F32),
        ],
    )
    out_arrived = scatter_rows(out_one, out_two, out_three)
    tail_sum = scatter_plane(tail_keep, tail_send)
    e_zero, e_one, e_two, e_three, col_keep, col_send = call(
        backward_kernel,
        "backward",
        [
            (block, F32), (block, BF), (block, F32), (block, BF),
            ((384, LANES), F32), ((384, LANES), BF),
        ],
        place, xhat, order, mat, h_one, h_two, d_up, q_low, k_low, v_low, probs, d_mixed, gains,
        cosine, sine, cotangent, live,
        scratch=[((COUNT, 2 * QUARTER), F32), ((COUNT, 3 * QUARTER), BF)],
    )
    e_arrived = scatter_rows(e_one, e_two, e_three)
    col_sum = scatter_plane(col_keep, col_send)
    low_sum = col_sum.astype(BF)
    arrived = exchange_t([low_sum[SHARD * k : SHARD * (k + 1)] for k in range(TP)])
    (output,) = call(
        output_kernel, "output", [(block, BF)], out_zero, *out_arrived, tokens, live, gains
    )
    (grad_tokens,) = call(
        input_kernel, "input_gradient", [(block, F32)], e_zero, *e_arrived, tokens, cotangent, live
    )
    sizes = [SHARD] * 5 + [3 * SHARD, 4 * SHARD]
    shard_qkv, shard_up, *vectors = call(
        columns_kernel, "columns",
        [((SHARD, 3 * WIDTH), F32), ((SHARD, 4 * WIDTH), F32)] + [((1, n), F32) for n in sizes],
        place, col_sum[:SHARD], *arrived[1:],
    )
    g_one, b_one, g_two, b_two, branch, qkv_bias, up_bias = [item[0] for item in vectors]
    return (
        output, grad_tokens, g_one, b_one, g_two, b_two, shard_qkv, qkv_bias,
        tail_sum[96 : 96 + SHARD], branch, shard_up, up_bias, tail_sum[:96], branch,
    )


def local(
    sizes,
    tokens,
    lengths,
    ln_attn_gain,
    ln_attn_bias,
    ln_mlp_gain,
    ln_mlp_bias,
    w_qkv,
    b_qkv,
    w_out,
    b_out,
    w_fc1,
    b_fc1,
    w_fc2,
    b_fc2,
    cotangent,
):
    if sizes == (2, 4) and w_qkv.shape == (SHARD, 3 * WIDTH) and tokens.shape == (ROWS, WIDTH):
        return plane_local(
            tokens, lengths, ln_attn_gain, ln_attn_bias, ln_mlp_gain, ln_mlp_bias, w_qkv, b_qkv,
            w_out, b_out, w_fc1, b_fc1, w_fc2, b_fc2, cotangent,
        )
    t = lax.axis_index("t")
    q = lax.axis_index("dq") * sizes[1] + lax.axis_index("fsdp")
    qs = sizes[0] * sizes[1]
    rows, width = tokens.shape
    shard = w_qkv.shape[0]
    part = width // TP
    hidden = w_fc1.shape[1] // TP
    units = w_fc2.shape[0]
    heads = HEADS // TP

    vectors = jnp.concatenate(
        [
            item.reshape(shard, -1)
            for item in (
                ln_attn_gain, ln_attn_bias, ln_mlp_gain, ln_mlp_bias, b_qkv, b_out, b_fc1, b_fc2
            )
        ],
        axis=1,
    )
    n_vec = vectors.shape[1]
    low_lengths = jnp.broadcast_to(lengths.astype(BF), (shard, lengths.shape[1]))
    small = jnp.concatenate([vectors, low_lengths], axis=1)
    qkv_parts = w_qkv.reshape(shard, 3, TP, part)
    fc1_parts = w_fc1.reshape(shard, TP, hidden)
    pieces = [
        jnp.concatenate(
            [
                pick(qkv_parts, t ^ k, 2).reshape(shard, 3 * part),
                small,
                pick(fc1_parts, t ^ k, 1),
            ],
            axis=1,
        )
        for k in range(TP)
    ]
    pieces = exchange_t(pieces)
    at = 3 * part
    group_lengths = [piece[0, at + n_vec : at + n_vec + 4].astype(jnp.int32) for piece in pieces]
    mine = jnp.stack(unxor(pieces, t))
    columns = gather_q(mine, q, sizes)
    columns = columns.transpose(1, 0, 2, 3).reshape(width, -1)
    mat_qkv = columns[:, : 3 * part]
    vecs = columns[:, at : at + n_vec].astype(F32)
    mat_up = columns[:, at + small.shape[1] :]
    tail = gather_q(jnp.concatenate([w_fc2, w_out], axis=0), q, sizes)
    mat_down = tail[:, :units].reshape(qs * units, width)
    mat_out = tail[:, units:].reshape(part, width)

    vecs_t = vecs.T
    gain_one, bias_one, gain_two, bias_two = vecs_t[0], vecs_t[1], vecs_t[2], vecs_t[3]
    all_b_qkv = vecs[:, 4:7].reshape(3, TP, part)
    vec_qkv = pick(all_b_qkv, t, 1).reshape(3 * part)
    vec_out = vecs_t[7]
    vec_up = pick(vecs[:, 8:12].reshape(TP, hidden), t)
    vec_down = vecs_t[12]

    token_slots = gather_t(tokens, t)
    upstream_slots = gather_t(cotangent, t)
    layouts = [layout(item, rows) for item in group_lengths]
    live = jnp.concatenate([item[0] for item in layouts])[:, None]
    attn_mask = jnp.stack([item[1] for item in layouts])[:, None]
    cosine = jnp.concatenate([item[2] for item in layouts])
    sine = jnp.concatenate([item[3] for item in layouts])
    resid = jnp.concatenate(token_slots).astype(F32)
    upstream_low = jnp.concatenate(upstream_slots) * live.astype(BF)

    center = jnp.mean(resid, axis=-1, keepdims=True)
    removed = resid - center
    rstd = lax.rsqrt(jnp.mean(removed * removed, axis=-1, keepdims=True) + epsilon)
    xhat = removed * rstd
    low_one = (xhat * gain_one + bias_one).astype(BF)
    low_two = (xhat * gain_two + bias_two).astype(BF)

    up_rows = contract(low_two, mat_up, 1, 0) + vec_up
    phi = 0.5 * (1.0 + lax.erf(up_rows * inv_sqrt_two))
    act_low = (up_rows * phi).astype(BF)
    slope = phi + up_rows * jnp.exp(-0.5 * up_rows * up_rows) * inv_sqrt_tau
    mlp_share = contract(act_low, mat_down, 1, 0)
    grad_down = contract(act_low, upstream_low, 0, 0)
    d_up_low = (contract(upstream_low, mat_down, 1, 1) * slope).astype(BF)
    grad_up = contract(low_two, d_up_low, 0, 0)
    grad_up_bias = jnp.sum(d_up_low.astype(F32), axis=0)
    d_h2 = contract(d_up_low, mat_up, 1, 1)

    count = TP * rows
    qkv = (contract(low_one, mat_qkv, 1, 0) + vec_qkv).reshape(count, 3, heads, HEAD)
    q_low = rotate(qkv[:, 0], cosine, sine).astype(BF).reshape(TP, rows, heads, HEAD)
    k_low = rotate(qkv[:, 1], cosine, sine).astype(BF).reshape(TP, rows, heads, HEAD)
    v_low = qkv[:, 2].astype(BF).reshape(TP, rows, heads, HEAD)
    scores = jnp.einsum("gqhd,gkhd->ghqk", q_low, k_low, preferred_element_type=F32) * 0.125
    scores = jnp.where(attn_mask, scores, neg_large)
    exponent = jnp.exp(scores - jnp.max(scores, axis=-1, keepdims=True))
    probs = exponent / jnp.sum(exponent, axis=-1, keepdims=True)
    probs_low = probs.astype(BF)
    mixed = jnp.einsum("ghqk,gkhd->gqhd", probs_low, v_low, preferred_element_type=F32)
    mixed_low = mixed.reshape(count, part).astype(BF)
    out_share = (mlp_share + contract(mixed_low, mat_out, 1, 0)).reshape(TP, rows, width)
    out_sum = scatter_t([out_share[k] for k in range(TP)])
    output = live[:rows] * (resid[:rows] + out_sum + vec_out + vec_down)

    grad_out = contract(mixed_low, upstream_low, 0, 0)
    d_mixed = contract(upstream_low, mat_out, 1, 1).astype(BF).reshape(TP, rows, heads, HEAD)
    d_probs = jnp.einsum("gqhd,gkhd->ghqk", d_mixed, v_low, preferred_element_type=F32)
    d_values = jnp.einsum("ghqk,gqhd->gkhd", probs_low, d_mixed, preferred_element_type=F32)
    delta = jnp.sum(probs * d_probs, axis=-1, keepdims=True)
    d_scores = (probs * (d_probs - delta)).astype(BF)
    d_query = jnp.einsum("ghqk,gkhd->gqhd", d_scores, k_low, preferred_element_type=F32) * 0.125
    d_keys = jnp.einsum("ghqk,gqhd->gkhd", d_scores, q_low, preferred_element_type=F32) * 0.125
    d_query = rotate(d_query.reshape(count, heads, HEAD), cosine, -sine).reshape(count, part)
    d_keys = rotate(d_keys.reshape(count, heads, HEAD), cosine, -sine).reshape(count, part)
    d_qkv = jnp.concatenate([d_query, d_keys, d_values.reshape(count, part)], axis=1).astype(BF)
    grad_qkv = contract(low_one, d_qkv, 0, 0)
    grad_qkv_bias = jnp.sum(d_qkv.astype(F32), axis=0)
    d_h1 = contract(d_qkv, mat_qkv, 1, 1)

    e_share = (d_h1 * gain_one + d_h2 * gain_two).reshape(TP, rows, width)
    e_sum = scatter_t([e_share[k] for k in range(TP)])
    own_xhat = xhat[:rows]
    dx = rstd[:rows] * (
        e_sum
        - jnp.mean(e_sum, axis=-1, keepdims=True)
        - own_xhat * jnp.mean(e_sum * own_xhat, axis=-1, keepdims=True)
    )
    own_upstream = upstream_low[:rows].astype(F32)
    grad_tokens = own_upstream + dx

    zero_qkv = jnp.zeros((3, TP, part), F32)
    full_b_qkv = lax.dynamic_update_index_in_dim(
        zero_qkv, grad_qkv_bias.reshape(3, 1, part), t, 1
    ).reshape(width, 3)
    zero_up = jnp.zeros((TP, hidden), F32)
    full_b_up = lax.dynamic_update_index_in_dim(zero_up, grad_up_bias[None], t, 0).reshape(width, 4)
    lanes = jnp.stack(
        [
            jnp.sum(d_h1 * xhat, axis=0),
            jnp.sum(d_h1, axis=0),
            jnp.sum(d_h2 * xhat, axis=0),
            jnp.sum(d_h2, axis=0),
            jnp.sum(own_upstream, axis=0),
        ],
        axis=1,
    )
    vec_grads = jnp.concatenate([lanes, full_b_qkv, full_b_up], axis=1)

    tail_grads = jnp.concatenate(
        [grad_down.reshape(qs, units, width), grad_out.reshape(qs, shard, width)], axis=1
    )
    tail_sum = scatter_q(tail_grads, q, sizes)
    shard_down, shard_out = tail_sum[:units], tail_sum[units:]
    column_grads = jnp.concatenate([grad_qkv, vec_grads, grad_up], axis=1)
    column_grads = column_grads.reshape(TP, qs, shard, -1).transpose(1, 0, 2, 3)
    column_sum = scatter_q(column_grads, q, sizes)
    low_sum = column_sum.astype(BF)
    got = exchange_t([pick(low_sum, t ^ k) for k in range(TP)])
    got = [pick(column_sum, t)] + [item.astype(F32) for item in got[1:]]
    vec_sum = sum(item[:, at : at + 12] for item in got)
    got = jnp.stack(unxor(got, t))
    shard_qkv = (
        got[:, :, : 3 * part].reshape(TP, shard, 3, part).transpose(1, 2, 0, 3).reshape(shard, -1)
    )
    shard_up = got[:, :, at + 12 :].transpose(1, 0, 2).reshape(shard, -1)
    shard_branch_bias = vec_sum[:, 4]
    return (
        output.astype(BF),
        grad_tokens,
        vec_sum[:, 0],
        vec_sum[:, 1],
        vec_sum[:, 2],
        vec_sum[:, 3],
        shard_qkv,
        vec_sum[:, 5:8].reshape(-1),
        shard_out,
        shard_branch_bias,
        shard_up,
        vec_sum[:, 8:12].reshape(-1),
        shard_down,
        shard_branch_bias,
    )


def solution(mesh):
    nd, nf = mesh.shape["dp"], mesh.shape["fsdp"]
    sizes = (nd // TP, nf)
    inner = Mesh(mesh.devices.reshape((TP,) + sizes), ("t", "dq", "fsdp"))
    axes = ("t", "dq", "fsdp")
    matrix, vector = P(axes, None), P(axes)
    return jax.shard_map(
        lambda *args: local(sizes, *args),
        mesh=inner,
        in_specs=(
            matrix, matrix, vector, vector, vector, vector, matrix, vector,
            matrix, vector, matrix, vector, matrix, vector, matrix,
        ),
        out_specs=(
            matrix, matrix, vector, vector, vector, vector, matrix, vector,
            matrix, vector, matrix, vector, matrix, vector,
        ),
        check_vma=False,
    )
```

```python
import math

import jax
import jax.numpy as jnp
from jax import lax
from jax.experimental import pallas as pl
from jax.experimental.pallas import tpu as pltpu
from jax.sharding import Mesh
from jax.sharding import PartitionSpec as P

HEADS = 12
HEAD = 64
ROT = 16
TP = 4
BF = jnp.bfloat16
F32 = jnp.float32

epsilon = 1e-05
neg_large = -1e30
inv_sqrt_two = 1.0 / math.sqrt(2.0)
inv_sqrt_tau = 1.0 / math.sqrt(2.0 * math.pi)


def xor_pairs(count, bit):
    return [(i, i ^ bit) for i in range(count)]


def pick(array, index, axis=0):
    return lax.dynamic_index_in_dim(array, index, axis, keepdims=False)


def unxor(slots, rank):
    bit = 1
    while bit < len(slots):
        flip = (rank & bit) != 0
        slots = [jnp.where(flip, slots[k ^ bit], slots[k]) for k in range(len(slots))]
        bit *= 2
    return slots


def gather_t(block, rank):
    one = lax.ppermute(block, "t", xor_pairs(TP, 1))
    two = lax.ppermute(block, "t", xor_pairs(TP, 2))
    near = lax.ppermute(block, "t", [(1, 2), (2, 1)])
    far = lax.ppermute(two, "t", [(2, 3), (1, 0)])
    middle = (rank == 1) | (rank == 2)
    return [block, one, two, jnp.where(middle, near, far)]


def scatter_t(slots):
    low = [slot.astype(BF) for slot in slots]
    one = lax.ppermute(low[1], "t", xor_pairs(TP, 1))
    near = lax.ppermute(low[3], "t", [(1, 2), (2, 1)])
    relay = lax.ppermute(low[3], "t", [(0, 1), (3, 2)])
    two = lax.ppermute((slots[2] + relay.astype(F32)).astype(BF), "t", xor_pairs(TP, 2))
    return slots[0] + one.astype(F32) + near.astype(F32) + two.astype(F32)


def exchange_t(pieces):
    return [pieces[0]] + [
        lax.ppermute(pieces[k], "t", xor_pairs(TP, k)) for k in range(1, TP)
    ]


def gather_q(block, rank, sizes):
    if sizes != (2, 4):
        return lax.all_gather(block, ("dq", "fsdp"), axis=0, tiled=False)
    half = block.shape[0] // 2
    one = lax.ppermute(block, "fsdp", xor_pairs(4, 1))
    two = lax.ppermute(block, "fsdp", xor_pairs(4, 2))
    upper = lax.ppermute(one[:half], "fsdp", xor_pairs(4, 2))
    lower = lax.ppermute(two[half:], "fsdp", xor_pairs(4, 1))
    three = jnp.concatenate([upper, lower], axis=0)
    mine = [block, one, two, three]
    other = [lax.ppermute(part, "dq", xor_pairs(2, 1)) for part in mine]
    return jnp.stack(unxor(mine + other, rank))


def scatter_q(blocks, rank, sizes):
    if sizes != (2, 4):
        return lax.psum_scatter(
            blocks.astype(BF), ("dq", "fsdp"), scatter_dimension=0, tiled=False
        ).astype(F32)
    core, spot = rank // 4, rank % 4
    halves = blocks.reshape((2, 4) + blocks.shape[1:])
    keep = pick(halves, core)
    send = pick(halves, 1 - core).astype(BF)
    pair = keep + lax.ppermute(send, "dq", xor_pairs(2, 1)).astype(F32)
    mine, one, two, three = [pick(pair, spot ^ k) for k in range(4)]
    half = mine.shape[0] // 2
    three = three.astype(BF)
    upper = lax.ppermute(three[:half], "fsdp", xor_pairs(4, 1))
    lower = lax.ppermute(three[half:], "fsdp", xor_pairs(4, 2))
    two = jnp.concatenate([two[:half] + upper.astype(F32), two[half:]], axis=0)
    one = jnp.concatenate([one[:half], one[half:] + lower.astype(F32)], axis=0)
    one = lax.ppermute(one.astype(BF), "fsdp", xor_pairs(4, 1))
    two = lax.ppermute(two.astype(BF), "fsdp", xor_pairs(4, 2))
    return mine + one.astype(F32) + two.astype(F32)


def layout(seq_lengths, row_count):
    row_index = jnp.arange(row_count, dtype=jnp.int32)
    slot_count = seq_lengths.shape[0]
    ends = jnp.cumsum(seq_lengths)
    starts = ends - seq_lengths
    segment = jnp.sum((row_index[:, None] >= ends[None, :]).astype(jnp.int32), axis=1)
    live_rows = row_index < ends[-1]
    unique_seg = jnp.where(live_rows, segment, slot_count + row_index)
    slot_index = jnp.arange(slot_count, dtype=jnp.int32)
    first_row = jnp.sum(
        jnp.where(segment[:, None] == slot_index[None, :], starts[None, :], 0), axis=1
    )
    position = jnp.where(live_rows, row_index - first_row, 0)
    attn_mask = (unique_seg[:, None] == unique_seg[None, :]) & (
        row_index[None, :] <= row_index[:, None]
    )
    half_rot = ROT // 2
    inverse_freq = 10000.0 ** (-(2.0 * jnp.arange(half_rot, dtype=jnp.float32)) / ROT)
    angle = position.astype(jnp.float32)[:, None] * inverse_freq[None, :]
    return (
        live_rows.astype(jnp.float32),
        attn_mask,
        jnp.cos(angle)[:, None, :],
        jnp.sin(angle)[:, None, :],
    )


def rotate(part, cosine, sine):
    half_rot = ROT // 2
    first = part[..., :half_rot]
    second = part[..., half_rot:ROT]
    return jnp.concatenate(
        [first * cosine - second * sine, second * cosine + first * sine, part[..., ROT:]], axis=-1
    )


def contract(left, right, left_dim, right_dim):
    return lax.dot_general(
        left, right, (((left_dim,), (right_dim,)), ((), ())), preferred_element_type=F32
    )


ROWS = 128
COUNT = TP * ROWS
WIDTH = 768
SHARD = 24
VEC_AT = 576
NARROW = 640
SCALE = 10**10
G_HEADS = HEADS // TP
QUARTER = WIDTH // TP


def iota(shape, axis):
    return lax.broadcasted_iota(jnp.int32, shape, axis)


def split(number, by):
    quotient = jnp.floor((number.astype(F32) + 0.5) * (1.0 / by)).astype(jnp.int32)
    return quotient, number - quotient * by


def hot(condition):
    return jnp.where(condition, 1.0, 0.0).astype(BF)


def owner_of_block(block, t, q):
    return ((block & 3) ^ t) * 8 + ((block >> 2) ^ q)


def feature_order(t, q):
    block, row = split(iota((1, WIDTH), 1), SHARD)
    return hot(iota((WIDTH, 1), 0) == owner_of_block(block, t, q) * SHARD + row)


def head_order(q):
    lane = iota((1, 256), 1)
    row = lane & 31
    place = ((lane >> 5) ^ q) * SHARD + row
    place = jnp.where(row < SHARD, place, -1)
    return hot(iota((QUARTER, 1), 0) == place)


def vector_rows():
    at = iota((160, 1), 0)
    return hot(iota((1, WIDTH), 1) == (at & 31) * SHARD + (at >> 5))


def dot(left, right, left_dim=1, right_dim=0):
    return lax.dot_general(
        left, right, (((left_dim,), (right_dim,)), ((), ())), preferred_element_type=F32
    )


def placing(number, length, owners):
    owner, element = split(number, length)
    return jnp.where(owners == owner, 1.0, 0.0), hot(iota((length, 1), 0) == element)


def all_places(t, q):
    block = iota((32, 1), 0)
    owners = owner_of_block(block, t, q)
    lane = iota((1, WIDTH), 1)
    third, rest = split(iota((1, 3 * QUARTER), 1), QUARTER)
    return (
        placing(lane, SHARD, block),
        placing(lane, SHARD, owners),
        placing(third * WIDTH + t * QUARTER + rest, 3 * SHARD, owners),
        placing(lane + t * WIDTH, 4 * SHARD, owners),
    )


def spread(values, places):
    mask, element = places
    return jnp.sum(dot(values.astype(BF), element) * mask, axis=0, keepdims=True)


def collect(row, places):
    mask, element = places
    return dot((mask * row).astype(BF), element, 1, 1)


def prepare_kernel(place, w_qkv, w_fc1, vector, tokens, *pieces):
    t = place[0]
    row = iota((SHARD, 64), 0)
    packed = jnp.zeros((SHARD, 64), F32)
    for i in range(5):
        packed = jnp.where(row == i, vector[:, 64 * i : 64 * i + 64], packed)
    packed = jnp.concatenate([packed.astype(BF), jnp.zeros((SHARD, 128), BF)], axis=1)
    pieces[1][48:, :] = tokens[:, :]
    pieces[2][48:, :] = tokens[:, :]
    for rank in range(TP):

        @pl.when(t == rank)
        def _(rank=rank):
            for k in range(TP):
                r = rank ^ k
                at = QUARTER * r
                lower = jnp.concatenate(
                    [
                        w_qkv[:, at : at + QUARTER],
                        w_qkv[:, WIDTH + at : WIDTH + at + QUARTER],
                        w_qkv[:, 2 * WIDTH + at : 2 * WIDTH + at + QUARTER],
                        packed,
                    ],
                    axis=1,
                )
                pieces[k][:48, :] = jnp.concatenate(
                    [w_fc1[:, WIDTH * r : WIDTH * (r + 1)], lower], axis=0
                )


def merge_kernel(zero, one, two, three, columns):
    parts = [ref[:48, :] for ref in (zero, one, two, three)]
    columns[:, :] = jnp.concatenate(
        [part[:SHARD] for part in parts] + [part[SHARD:] for part in parts], axis=0
    )


def normalize_kernel(place, *refs):
    *slots, xhat, order = refs
    order[:, :] = feature_order(place[0], place[1])
    for k in range(TP):
        first = 48 if slots[k].shape[0] == 48 + ROWS else 0
        rows = dot(slots[k][first : first + ROWS, :], order[:, :])
        removed = rows - jnp.mean(rows, axis=-1, keepdims=True)
        variance = jnp.mean(removed * removed, axis=-1, keepdims=True)
        xhat[ROWS * k : ROWS * (k + 1), :] = removed * lax.rsqrt(variance + epsilon)


def frequency_lanes():
    member = iota((1, 128), 1) & 7
    lanes = jnp.zeros((1, 128), F32)
    for i in range(ROT // 2):
        lanes = jnp.where(member == i, 10000.0 ** (-2.0 * i / ROT), lanes)
    return lanes


def turn(values, cosine, sine):
    member = iota((1, 384), 1) & 63
    ahead = pltpu.roll(values, 384 - ROT // 2, 1)
    behind = pltpu.roll(values, ROT // 2, 1)
    partner = jnp.where(member < ROT // 2, ahead, behind)
    return values * jnp.concatenate([cosine] * 3, axis=1) + partner * jnp.concatenate(
        [sine] * 3, axis=1
    )


def forward_kernel(place, xhat, *refs):
    columns = refs[:2]
    (
        mat_up, mat_qkv, h_one, h_two, act, slope, q_low, k_low, v_low, probs, mixed_slots, gains,
        cosine, sine, live, mixed,
    ) = refs[2:]
    t, q = place[0], place[1]
    for kq in range(8):
        ref, at = columns[kq // 4], 192 * (kq % 4)
        mat_up[96 * kq : 96 * kq + 96, :] = ref[at : at + 96, :]
        mat_qkv[96 * kq : 96 * kq + 96, :] = ref[at + 96 : at + 192, :NARROW]

    slots, plain, of_qkv, of_up = all_places(t, q)
    packed = dot(vector_rows(), mat_qkv[:, VEC_AT:])
    vectors = jnp.concatenate([packed[32 * i : 32 * i + 32] for i in range(5)], axis=1)
    gain_one, bias_one, gain_two, bias_two = [
        spread(vectors[:, SHARD * i : SHARD * i + SHARD], slots) for i in range(4)
    ]
    vec_qkv = spread(vectors[:, 96:168], of_qkv)
    vec_up = spread(vectors[:, 192:288], of_up)
    vec_out = spread(vectors[:, 168:192], plain) + spread(vectors[:, 288:312], plain)
    gains[:, :] = jnp.concatenate([gain_one, gain_two, vec_out, jnp.zeros((5, WIDTH), F32)], axis=0)

    column = iota((1, ROWS), 1).astype(F32)
    line = iota((ROWS, 1), 0).astype(F32)
    masks = []
    for k in range(TP):
        end = jnp.zeros((1, 1), F32)
        segment_line, segment_column = jnp.zeros((ROWS, 1), F32), jnp.zeros((1, ROWS), F32)
        first_line = jnp.zeros((ROWS, 1), F32)
        for s in range(4):
            size = vectors[k : k + 1, 312 + s : 313 + s]
            end = end + size
            first_line = first_line + jnp.where(line >= end, size, 0.0)
            segment_line = segment_line + jnp.where(line >= end, 1.0, 0.0)
            segment_column = segment_column + jnp.where(column >= end, 1.0, 0.0)
        lives = line < end
        masks.append(
            (line == column) | (lives & (segment_line == segment_column) & (column <= line))
        )
        angle = jnp.where(lives, line - first_line, 0.0) * frequency_lanes()
        member = iota((1, 128), 1) & 63
        at = slice(ROWS * k, ROWS * (k + 1))
        cosine[at, :] = jnp.where(member < ROT, jnp.cos(angle), 1.0)
        sine[at, :] = jnp.where(member < ROT, jnp.sin(angle), 0.0) * jnp.where(
            member < ROT // 2, -1.0, 1.0
        )
        live[at, :] = jnp.where(lives, 1.0, 0.0)

    h_two[:, :] = (xhat[:, :] * gain_two + bias_two).astype(BF)
    up = dot(h_two[:, :], mat_up[:, :]) + vec_up
    phi = 0.5 * (1.0 + lax.erf(up * inv_sqrt_two))
    act[:, :] = (up * phi).astype(BF)
    slope[:, :] = phi + up * jnp.exp(-0.5 * up * up) * inv_sqrt_tau

    h_one[:, :] = (xhat[:, :] * gain_one + bias_one).astype(BF)
    qkv = dot(h_one[:, :], mat_qkv[:, :VEC_AT]) + vec_qkv
    turned = turn(qkv[:, : 2 * QUARTER], cosine[:, :], sine[:, :])
    q_low[:, :] = turned[:, :QUARTER].astype(BF)
    k_low[:, :] = turned[:, QUARTER:].astype(BF)
    v_low[:, :] = qkv[:, 2 * QUARTER :].astype(BF)
    for k in range(TP):
        at = slice(ROWS * k, ROWS * (k + 1))
        for head in range(G_HEADS):
            lanes = slice(HEAD * head, HEAD * (head + 1))
            scores = dot(q_low[at, lanes], k_low[at, lanes], 1, 1) * 0.125
            scores = jnp.where(masks[k], scores, neg_large)
            exponent = jnp.exp(scores - jnp.max(scores, axis=-1, keepdims=True))
            chances = exponent / jnp.sum(exponent, axis=-1, keepdims=True)
            probs[G_HEADS * k + head] = chances
            mixed[at, lanes] = dot(chances.astype(BF), v_low[at, lanes]).astype(BF)
    mixed_slots[:, :] = dot(mixed[:, :], head_order(q)).astype(BF)


def share_kernel(place, act, mixed_slots, *refs):
    tails, down, out_mat, shares = refs[:2], refs[2], refs[3], refs[4:]
    q = place[1]
    for kq in range(8):
        ref, at = tails[kq // 4], 128 * (kq % 4)
        first = pl.multiple_of((q ^ kq) * 96, 32)
        down[pl.ds(first, 96), :] = ref[at : at + 96, :]
        out_mat[32 * kq : 32 * kq + 32, :] = ref[at + 96 : at + 128, :]
    total = dot(act[:, :], down[:, :]) + dot(mixed_slots[:, :], out_mat[:, :])
    for k in range(TP):
        shares[k][:, :] = total[ROWS * k : ROWS * (k + 1)].astype(shares[k].dtype)


def upstream_kernel(place, *refs):
    cots = refs[:4]
    (
        live, h_two, act, slope, mixed_slots, down, out_mat, d_up, d_mixed, keep, send,
        upstream, grad_down,
    ) = refs[4:]
    q = place[1]
    for k in range(TP):
        at = slice(ROWS * k, ROWS * (k + 1))
        last = cots[k].shape[0]
        upstream[at, :] = (cots[k][last - ROWS :, :].astype(F32) * live[at, :]).astype(BF)
    d_up[:, :] = (dot(upstream[:, :], down[:, :], 1, 1) * slope[:, :]).astype(BF)
    grad_up = dot(h_two[:, :], d_up[:, :], 0, 0)
    grad_down[:, :] = dot(act[:, :], upstream[:, :], 0, 0)
    grad_out = dot(mixed_slots[:, :], upstream[:, :], 0, 0)
    for kq in range(8):
        target = keep if kq < 4 else send
        at = 224 * (kq % 4)
        first = pl.multiple_of((q ^ kq) * 96, 32)
        target[at : at + 96, :] = grad_down[pl.ds(first, 96), :].astype(target.dtype)
        target[at + 96 : at + 128, :] = grad_out[32 * kq : 32 * kq + 32].astype(target.dtype)
        target[at + 128 : at + 224, :] = grad_up[96 * kq : 96 * kq + 96].astype(target.dtype)
    d_slots = dot(upstream[:, :], out_mat[:, :], 1, 1).astype(BF)
    d_mixed[:, :] = dot(d_slots, head_order(q), 1, 1).astype(BF)


def attention_kernel(
    q_low, k_low, v_low, probs, d_mixed, cosine, sine, d_qkv, d_turned
):
    for k in range(TP):
        at = slice(ROWS * k, ROWS * (k + 1))
        for head in range(G_HEADS):
            lanes = slice(HEAD * head, HEAD * (head + 1))
            chances = probs[G_HEADS * k + head]
            d_out = d_mixed[at, lanes]
            d_probs = dot(d_out, v_low[at, lanes], 1, 1)
            delta = jnp.sum(chances * d_probs, axis=-1, keepdims=True)
            d_scores = (chances * (d_probs - delta)).astype(BF)
            d_turned[at, lanes] = dot(d_scores, k_low[at, lanes]) * 0.125
            d_turned[at, QUARTER + HEAD * head : QUARTER + HEAD * (head + 1)] = (
                dot(d_scores, q_low[at, lanes], 0, 0) * 0.125
            )
            d_qkv[at, 2 * QUARTER + HEAD * head : 2 * QUARTER + HEAD * (head + 1)] = dot(
                chances.astype(BF), d_out, 0, 0
            ).astype(BF)
    d_qkv[:, : 2 * QUARTER] = turn(d_turned[:, :], cosine[:, :], -sine[:, :]).astype(BF)


def backward_kernel(
    place, xhat, order, mat_up, mat_qkv, h_one, d_up, d_qkv, gains, cot, live, *refs
):
    shares, (keep, send) = refs[:4], refs[4:]
    t, q = place[0], place[1]
    d_one = dot(d_qkv[:, :], mat_qkv[:, :VEC_AT], 1, 1)
    d_two = dot(d_up[:, :], mat_up[:, :], 1, 1)
    share = (d_one * gains[0:1, :] + d_two * gains[1:2, :]).astype(BF)
    share = dot(share, order[:, :], 1, 1)
    for k in range(TP):
        shares[k][:, :] = share[ROWS * k : ROWS * (k + 1)].astype(shares[k].dtype)

    slots, plain, of_qkv, of_up = all_places(t, q)

    def total(rows):
        return jnp.sum(rows, axis=0, keepdims=True)

    vectors = jnp.concatenate(
        [
            collect(total(d_one * xhat[:, :]), slots),
            collect(total(d_one), slots),
            collect(total(d_two * xhat[:, :]), slots),
            collect(total(d_two), slots),
            collect(total(cot[:, :].astype(F32) * live[:ROWS, :]), plain),
            collect(total(d_qkv[:, :].astype(F32)), of_qkv),
            collect(total(d_up[:, :].astype(F32)), of_up),
            jnp.zeros((32, 32), F32),
        ],
        axis=1,
    ).astype(BF)
    packed = jnp.concatenate([vectors[:, 64 * i : 64 * i + 64] for i in range(5)], axis=0)
    grads = jnp.concatenate(
        [dot(h_one[:, :], d_qkv[:, :], 0, 0), dot(vector_rows(), packed, 0, 0)], axis=1
    )
    keep[:, :] = grads[:384]
    send[:, :] = grads[384:].astype(BF)


def columns_kernel(place, zero, one, two, three, qkv, up, *vectors):
    t = place[0]
    parts = [zero[:, :]] + [ref[:, :].astype(F32) for ref in (one, two, three)]
    for rank in range(TP):

        @pl.when(t == rank)
        def _(rank=rank):
            by_rank = [parts[rank ^ s] for s in range(TP)]
            up[:, :] = jnp.concatenate([item[:, :WIDTH] for item in by_rank], axis=1)
            qkv[:, :] = jnp.concatenate(
                [
                    item[:, WIDTH + QUARTER * i : WIDTH + QUARTER * (i + 1)]
                    for i in range(3)
                    for item in by_rank
                ],
                axis=1,
            )

    packed = sum(item[:8, WIDTH + VEC_AT :] for item in parts)
    row = jnp.concatenate([packed[i : i + 1] for i in range(5)], axis=1)
    at = 0
    for ref in vectors[:-1]:
        size = ref.shape[1]
        ref[:, :] = row[:, at : at + size]
        at += size
    vectors[-1][:, :] = row[:, 4 * SHARD : 5 * SHARD]


def output_kernel(zero, one, two, three, tokens, live, gains, output):
    share = zero[:, :] + one[:, :].astype(F32) + two[:, :].astype(F32) + three[:, :].astype(F32)
    output[:, :] = (live[:, :] * (tokens[:, :].astype(F32) + share + gains[2:3, :])).astype(BF)


def input_kernel(zero, one, two, three, tokens, cot, live, grad):
    e = zero[:, :] + one[:, :].astype(F32) + two[:, :].astype(F32) + three[:, :].astype(F32)
    rows = tokens[:, :].astype(F32)
    removed = rows - jnp.mean(rows, axis=-1, keepdims=True)
    rstd = lax.rsqrt(jnp.mean(removed * removed, axis=-1, keepdims=True) + epsilon)
    xhat = removed * rstd
    dx = rstd * (
        e - jnp.mean(e, axis=-1, keepdims=True) - xhat * jnp.mean(e * xhat, axis=-1, keepdims=True)
    )
    grad[:, :] = cot[:, :].astype(F32) * live[:, :] + dx


def call(kernel, name, outs, *args, scratch=(), mib=16, us=1):
    space = [pl.BlockSpec(memory_space=pltpu.VMEM)] * len(args)
    if args[0].dtype == jnp.int32:
        space[0] = pl.BlockSpec(memory_space=pltpu.SMEM)
    shapes = [jax.ShapeDtypeStruct(shape, kind) for shape, kind in outs]
    return pl.pallas_call(
        kernel,
        name=name,
        out_shape=shapes,
        in_specs=space,
        out_specs=[pl.BlockSpec(memory_space=pltpu.VMEM)] * len(shapes),
        scratch_shapes=[pltpu.VMEM(shape, kind) for shape, kind in scratch],
        cost_estimate=pl.CostEstimate(flops=us * SCALE, transcendentals=0, bytes_accessed=us * SCALE // 1000),
        compiler_params=pltpu.CompilerParams(vmem_limit_bytes=mib * 1024 * 1024),
    )(*args)


def after(array, *others):
    return lax.optimization_barrier((array, others))[0]


def xor_permutes(block, axis, count):
    return [lax.ppermute(block, axis, xor_pairs(count, k)) for k in range(1, 4)]


def plane_pair(keep, send):
    return keep + lax.ppermute(send, "dq", xor_pairs(2, 1)).astype(F32)


def plane_relay(pair):
    rows = pair.shape[0] // 4
    three = pair[3 * rows :].astype(BF)
    upper = lax.ppermute(three[: rows // 2], "fsdp", xor_pairs(4, 1))
    lower = lax.ppermute(three[rows // 2 :], "fsdp", xor_pairs(4, 2))
    return upper, lower


def plane_last(pair, upper, lower):
    rows = pair.shape[0] // 4
    half = rows // 2
    mine, one, two = [pair[rows * k : rows * (k + 1)] for k in range(3)]
    two = jnp.concatenate([two[:half] + upper.astype(F32), two[half:]], axis=0)
    one = jnp.concatenate([one[:half], one[half:] + lower.astype(F32)], axis=0)
    one = lax.ppermute(one.astype(BF), "fsdp", xor_pairs(4, 1))
    two = lax.ppermute(two.astype(BF), "fsdp", xor_pairs(4, 2))
    return mine + one.astype(F32) + two.astype(F32)


def plane_local(
    tokens, lengths, ln_attn_gain, ln_attn_bias, ln_mlp_gain, ln_mlp_bias, w_qkv, b_qkv,
    w_out, b_out, w_fc1, b_fc1, w_fc2, b_fc2, cotangent,
):
    t = lax.axis_index("t")
    q = lax.axis_index("dq") * 4 + lax.axis_index("fsdp")
    place = jnp.stack([t, q]).astype(jnp.int32)
    live = jnp.where(iota((ROWS, 1), 0) < jnp.sum(lengths), 1.0, 0.0)
    vector = jnp.concatenate(
        [
            ln_attn_gain, ln_attn_bias, ln_mlp_gain, ln_mlp_bias, b_qkv, b_out, b_fc1, b_fc2,
            lengths[0].astype(BF), jnp.zeros((68,), BF),
        ]
    )
    block = (ROWS, WIDTH)
    piece = ((48, WIDTH), BF)
    tail = jnp.concatenate([w_fc2, w_out, jnp.zeros((8, WIDTH), BF)], axis=0)
    tail_one = lax.ppermute(tail, "fsdp", xor_pairs(4, 1))
    tail_two = lax.ppermute(tail, "fsdp", xor_pairs(4, 2))
    tail_three = lax.ppermute(after(tail, tail_one), "fsdp", xor_pairs(4, 3))
    piece_rows = ((48 + ROWS, WIDTH), BF)
    pieces = call(
        prepare_kernel, "prepare", [piece, piece_rows, piece_rows, piece],
        place, w_qkv, w_fc1, vector.astype(F32)[None], tokens,
    )
    pieces = exchange_t(pieces)
    token_one, token_two = pieces[1], pieces[2]
    (columns,) = call(merge_kernel, "merge", [((192, WIDTH), BF)], *pieces)
    columns = after(columns, tail_one, tail_two, tail_three)
    rows_three = lax.ppermute(
        after(jnp.concatenate([tokens, cotangent], axis=0), token_one), "t", xor_pairs(TP, 3)
    )
    arrived = xor_permutes(columns, "fsdp", 4)
    columns = jnp.concatenate([columns] + arrived, axis=0)
    columns = [columns, lax.ppermute(columns, "dq", xor_pairs(2, 1))]
    tail = jnp.concatenate([tail, tail_one, tail_two, tail_three], axis=0)
    tail = [tail, lax.ppermute(tail, "dq", xor_pairs(2, 1))]
    wide = (COUNT, WIDTH)
    xhat, order = call(
        normalize_kernel, "normalize", [(wide, F32), ((WIDTH, WIDTH), BF)],
        place, tokens, token_one, token_two, rows_three,
    )
    cot = after(cotangent, xhat)
    cot_slots = [lax.ppermute(cot, "t", xor_pairs(TP, k)) for k in (1, 2)] + [rows_three]
    third = (COUNT, QUARTER)
    (
        mat_up, mat_qkv, h_one, h_two, act, slope, q_low, k_low, v_low, probs, mixed_slots, gains,
        cosine, sine, lives,
    ) = call(
        forward_kernel,
        "forward",
        [
            ((WIDTH, WIDTH), BF), ((WIDTH, NARROW), BF),
            (wide, BF), (wide, BF), (wide, BF), (wide, F32), (third, BF), (third, BF),
            (third, BF), ((HEADS, ROWS, ROWS), F32), ((COUNT, 256), BF), ((8, WIDTH), F32),
            ((COUNT, 128), F32), ((COUNT, 128), F32), ((COUNT, 1), F32),
        ],
        place, xhat, *columns,
        scratch=[(third, BF)],
        us=8,
    )
    shares = [(block, F32)] + [(block, BF)] * 3
    down, out_mat, *out = call(
        share_kernel, "share", [((WIDTH, WIDTH), BF), ((256, WIDTH), BF)] + shares,
        place, act, mixed_slots, *tail,
        us=2,
    )
    out = exchange_t(out)
    d_up, d_mixed, tail_keep, tail_send = call(
        upstream_kernel,
        "upstream",
        [(wide, BF), (third, BF), ((896, WIDTH), F32), ((896, WIDTH), BF)],
        place, cotangent, *cot_slots, lives, h_two, act, slope, mixed_slots, down, out_mat,
        scratch=[(wide, BF), ((WIDTH, WIDTH), F32)],
        us=4,
    )
    tail_pair = plane_pair(tail_keep, tail_send)
    (d_qkv,) = call(
        attention_kernel, "attention", [((COUNT, 3 * QUARTER), BF)],
        q_low, k_low, v_low, probs, d_mixed, cosine, sine,
        scratch=[((COUNT, 2 * QUARTER), F32)],
        us=5,
    )
    d_qkv = after(d_qkv, tail_pair, out[1])
    tail_relay = plane_relay(tail_pair)
    *e, col_keep, col_send = call(
        backward_kernel,
        "backward",
        shares + [((384, NARROW), F32), ((384, NARROW), BF)],
        place, xhat, order, mat_up, mat_qkv, h_one, d_up, d_qkv, gains, cotangent, lives,
        us=4,
    )
    col_pair = plane_pair(col_keep, after(col_send, tail_relay, out[2:]))
    col_relay = plane_relay(col_pair)
    e = exchange_t([after(item, out, col_pair) for item in e])
    col_sum = plane_last(col_pair, *col_relay)
    tail_sum = plane_last(tail_pair, *tail_relay)
    col_sum = jnp.concatenate([tail_sum[128:], col_sum], axis=1)
    low_sum = col_sum.astype(BF)
    arrived = exchange_t([low_sum[SHARD * k : SHARD * (k + 1)] for k in range(TP)])
    (output,) = call(
        output_kernel, "output", [(block, BF)], *out, tokens, after(live, col_relay), gains
    )
    (grad_tokens,) = call(
        input_kernel, "input_gradient", [(block, F32)], *e, tokens, cotangent, live
    )
    sizes = [SHARD] * 5 + [3 * SHARD, 4 * SHARD, SHARD]
    shard_qkv, shard_up, *vectors = call(
        columns_kernel, "columns",
        [((SHARD, 3 * WIDTH), F32), ((SHARD, 4 * WIDTH), F32)] + [((1, n), F32) for n in sizes],
        place, col_sum[:SHARD], *arrived[1:],
    )
    g_one, b_one, g_two, b_two, branch, qkv_bias, up_bias, again = [item[0] for item in vectors]
    return (
        output, grad_tokens, g_one, b_one, g_two, b_two, shard_qkv, qkv_bias,
        tail_sum[96 : 96 + SHARD], branch, shard_up, up_bias, tail_sum[:96], again,
    )


def local(
    sizes,
    tokens,
    lengths,
    ln_attn_gain,
    ln_attn_bias,
    ln_mlp_gain,
    ln_mlp_bias,
    w_qkv,
    b_qkv,
    w_out,
    b_out,
    w_fc1,
    b_fc1,
    w_fc2,
    b_fc2,
    cotangent,
):
    if sizes == (2, 4) and w_qkv.shape == (SHARD, 3 * WIDTH) and tokens.shape == (ROWS, WIDTH):
        return plane_local(
            tokens, lengths, ln_attn_gain, ln_attn_bias, ln_mlp_gain, ln_mlp_bias, w_qkv, b_qkv,
            w_out, b_out, w_fc1, b_fc1, w_fc2, b_fc2, cotangent,
        )
    t = lax.axis_index("t")
    q = lax.axis_index("dq") * sizes[1] + lax.axis_index("fsdp")
    qs = sizes[0] * sizes[1]
    rows, width = tokens.shape
    shard = w_qkv.shape[0]
    part = width // TP
    hidden = w_fc1.shape[1] // TP
    units = w_fc2.shape[0]
    heads = HEADS // TP

    vectors = jnp.concatenate(
        [
            item.reshape(shard, -1)
            for item in (
                ln_attn_gain, ln_attn_bias, ln_mlp_gain, ln_mlp_bias, b_qkv, b_out, b_fc1, b_fc2
            )
        ],
        axis=1,
    )
    n_vec = vectors.shape[1]
    low_lengths = jnp.broadcast_to(lengths.astype(BF), (shard, lengths.shape[1]))
    small = jnp.concatenate([vectors, low_lengths], axis=1)
    qkv_parts = w_qkv.reshape(shard, 3, TP, part)
    fc1_parts = w_fc1.reshape(shard, TP, hidden)
    pieces = [
        jnp.concatenate(
            [
                pick(qkv_parts, t ^ k, 2).reshape(shard, 3 * part),
                small,
                pick(fc1_parts, t ^ k, 1),
            ],
            axis=1,
        )
        for k in range(TP)
    ]
    pieces = exchange_t(pieces)
    at = 3 * part
    group_lengths = [piece[0, at + n_vec : at + n_vec + 4].astype(jnp.int32) for piece in pieces]
    mine = jnp.stack(unxor(pieces, t))
    columns = gather_q(mine, q, sizes)
    columns = columns.transpose(1, 0, 2, 3).reshape(width, -1)
    mat_qkv = columns[:, : 3 * part]
    vecs = columns[:, at : at + n_vec].astype(F32)
    mat_up = columns[:, at + small.shape[1] :]
    tail = gather_q(jnp.concatenate([w_fc2, w_out], axis=0), q, sizes)
    mat_down = tail[:, :units].reshape(qs * units, width)
    mat_out = tail[:, units:].reshape(part, width)

    vecs_t = vecs.T
    gain_one, bias_one, gain_two, bias_two = vecs_t[0], vecs_t[1], vecs_t[2], vecs_t[3]
    all_b_qkv = vecs[:, 4:7].reshape(3, TP, part)
    vec_qkv = pick(all_b_qkv, t, 1).reshape(3 * part)
    vec_out = vecs_t[7]
    vec_up = pick(vecs[:, 8:12].reshape(TP, hidden), t)
    vec_down = vecs_t[12]

    token_slots = gather_t(tokens, t)
    upstream_slots = gather_t(cotangent, t)
    layouts = [layout(item, rows) for item in group_lengths]
    live = jnp.concatenate([item[0] for item in layouts])[:, None]
    attn_mask = jnp.stack([item[1] for item in layouts])[:, None]
    cosine = jnp.concatenate([item[2] for item in layouts])
    sine = jnp.concatenate([item[3] for item in layouts])
    resid = jnp.concatenate(token_slots).astype(F32)
    upstream_low = jnp.concatenate(upstream_slots) * live.astype(BF)

    center = jnp.mean(resid, axis=-1, keepdims=True)
    removed = resid - center
    rstd = lax.rsqrt(jnp.mean(removed * removed, axis=-1, keepdims=True) + epsilon)
    xhat = removed * rstd
    low_one = (xhat * gain_one + bias_one).astype(BF)
    low_two = (xhat * gain_two + bias_two).astype(BF)

    up_rows = contract(low_two, mat_up, 1, 0) + vec_up
    phi = 0.5 * (1.0 + lax.erf(up_rows * inv_sqrt_two))
    act_low = (up_rows * phi).astype(BF)
    slope = phi + up_rows * jnp.exp(-0.5 * up_rows * up_rows) * inv_sqrt_tau
    mlp_share = contract(act_low, mat_down, 1, 0)
    grad_down = contract(act_low, upstream_low, 0, 0)
    d_up_low = (contract(upstream_low, mat_down, 1, 1) * slope).astype(BF)
    grad_up = contract(low_two, d_up_low, 0, 0)
    grad_up_bias = jnp.sum(d_up_low.astype(F32), axis=0)
    d_h2 = contract(d_up_low, mat_up, 1, 1)

    count = TP * rows
    qkv = (contract(low_one, mat_qkv, 1, 0) + vec_qkv).reshape(count, 3, heads, HEAD)
    q_low = rotate(qkv[:, 0], cosine, sine).astype(BF).reshape(TP, rows, heads, HEAD)
    k_low = rotate(qkv[:, 1], cosine, sine).astype(BF).reshape(TP, rows, heads, HEAD)
    v_low = qkv[:, 2].astype(BF).reshape(TP, rows, heads, HEAD)
    scores = jnp.einsum("gqhd,gkhd->ghqk", q_low, k_low, preferred_element_type=F32) * 0.125
    scores = jnp.where(attn_mask, scores, neg_large)
    exponent = jnp.exp(scores - jnp.max(scores, axis=-1, keepdims=True))
    probs = exponent / jnp.sum(exponent, axis=-1, keepdims=True)
    probs_low = probs.astype(BF)
    mixed = jnp.einsum("ghqk,gkhd->gqhd", probs_low, v_low, preferred_element_type=F32)
    mixed_low = mixed.reshape(count, part).astype(BF)
    out_share = (mlp_share + contract(mixed_low, mat_out, 1, 0)).reshape(TP, rows, width)
    out_sum = scatter_t([out_share[k] for k in range(TP)])
    output = live[:rows] * (resid[:rows] + out_sum + vec_out + vec_down)

    grad_out = contract(mixed_low, upstream_low, 0, 0)
    d_mixed = contract(upstream_low, mat_out, 1, 1).astype(BF).reshape(TP, rows, heads, HEAD)
    d_probs = jnp.einsum("gqhd,gkhd->ghqk", d_mixed, v_low, preferred_element_type=F32)
    d_values = jnp.einsum("ghqk,gqhd->gkhd", probs_low, d_mixed, preferred_element_type=F32)
    delta = jnp.sum(probs * d_probs, axis=-1, keepdims=True)
    d_scores = (probs * (d_probs - delta)).astype(BF)
    d_query = jnp.einsum("ghqk,gkhd->gqhd", d_scores, k_low, preferred_element_type=F32) * 0.125
    d_keys = jnp.einsum("ghqk,gqhd->gkhd", d_scores, q_low, preferred_element_type=F32) * 0.125
    d_query = rotate(d_query.reshape(count, heads, HEAD), cosine, -sine).reshape(count, part)
    d_keys = rotate(d_keys.reshape(count, heads, HEAD), cosine, -sine).reshape(count, part)
    d_qkv = jnp.concatenate([d_query, d_keys, d_values.reshape(count, part)], axis=1).astype(BF)
    grad_qkv = contract(low_one, d_qkv, 0, 0)
    grad_qkv_bias = jnp.sum(d_qkv.astype(F32), axis=0)
    d_h1 = contract(d_qkv, mat_qkv, 1, 1)

    e_share = (d_h1 * gain_one + d_h2 * gain_two).reshape(TP, rows, width)
    e_sum = scatter_t([e_share[k] for k in range(TP)])
    own_xhat = xhat[:rows]
    dx = rstd[:rows] * (
        e_sum
        - jnp.mean(e_sum, axis=-1, keepdims=True)
        - own_xhat * jnp.mean(e_sum * own_xhat, axis=-1, keepdims=True)
    )
    own_upstream = upstream_low[:rows].astype(F32)
    grad_tokens = own_upstream + dx

    zero_qkv = jnp.zeros((3, TP, part), F32)
    full_b_qkv = lax.dynamic_update_index_in_dim(
        zero_qkv, grad_qkv_bias.reshape(3, 1, part), t, 1
    ).reshape(width, 3)
    zero_up = jnp.zeros((TP, hidden), F32)
    full_b_up = lax.dynamic_update_index_in_dim(zero_up, grad_up_bias[None], t, 0).reshape(width, 4)
    lanes = jnp.stack(
        [
            jnp.sum(d_h1 * xhat, axis=0),
            jnp.sum(d_h1, axis=0),
            jnp.sum(d_h2 * xhat, axis=0),
            jnp.sum(d_h2, axis=0),
            jnp.sum(own_upstream, axis=0),
        ],
        axis=1,
    )
    vec_grads = jnp.concatenate([lanes, full_b_qkv, full_b_up], axis=1)

    tail_grads = jnp.concatenate(
        [grad_down.reshape(qs, units, width), grad_out.reshape(qs, shard, width)], axis=1
    )
    tail_sum = scatter_q(tail_grads, q, sizes)
    shard_down, shard_out = tail_sum[:units], tail_sum[units:]
    column_grads = jnp.concatenate([grad_qkv, vec_grads, grad_up], axis=1)
    column_grads = column_grads.reshape(TP, qs, shard, -1).transpose(1, 0, 2, 3)
    column_sum = scatter_q(column_grads, q, sizes)
    low_sum = column_sum.astype(BF)
    got = exchange_t([pick(low_sum, t ^ k) for k in range(TP)])
    got = [pick(column_sum, t)] + [item.astype(F32) for item in got[1:]]
    vec_sum = sum(item[:, at : at + 12] for item in got)
    got = jnp.stack(unxor(got, t))
    shard_qkv = (
        got[:, :, : 3 * part].reshape(TP, shard, 3, part).transpose(1, 2, 0, 3).reshape(shard, -1)
    )
    shard_up = got[:, :, at + 12 :].transpose(1, 0, 2).reshape(shard, -1)
    shard_branch_bias = vec_sum[:, 4]
    return (
        output.astype(BF),
        grad_tokens,
        vec_sum[:, 0],
        vec_sum[:, 1],
        vec_sum[:, 2],
        vec_sum[:, 3],
        shard_qkv,
        vec_sum[:, 5:8].reshape(-1),
        shard_out,
        shard_branch_bias,
        shard_up,
        vec_sum[:, 8:12].reshape(-1),
        shard_down,
        shard_branch_bias,
    )


def solution(mesh):
    nd, nf = mesh.shape["dp"], mesh.shape["fsdp"]
    sizes = (nd // TP, nf)
    inner = Mesh(mesh.devices.reshape((TP,) + sizes), ("t", "dq", "fsdp"))
    axes = ("t", "dq", "fsdp")
    matrix, vector = P(axes, None), P(axes)
    return jax.shard_map(
        lambda *args: local(sizes, *args),
        mesh=inner,
        in_specs=(
            matrix, matrix, vector, vector, vector, vector, matrix, vector,
            matrix, vector, matrix, vector, matrix, vector, matrix,
        ),
        out_specs=(
            matrix, matrix, vector, vector, vector, vector, matrix, vector,
            matrix, vector, matrix, vector, matrix, vector,
        ),
        check_vma=False,
    )
```

```python
import math

import jax
import jax.numpy as jnp
from jax import lax
from jax.experimental import pallas as pl
from jax.experimental.pallas import tpu as pltpu
from jax.sharding import Mesh
from jax.sharding import PartitionSpec as P

HEADS = 12
HEAD = 64
ROT = 16
TP = 4
BF = jnp.bfloat16
F32 = jnp.float32

epsilon = 1e-05
neg_large = -1e30
inv_sqrt_two = 1.0 / math.sqrt(2.0)
inv_sqrt_tau = 1.0 / math.sqrt(2.0 * math.pi)


def xor_pairs(count, bit):
    return [(i, i ^ bit) for i in range(count)]


def pick(array, index, axis=0):
    return lax.dynamic_index_in_dim(array, index, axis, keepdims=False)


def unxor(slots, rank):
    bit = 1
    while bit < len(slots):
        flip = (rank & bit) != 0
        slots = [jnp.where(flip, slots[k ^ bit], slots[k]) for k in range(len(slots))]
        bit *= 2
    return slots


def gather_t(block, rank):
    one = lax.ppermute(block, "t", xor_pairs(TP, 1))
    two = lax.ppermute(block, "t", xor_pairs(TP, 2))
    near = lax.ppermute(block, "t", [(1, 2), (2, 1)])
    far = lax.ppermute(two, "t", [(2, 3), (1, 0)])
    middle = (rank == 1) | (rank == 2)
    return [block, one, two, jnp.where(middle, near, far)]


def scatter_t(slots):
    low = [slot.astype(BF) for slot in slots]
    one = lax.ppermute(low[1], "t", xor_pairs(TP, 1))
    near = lax.ppermute(low[3], "t", [(1, 2), (2, 1)])
    relay = lax.ppermute(low[3], "t", [(0, 1), (3, 2)])
    two = lax.ppermute((slots[2] + relay.astype(F32)).astype(BF), "t", xor_pairs(TP, 2))
    return slots[0] + one.astype(F32) + near.astype(F32) + two.astype(F32)


def exchange_t(pieces):
    return [pieces[0]] + [
        lax.ppermute(pieces[k], "t", xor_pairs(TP, k)) for k in range(1, TP)
    ]


def gather_q(block, rank, sizes):
    if sizes != (2, 4):
        return lax.all_gather(block, ("dq", "fsdp"), axis=0, tiled=False)
    half = block.shape[0] // 2
    one = lax.ppermute(block, "fsdp", xor_pairs(4, 1))
    two = lax.ppermute(block, "fsdp", xor_pairs(4, 2))
    upper = lax.ppermute(one[:half], "fsdp", xor_pairs(4, 2))
    lower = lax.ppermute(two[half:], "fsdp", xor_pairs(4, 1))
    three = jnp.concatenate([upper, lower], axis=0)
    mine = [block, one, two, three]
    other = [lax.ppermute(part, "dq", xor_pairs(2, 1)) for part in mine]
    return jnp.stack(unxor(mine + other, rank))


def scatter_q(blocks, rank, sizes):
    if sizes != (2, 4):
        return lax.psum_scatter(
            blocks.astype(BF), ("dq", "fsdp"), scatter_dimension=0, tiled=False
        ).astype(F32)
    core, spot = rank // 4, rank % 4
    halves = blocks.reshape((2, 4) + blocks.shape[1:])
    keep = pick(halves, core)
    send = pick(halves, 1 - core).astype(BF)
    pair = keep + lax.ppermute(send, "dq", xor_pairs(2, 1)).astype(F32)
    mine, one, two, three = [pick(pair, spot ^ k) for k in range(4)]
    half = mine.shape[0] // 2
    three = three.astype(BF)
    upper = lax.ppermute(three[:half], "fsdp", xor_pairs(4, 1))
    lower = lax.ppermute(three[half:], "fsdp", xor_pairs(4, 2))
    two = jnp.concatenate([two[:half] + upper.astype(F32), two[half:]], axis=0)
    one = jnp.concatenate([one[:half], one[half:] + lower.astype(F32)], axis=0)
    one = lax.ppermute(one.astype(BF), "fsdp", xor_pairs(4, 1))
    two = lax.ppermute(two.astype(BF), "fsdp", xor_pairs(4, 2))
    return mine + one.astype(F32) + two.astype(F32)


def layout(seq_lengths, row_count):
    row_index = jnp.arange(row_count, dtype=jnp.int32)
    slot_count = seq_lengths.shape[0]
    ends = jnp.cumsum(seq_lengths)
    starts = ends - seq_lengths
    segment = jnp.sum((row_index[:, None] >= ends[None, :]).astype(jnp.int32), axis=1)
    live_rows = row_index < ends[-1]
    unique_seg = jnp.where(live_rows, segment, slot_count + row_index)
    slot_index = jnp.arange(slot_count, dtype=jnp.int32)
    first_row = jnp.sum(
        jnp.where(segment[:, None] == slot_index[None, :], starts[None, :], 0), axis=1
    )
    position = jnp.where(live_rows, row_index - first_row, 0)
    attn_mask = (unique_seg[:, None] == unique_seg[None, :]) & (
        row_index[None, :] <= row_index[:, None]
    )
    half_rot = ROT // 2
    inverse_freq = 10000.0 ** (-(2.0 * jnp.arange(half_rot, dtype=jnp.float32)) / ROT)
    angle = position.astype(jnp.float32)[:, None] * inverse_freq[None, :]
    return (
        live_rows.astype(jnp.float32),
        attn_mask,
        jnp.cos(angle)[:, None, :],
        jnp.sin(angle)[:, None, :],
    )


def rotate(part, cosine, sine):
    half_rot = ROT // 2
    first = part[..., :half_rot]
    second = part[..., half_rot:ROT]
    return jnp.concatenate(
        [first * cosine - second * sine, second * cosine + first * sine, part[..., ROT:]], axis=-1
    )


def contract(left, right, left_dim, right_dim):
    return lax.dot_general(
        left, right, (((left_dim,), (right_dim,)), ((), ())), preferred_element_type=F32
    )


ROWS = 128
COUNT = TP * ROWS
WIDTH = 768
SHARD = 24
VEC_AT = 576
NARROW = 640
G_HEADS = HEADS // TP
QUARTER = WIDTH // TP


def iota(shape, axis):
    return lax.broadcasted_iota(jnp.int32, shape, axis)


def split(number, by):
    quotient = jnp.floor((number.astype(F32) + 0.5) * (1.0 / by)).astype(jnp.int32)
    return quotient, number - quotient * by


def hot(condition):
    return jnp.where(condition, 1.0, 0.0).astype(BF)


def owner_of_block(block, t, q):
    return ((block & 3) ^ t) * 8 + ((block >> 2) ^ q)


def feature_order(t, q):
    block, row = split(iota((1, WIDTH), 1), SHARD)
    return hot(iota((WIDTH, 1), 0) == owner_of_block(block, t, q) * SHARD + row)


def head_order(q):
    lane = iota((1, 256), 1)
    row = lane & 31
    place = ((lane >> 5) ^ q) * SHARD + row
    place = jnp.where(row < SHARD, place, -1)
    return hot(iota((QUARTER, 1), 0) == place)


def vector_rows():
    at = iota((160, 1), 0)
    return hot(iota((1, WIDTH), 1) == (at & 31) * SHARD + (at >> 5))


def dot(left, right, left_dim=1, right_dim=0):
    return lax.dot_general(
        left, right, (((left_dim,), (right_dim,)), ((), ())), preferred_element_type=F32
    )


def placing(number, length, owners):
    owner, element = split(number, length)
    return jnp.where(owners == owner, 1.0, 0.0), hot(iota((length, 1), 0) == element)


def all_places(t, q):
    block = iota((32, 1), 0)
    owners = owner_of_block(block, t, q)
    lane = iota((1, WIDTH), 1)
    third, rest = split(iota((1, 3 * QUARTER), 1), QUARTER)
    return (
        placing(lane, SHARD, block),
        placing(lane, SHARD, owners),
        placing(third * WIDTH + t * QUARTER + rest, 3 * SHARD, owners),
        placing(lane + t * WIDTH, 4 * SHARD, owners),
    )


def spread(values, places):
    mask, element = places
    return jnp.sum(dot(values.astype(BF), element) * mask, axis=0, keepdims=True)


def collect(row, places):
    mask, element = places
    return dot((mask * row).astype(BF), element, 1, 1)


def prepare_kernel(place, w_qkv, w_fc1, vector, tokens, *pieces):
    t = place[0]
    row = iota((SHARD, 64), 0)
    packed = jnp.zeros((SHARD, 64), F32)
    for i in range(5):
        packed = jnp.where(row == i, vector[:, 64 * i : 64 * i + 64], packed)
    packed = jnp.concatenate([packed.astype(BF), jnp.zeros((SHARD, 128), BF)], axis=1)
    for item in pieces:
        if item.shape[0] > 48:
            item[48:, :] = tokens[:, :]
    for rank in range(TP):

        @pl.when(t == rank)
        def _(rank=rank):
            for k in range(TP):
                r = rank ^ k
                at = QUARTER * r
                lower = jnp.concatenate(
                    [
                        w_qkv[:, at : at + QUARTER],
                        w_qkv[:, WIDTH + at : WIDTH + at + QUARTER],
                        w_qkv[:, 2 * WIDTH + at : 2 * WIDTH + at + QUARTER],
                        packed,
                    ],
                    axis=1,
                )
                pieces[k][:48, :] = jnp.concatenate(
                    [w_fc1[:, WIDTH * r : WIDTH * (r + 1)], lower], axis=0
                )


def merge_kernel(zero, one, two, three, columns):
    parts = [ref[:48, :] for ref in (zero, one, two, three)]
    columns[:, :] = jnp.concatenate(
        [part[:SHARD] for part in parts] + [part[SHARD:] for part in parts], axis=0
    )


def frequency_lanes():
    member = iota((1, 128), 1) & 7
    lanes = jnp.zeros((1, 128), F32)
    for i in range(ROT // 2):
        lanes = jnp.where(member == i, 10000.0 ** (-2.0 * i / ROT), lanes)
    return lanes


def normalized(rows):
    removed = rows - jnp.mean(rows, axis=-1, keepdims=True)
    return removed * lax.rsqrt(jnp.mean(removed * removed, axis=-1, keepdims=True) + epsilon)


def early_kernel(place, zero, one, two, three, tokens, xhat, order, masks, cosine, sine, live):
    order[:, :] = feature_order(place[0], place[1])
    column = iota((1, ROWS), 1).astype(F32)
    line = iota((ROWS, 1), 0).astype(F32)
    member = iota((1, 128), 1) & 63
    for k, piece in enumerate((zero, one, two, three)):
        at = slice(ROWS * k, ROWS * (k + 1))
        if k < 3:
            rows = tokens[:, :] if k == 0 else piece[48:, :]
            xhat[at, :] = normalized(dot(rows, order[:, :]))
        sizes = piece[16:32, 512:640].astype(F32)[12:13, 120:124]
        end = jnp.zeros((1, 1), F32)
        segment_line, segment_column = jnp.zeros((ROWS, 1), F32), jnp.zeros((1, ROWS), F32)
        first_line = jnp.zeros((ROWS, 1), F32)
        for s in range(4):
            size = sizes[:, s : s + 1]
            end = end + size
            first_line = first_line + jnp.where(line >= end, size, 0.0)
            segment_line = segment_line + jnp.where(line >= end, 1.0, 0.0)
            segment_column = segment_column + jnp.where(column >= end, 1.0, 0.0)
        lives = line < end
        mask = (line == column) | (lives & (segment_line == segment_column) & (column <= line))
        masks[at, :] = jnp.where(mask, 1.0, 0.0)
        angle = jnp.where(lives, line - first_line, 0.0) * frequency_lanes()
        cosine[at, :] = jnp.where(member < ROT, jnp.cos(angle), 1.0)
        sine[at, :] = jnp.where(member < ROT, jnp.sin(angle), 0.0) * jnp.where(
            member < ROT // 2, -1.0, 1.0
        )
        live[at, :] = jnp.where(lives, 1.0, 0.0)


def last_kernel(rows, order, xhat):
    xhat[:, :] = normalized(dot(rows[:ROWS, :], order[:, :]))


def turn(values, cosine, sine):
    member = iota((1, 384), 1) & 63
    ahead = pltpu.roll(values, 384 - ROT // 2, 1)
    behind = pltpu.roll(values, ROT // 2, 1)
    partner = jnp.where(member < ROT // 2, ahead, behind)
    return values * jnp.concatenate([cosine] * 3, axis=1) + partner * jnp.concatenate(
        [sine] * 3, axis=1
    )


def forward_kernel(place, xhat, xhat_last, masks, cosine, sine, *refs):
    columns = refs[:2]
    (
        mat_up, mat_qkv, h_one, h_two, act, slope, q_low, k_low, v_low, probs, mixed_slots, gains,
        mixed,
    ) = refs[2:]
    t, q = place[0], place[1]
    for kq in range(8):
        ref, at = columns[kq // 4], 192 * (kq % 4)
        mat_up[96 * kq : 96 * kq + 96, :] = ref[at : at + 96, :]
        mat_qkv[96 * kq : 96 * kq + 96, :] = ref[at + 96 : at + 192, :NARROW]

    slots, plain, of_qkv, of_up = all_places(t, q)
    packed = dot(vector_rows(), mat_qkv[:, VEC_AT:])
    vectors = jnp.concatenate([packed[32 * i : 32 * i + 32] for i in range(5)], axis=1)
    gain_one, bias_one, gain_two, bias_two = [
        spread(vectors[:, SHARD * i : SHARD * i + SHARD], slots) for i in range(4)
    ]
    vec_qkv = spread(vectors[:, 96:168], of_qkv)
    vec_up = spread(vectors[:, 192:288], of_up)
    vec_out = spread(vectors[:, 168:192], plain) + spread(vectors[:, 288:312], plain)
    gains[:, :] = jnp.concatenate([gain_one, gain_two, vec_out, jnp.zeros((5, WIDTH), F32)], axis=0)

    h_two[: 3 * ROWS, :] = (xhat[:, :] * gain_two + bias_two).astype(BF)
    h_two[3 * ROWS :, :] = (xhat_last[:, :] * gain_two + bias_two).astype(BF)
    up = dot(h_two[:, :], mat_up[:, :]) + vec_up
    phi = 0.5 * (1.0 + lax.erf(up * inv_sqrt_two))
    act[:, :] = (up * phi).astype(BF)
    slope[:, :] = phi + up * jnp.exp(-0.5 * up * up) * inv_sqrt_tau

    h_one[: 3 * ROWS, :] = (xhat[:, :] * gain_one + bias_one).astype(BF)
    h_one[3 * ROWS :, :] = (xhat_last[:, :] * gain_one + bias_one).astype(BF)
    qkv = dot(h_one[:, :], mat_qkv[:, :VEC_AT]) + vec_qkv
    turned = turn(qkv[:, : 2 * QUARTER], cosine[:, :], sine[:, :])
    q_low[:, :] = turned[:, :QUARTER].astype(BF)
    k_low[:, :] = turned[:, QUARTER:].astype(BF)
    v_low[:, :] = qkv[:, 2 * QUARTER :].astype(BF)
    for k in range(TP):
        at = slice(ROWS * k, ROWS * (k + 1))
        for head in range(G_HEADS):
            lanes = slice(HEAD * head, HEAD * (head + 1))
            scores = dot(q_low[at, lanes], k_low[at, lanes], 1, 1) * 0.125
            scores = jnp.where(masks[at, :] > 0.0, scores, neg_large)
            exponent = jnp.exp(scores - jnp.max(scores, axis=-1, keepdims=True))
            chances = exponent / jnp.sum(exponent, axis=-1, keepdims=True)
            probs[G_HEADS * k + head] = chances
            mixed[at, lanes] = dot(chances.astype(BF), v_low[at, lanes]).astype(BF)
    mixed_slots[:, :] = dot(mixed[:, :], head_order(q)).astype(BF)


def share_kernel(place, act, mixed_slots, *refs):
    tails, down, out_mat, shares = refs[:2], refs[2], refs[3], refs[4:]
    q = place[1]
    for kq in range(8):
        ref, at = tails[kq // 4], 128 * (kq % 4)
        first = pl.multiple_of((q ^ kq) * 96, 32)
        down[pl.ds(first, 96), :] = ref[at : at + 96, :]
        out_mat[32 * kq : 32 * kq + 32, :] = ref[at + 96 : at + 128, :]
    total = dot(act[:, :], down[:, :]) + dot(mixed_slots[:, :], out_mat[:, :])
    for k in range(TP):
        shares[k][:, :] = total[ROWS * k : ROWS * (k + 1)].astype(shares[k].dtype)


def upstream_kernel(place, *refs):
    cots = refs[:4]
    (
        live, h_two, act, slope, mixed_slots, down, out_mat, d_up, d_mixed, keep, send,
        upstream, grad_down,
    ) = refs[4:]
    q = place[1]
    for k in range(TP):
        at = slice(ROWS * k, ROWS * (k + 1))
        last = cots[k].shape[0]
        upstream[at, :] = (cots[k][last - ROWS :, :].astype(F32) * live[at, :]).astype(BF)
    d_up[:, :] = (dot(upstream[:, :], down[:, :], 1, 1) * slope[:, :]).astype(BF)
    grad_up = dot(h_two[:, :], d_up[:, :], 0, 0)
    grad_down[:, :] = dot(act[:, :], upstream[:, :], 0, 0)
    grad_out = dot(mixed_slots[:, :], upstream[:, :], 0, 0)
    for kq in range(8):
        target = keep if kq < 4 else send
        at = 224 * (kq % 4)
        first = pl.multiple_of((q ^ kq) * 96, 32)
        target[at : at + 96, :] = grad_down[pl.ds(first, 96), :].astype(target.dtype)
        target[at + 96 : at + 128, :] = grad_out[32 * kq : 32 * kq + 32].astype(target.dtype)
        target[at + 128 : at + 224, :] = grad_up[96 * kq : 96 * kq + 96].astype(target.dtype)
    d_slots = dot(upstream[:, :], out_mat[:, :], 1, 1).astype(BF)
    d_mixed[:, :] = dot(d_slots, head_order(q), 1, 1).astype(BF)


def attention_kernel(
    q_low, k_low, v_low, probs, d_mixed, cosine, sine, d_qkv, d_turned
):
    for k in range(TP):
        at = slice(ROWS * k, ROWS * (k + 1))
        for head in range(G_HEADS):
            lanes = slice(HEAD * head, HEAD * (head + 1))
            chances = probs[G_HEADS * k + head]
            d_out = d_mixed[at, lanes]
            d_probs = dot(d_out, v_low[at, lanes], 1, 1)
            delta = jnp.sum(chances * d_probs, axis=-1, keepdims=True)
            d_scores = (chances * (d_probs - delta)).astype(BF)
            d_turned[at, lanes] = dot(d_scores, k_low[at, lanes]) * 0.125
            d_turned[at, QUARTER + HEAD * head : QUARTER + HEAD * (head + 1)] = (
                dot(d_scores, q_low[at, lanes], 0, 0) * 0.125
            )
            d_qkv[at, 2 * QUARTER + HEAD * head : 2 * QUARTER + HEAD * (head + 1)] = dot(
                chances.astype(BF), d_out, 0, 0
            ).astype(BF)
    d_qkv[:, : 2 * QUARTER] = turn(d_turned[:, :], cosine[:, :], -sine[:, :]).astype(BF)


def backward_kernel(
    place, xhat, xhat_last, order, mat_up, mat_qkv, h_one, d_up, d_qkv, gains, cot, live, *refs
):
    shares, (keep, send) = refs[:4], refs[4:]
    t, q = place[0], place[1]
    d_one = dot(d_qkv[:, :], mat_qkv[:, :VEC_AT], 1, 1)
    d_two = dot(d_up[:, :], mat_up[:, :], 1, 1)
    share = (d_one * gains[0:1, :] + d_two * gains[1:2, :]).astype(BF)
    share = dot(share, order[:, :], 1, 1)
    for k in range(TP):
        shares[k][:, :] = share[ROWS * k : ROWS * (k + 1)].astype(shares[k].dtype)

    slots, plain, of_qkv, of_up = all_places(t, q)

    def total(rows):
        return jnp.sum(rows, axis=0, keepdims=True)

    def with_xhat(rows):
        return total(rows[: 3 * ROWS] * xhat[:, :]) + total(rows[3 * ROWS :] * xhat_last[:, :])

    vectors = jnp.concatenate(
        [
            collect(with_xhat(d_one), slots),
            collect(total(d_one), slots),
            collect(with_xhat(d_two), slots),
            collect(total(d_two), slots),
            collect(total(cot[:, :].astype(F32) * live[:ROWS, :]), plain),
            collect(total(d_qkv[:, :].astype(F32)), of_qkv),
            collect(total(d_up[:, :].astype(F32)), of_up),
            jnp.zeros((32, 32), F32),
        ],
        axis=1,
    ).astype(BF)
    packed = jnp.concatenate([vectors[:, 64 * i : 64 * i + 64] for i in range(5)], axis=0)
    grads = jnp.concatenate(
        [dot(h_one[:, :], d_qkv[:, :], 0, 0), dot(vector_rows(), packed, 0, 0)], axis=1
    )
    keep[:, :] = grads[:384]
    send[:, :] = grads[384:].astype(BF)


def columns_kernel(place, zero, one, two, three, qkv, up, *vectors):
    t = place[0]
    parts = [zero[:, :]] + [ref[:, :].astype(F32) for ref in (one, two, three)]
    for rank in range(TP):

        @pl.when(t == rank)
        def _(rank=rank):
            by_rank = [parts[rank ^ s] for s in range(TP)]
            up[:, :] = jnp.concatenate([item[:, :WIDTH] for item in by_rank], axis=1)
            qkv[:, :] = jnp.concatenate(
                [
                    item[:, WIDTH + QUARTER * i : WIDTH + QUARTER * (i + 1)]
                    for i in range(3)
                    for item in by_rank
                ],
                axis=1,
            )

    packed = sum(item[:8, WIDTH + VEC_AT :] for item in parts)
    row = jnp.concatenate([packed[i : i + 1] for i in range(5)], axis=1)
    at = 0
    for ref in vectors[:-1]:
        size = ref.shape[1]
        ref[:, :] = row[:, at : at + size]
        at += size
    vectors[-1][:, :] = row[:, 4 * SHARD : 5 * SHARD]


def output_kernel(zero, one, two, three, tokens, live, gains, output):
    share = zero[:, :] + one[:, :].astype(F32) + two[:, :].astype(F32) + three[:, :].astype(F32)
    output[:, :] = (live[:ROWS, :] * (tokens[:, :].astype(F32) + share + gains[2:3, :])).astype(BF)


def input_kernel(zero, one, two, three, tokens, cot, live, grad):
    e = zero[:, :] + one[:, :].astype(F32) + two[:, :].astype(F32) + three[:, :].astype(F32)
    rows = tokens[:, :].astype(F32)
    removed = rows - jnp.mean(rows, axis=-1, keepdims=True)
    rstd = lax.rsqrt(jnp.mean(removed * removed, axis=-1, keepdims=True) + epsilon)
    xhat = removed * rstd
    dx = rstd * (
        e - jnp.mean(e, axis=-1, keepdims=True) - xhat * jnp.mean(e * xhat, axis=-1, keepdims=True)
    )
    grad[:, :] = cot[:, :].astype(F32) * live[:ROWS, :] + dx


def call(kernel, name, outs, *args, scratch=(), mib=16, weight=1):
    space = [pl.BlockSpec(memory_space=pltpu.VMEM)] * len(args)
    if args[0].dtype == jnp.int32:
        space[0] = pl.BlockSpec(memory_space=pltpu.SMEM)
    shapes = [jax.ShapeDtypeStruct(shape, kind) for shape, kind in outs]
    return pl.pallas_call(
        kernel,
        name=name,
        out_shape=shapes,
        in_specs=space,
        out_specs=[pl.BlockSpec(memory_space=pltpu.VMEM)] * len(shapes),
        scratch_shapes=[pltpu.VMEM(shape, kind) for shape, kind in scratch],
        cost_estimate=pl.CostEstimate(flops=weight * 10**9, transcendentals=0, bytes_accessed=weight * 10**6),
        compiler_params=pltpu.CompilerParams(vmem_limit_bytes=mib * 1024 * 1024),
    )(*args)


def after(array, *others):
    return lax.optimization_barrier((array, others))[0]


def xor_permutes(block, axis, count):
    return [lax.ppermute(block, axis, xor_pairs(count, k)) for k in range(1, 4)]


def plane_pair(keep, send):
    return keep + lax.ppermute(send, "dq", xor_pairs(2, 1)).astype(F32)


def plane_relay(pair):
    rows = pair.shape[0] // 4
    three = pair[3 * rows :].astype(BF)
    upper = lax.ppermute(three[: rows // 2], "fsdp", xor_pairs(4, 1))
    lower = lax.ppermute(three[rows // 2 :], "fsdp", xor_pairs(4, 2))
    return upper, lower


def plane_last(pair, upper, lower):
    rows = pair.shape[0] // 4
    half = rows // 2
    mine, one, two = [pair[rows * k : rows * (k + 1)] for k in range(3)]
    two = jnp.concatenate([two[:half] + upper.astype(F32), two[half:]], axis=0)
    one = jnp.concatenate([one[:half], one[half:] + lower.astype(F32)], axis=0)
    one = lax.ppermute(one.astype(BF), "fsdp", xor_pairs(4, 1))
    two = lax.ppermute(two.astype(BF), "fsdp", xor_pairs(4, 2))
    return mine + one.astype(F32) + two.astype(F32)


def plane_local(
    tokens, lengths, ln_attn_gain, ln_attn_bias, ln_mlp_gain, ln_mlp_bias, w_qkv, b_qkv,
    w_out, b_out, w_fc1, b_fc1, w_fc2, b_fc2, cotangent,
):
    t = lax.axis_index("t")
    q = lax.axis_index("dq") * 4 + lax.axis_index("fsdp")
    place = jnp.stack([t, q]).astype(jnp.int32)
    vector = jnp.concatenate(
        [
            ln_attn_gain, ln_attn_bias, ln_mlp_gain, ln_mlp_bias, b_qkv, b_out, b_fc1, b_fc2,
            lengths[0].astype(BF), jnp.zeros((68,), BF),
        ]
    )
    block = (ROWS, WIDTH)
    piece = ((48, WIDTH), BF)
    piece_rows = ((48 + ROWS, WIDTH), BF)
    tail = jnp.concatenate([w_fc2, w_out, jnp.zeros((8, WIDTH), BF)], axis=0)
    pieces = call(
        prepare_kernel, "prepare", [piece, piece_rows, piece_rows, piece],
        place, w_qkv, w_fc1, vector.astype(F32)[None], tokens, weight=10,
    )
    pieces = exchange_t(pieces)
    token_one = pieces[1]
    both = after(jnp.concatenate([tokens, cotangent], axis=0), token_one)
    rows_three = lax.ppermute(both, "t", xor_pairs(TP, 3))
    tail_one = lax.ppermute(tail, "fsdp", xor_pairs(4, 1))
    tail_two = lax.ppermute(tail, "fsdp", xor_pairs(4, 2))
    tail_three = lax.ppermute(after(tail, tail_one), "fsdp", xor_pairs(4, 3))
    (columns,) = call(merge_kernel, "merge", [((192, WIDTH), BF)], *pieces, weight=10)
    columns = after(columns, tail_one, tail_two, tail_three)
    arrived = xor_permutes(columns, "fsdp", 4)
    columns = jnp.concatenate([columns] + arrived, axis=0)
    columns = [columns, lax.ppermute(columns, "dq", xor_pairs(2, 1))]
    wide = (COUNT, WIDTH)
    square = ((COUNT, 128), F32)
    xhat, order, masks, cosine, sine, lives = call(
        early_kernel,
        "early",
        [((3 * ROWS, WIDTH), F32), ((WIDTH, WIDTH), BF), square, square, square, ((COUNT, 1), F32)],
        place, *pieces, tokens,
        weight=10,
    )
    (xhat_last,) = call(
        last_kernel, "last", [(block, F32)], rows_three, order, weight=5
    )
    cot_one = lax.ppermute(after(cotangent, xhat_last), "t", xor_pairs(TP, 1))
    cot_two = lax.ppermute(after(cotangent, xhat_last), "t", xor_pairs(TP, 2))
    cot_slots = [cot_one, cot_two, rows_three]
    third = (COUNT, QUARTER)
    (
        mat_up, mat_qkv, h_one, h_two, act, slope, q_low, k_low, v_low, probs, mixed_slots, gains,
    ) = call(
        forward_kernel,
        "forward",
        [
            ((WIDTH, WIDTH), BF), ((WIDTH, NARROW), BF),
            (wide, BF), (wide, BF), (wide, BF), (wide, F32), (third, BF), (third, BF),
            (third, BF), ((HEADS, ROWS, ROWS), F32), ((COUNT, 256), BF), ((8, WIDTH), F32),
        ],
        place, xhat, xhat_last, masks, cosine, sine, *columns,
        scratch=[(third, BF)],
        weight=100,
    )
    tail = jnp.concatenate([tail, tail_one, tail_two, tail_three], axis=0)
    tail = [tail, lax.ppermute(tail, "dq", xor_pairs(2, 1))]
    shares = [(block, F32)] + [(block, BF)] * 3
    down, out_mat, *out = call(
        share_kernel, "share", [((WIDTH, WIDTH), BF), ((256, WIDTH), BF)] + shares,
        place, act, mixed_slots, *tail,
        weight=10,
    )
    out = exchange_t(out)
    d_up, d_mixed, tail_keep, tail_send = call(
        upstream_kernel,
        "upstream",
        [(wide, BF), (third, BF), ((896, WIDTH), F32), ((896, WIDTH), BF)],
        place, cotangent, *cot_slots, lives, h_two, act, slope, mixed_slots, down, out_mat,
        scratch=[(wide, BF), ((WIDTH, WIDTH), F32)],
        weight=40,
    )
    tail_pair = plane_pair(tail_keep, tail_send)
    (d_qkv,) = call(
        attention_kernel, "attention", [((COUNT, 3 * QUARTER), BF)],
        q_low, k_low, v_low, probs, d_mixed, cosine, sine,
        scratch=[((COUNT, 2 * QUARTER), F32)],
        weight=50,
    )
    tail_got = plane_relay(tail_pair)
    d_qkv = after(d_qkv, tail_pair, out[1])
    *e, col_keep, col_send = call(
        backward_kernel,
        "backward",
        shares + [((384, NARROW), F32), ((384, NARROW), BF)],
        place, xhat, xhat_last, order, mat_up, mat_qkv, h_one, d_up, d_qkv, gains, cotangent, lives,
        weight=40,
    )
    col_pair = plane_pair(col_keep, after(col_send, tail_got, out[2:]))
    col_got = plane_relay(col_pair)
    e = [after(item, out) for item in e]
    e[3] = after(e[3], col_pair)
    e = exchange_t(e)
    col_sum = plane_last(col_pair, *col_got)
    tail_sum = plane_last(after(tail_pair, col_got), *tail_got)
    col_sum = jnp.concatenate([tail_sum[128:], col_sum], axis=1)
    low_sum = col_sum.astype(BF)
    back = [low_sum[SHARD * k : SHARD * (k + 1)] for k in range(TP)]
    arrived = exchange_t(back)
    (output,) = call(
        output_kernel, "output", [(block, BF)], *out, tokens, after(lives, col_keep), gains,
        weight=10,
    )
    (grad_tokens,) = call(
        input_kernel, "input_gradient", [(block, F32)], *e, tokens, cotangent, lives,
        weight=10,
    )
    sizes = [SHARD] * 5 + [3 * SHARD, 4 * SHARD, SHARD]
    shard_qkv, shard_up, *vectors = call(
        columns_kernel, "columns",
        [((SHARD, 3 * WIDTH), F32), ((SHARD, 4 * WIDTH), F32)] + [((1, n), F32) for n in sizes],
        place, col_sum[:SHARD], *arrived[1:],
    )
    g_one, b_one, g_two, b_two, branch, qkv_bias, up_bias, again = [item[0] for item in vectors]
    return (
        output, grad_tokens, g_one, b_one, g_two, b_two, shard_qkv, qkv_bias,
        tail_sum[96 : 96 + SHARD], branch, shard_up, up_bias, tail_sum[:96], again,
    )


def local(
    sizes,
    tokens,
    lengths,
    ln_attn_gain,
    ln_attn_bias,
    ln_mlp_gain,
    ln_mlp_bias,
    w_qkv,
    b_qkv,
    w_out,
    b_out,
    w_fc1,
    b_fc1,
    w_fc2,
    b_fc2,
    cotangent,
):
    if sizes == (2, 4) and w_qkv.shape == (SHARD, 3 * WIDTH) and tokens.shape == (ROWS, WIDTH):
        return plane_local(
            tokens, lengths, ln_attn_gain, ln_attn_bias, ln_mlp_gain, ln_mlp_bias, w_qkv, b_qkv,
            w_out, b_out, w_fc1, b_fc1, w_fc2, b_fc2, cotangent,
        )
    t = lax.axis_index("t")
    q = lax.axis_index("dq") * sizes[1] + lax.axis_index("fsdp")
    qs = sizes[0] * sizes[1]
    rows, width = tokens.shape
    shard = w_qkv.shape[0]
    part = width // TP
    hidden = w_fc1.shape[1] // TP
    units = w_fc2.shape[0]
    heads = HEADS // TP

    vectors = jnp.concatenate(
        [
            item.reshape(shard, -1)
            for item in (
                ln_attn_gain, ln_attn_bias, ln_mlp_gain, ln_mlp_bias, b_qkv, b_out, b_fc1, b_fc2
            )
        ],
        axis=1,
    )
    n_vec = vectors.shape[1]
    low_lengths = jnp.broadcast_to(lengths.astype(BF), (shard, lengths.shape[1]))
    small = jnp.concatenate([vectors, low_lengths], axis=1)
    qkv_parts = w_qkv.reshape(shard, 3, TP, part)
    fc1_parts = w_fc1.reshape(shard, TP, hidden)
    pieces = [
        jnp.concatenate(
            [
                pick(qkv_parts, t ^ k, 2).reshape(shard, 3 * part),
                small,
                pick(fc1_parts, t ^ k, 1),
            ],
            axis=1,
        )
        for k in range(TP)
    ]
    pieces = exchange_t(pieces)
    at = 3 * part
    group_lengths = [piece[0, at + n_vec : at + n_vec + 4].astype(jnp.int32) for piece in pieces]
    mine = jnp.stack(unxor(pieces, t))
    columns = gather_q(mine, q, sizes)
    columns = columns.transpose(1, 0, 2, 3).reshape(width, -1)
    mat_qkv = columns[:, : 3 * part]
    vecs = columns[:, at : at + n_vec].astype(F32)
    mat_up = columns[:, at + small.shape[1] :]
    tail = gather_q(jnp.concatenate([w_fc2, w_out], axis=0), q, sizes)
    mat_down = tail[:, :units].reshape(qs * units, width)
    mat_out = tail[:, units:].reshape(part, width)

    vecs_t = vecs.T
    gain_one, bias_one, gain_two, bias_two = vecs_t[0], vecs_t[1], vecs_t[2], vecs_t[3]
    all_b_qkv = vecs[:, 4:7].reshape(3, TP, part)
    vec_qkv = pick(all_b_qkv, t, 1).reshape(3 * part)
    vec_out = vecs_t[7]
    vec_up = pick(vecs[:, 8:12].reshape(TP, hidden), t)
    vec_down = vecs_t[12]

    token_slots = gather_t(tokens, t)
    upstream_slots = gather_t(cotangent, t)
    layouts = [layout(item, rows) for item in group_lengths]
    live = jnp.concatenate([item[0] for item in layouts])[:, None]
    attn_mask = jnp.stack([item[1] for item in layouts])[:, None]
    cosine = jnp.concatenate([item[2] for item in layouts])
    sine = jnp.concatenate([item[3] for item in layouts])
    resid = jnp.concatenate(token_slots).astype(F32)
    upstream_low = jnp.concatenate(upstream_slots) * live.astype(BF)

    center = jnp.mean(resid, axis=-1, keepdims=True)
    removed = resid - center
    rstd = lax.rsqrt(jnp.mean(removed * removed, axis=-1, keepdims=True) + epsilon)
    xhat = removed * rstd
    low_one = (xhat * gain_one + bias_one).astype(BF)
    low_two = (xhat * gain_two + bias_two).astype(BF)

    up_rows = contract(low_two, mat_up, 1, 0) + vec_up
    phi = 0.5 * (1.0 + lax.erf(up_rows * inv_sqrt_two))
    act_low = (up_rows * phi).astype(BF)
    slope = phi + up_rows * jnp.exp(-0.5 * up_rows * up_rows) * inv_sqrt_tau
    mlp_share = contract(act_low, mat_down, 1, 0)
    grad_down = contract(act_low, upstream_low, 0, 0)
    d_up_low = (contract(upstream_low, mat_down, 1, 1) * slope).astype(BF)
    grad_up = contract(low_two, d_up_low, 0, 0)
    grad_up_bias = jnp.sum(d_up_low.astype(F32), axis=0)
    d_h2 = contract(d_up_low, mat_up, 1, 1)

    count = TP * rows
    qkv = (contract(low_one, mat_qkv, 1, 0) + vec_qkv).reshape(count, 3, heads, HEAD)
    q_low = rotate(qkv[:, 0], cosine, sine).astype(BF).reshape(TP, rows, heads, HEAD)
    k_low = rotate(qkv[:, 1], cosine, sine).astype(BF).reshape(TP, rows, heads, HEAD)
    v_low = qkv[:, 2].astype(BF).reshape(TP, rows, heads, HEAD)
    scores = jnp.einsum("gqhd,gkhd->ghqk", q_low, k_low, preferred_element_type=F32) * 0.125
    scores = jnp.where(attn_mask, scores, neg_large)
    exponent = jnp.exp(scores - jnp.max(scores, axis=-1, keepdims=True))
    probs = exponent / jnp.sum(exponent, axis=-1, keepdims=True)
    probs_low = probs.astype(BF)
    mixed = jnp.einsum("ghqk,gkhd->gqhd", probs_low, v_low, preferred_element_type=F32)
    mixed_low = mixed.reshape(count, part).astype(BF)
    out_share = (mlp_share + contract(mixed_low, mat_out, 1, 0)).reshape(TP, rows, width)
    out_sum = scatter_t([out_share[k] for k in range(TP)])
    output = live[:rows] * (resid[:rows] + out_sum + vec_out + vec_down)

    grad_out = contract(mixed_low, upstream_low, 0, 0)
    d_mixed = contract(upstream_low, mat_out, 1, 1).astype(BF).reshape(TP, rows, heads, HEAD)
    d_probs = jnp.einsum("gqhd,gkhd->ghqk", d_mixed, v_low, preferred_element_type=F32)
    d_values = jnp.einsum("ghqk,gqhd->gkhd", probs_low, d_mixed, preferred_element_type=F32)
    delta = jnp.sum(probs * d_probs, axis=-1, keepdims=True)
    d_scores = (probs * (d_probs - delta)).astype(BF)
    d_query = jnp.einsum("ghqk,gkhd->gqhd", d_scores, k_low, preferred_element_type=F32) * 0.125
    d_keys = jnp.einsum("ghqk,gqhd->gkhd", d_scores, q_low, preferred_element_type=F32) * 0.125
    d_query = rotate(d_query.reshape(count, heads, HEAD), cosine, -sine).reshape(count, part)
    d_keys = rotate(d_keys.reshape(count, heads, HEAD), cosine, -sine).reshape(count, part)
    d_qkv = jnp.concatenate([d_query, d_keys, d_values.reshape(count, part)], axis=1).astype(BF)
    grad_qkv = contract(low_one, d_qkv, 0, 0)
    grad_qkv_bias = jnp.sum(d_qkv.astype(F32), axis=0)
    d_h1 = contract(d_qkv, mat_qkv, 1, 1)

    e_share = (d_h1 * gain_one + d_h2 * gain_two).reshape(TP, rows, width)
    e_sum = scatter_t([e_share[k] for k in range(TP)])
    own_xhat = xhat[:rows]
    dx = rstd[:rows] * (
        e_sum
        - jnp.mean(e_sum, axis=-1, keepdims=True)
        - own_xhat * jnp.mean(e_sum * own_xhat, axis=-1, keepdims=True)
    )
    own_upstream = upstream_low[:rows].astype(F32)
    grad_tokens = own_upstream + dx

    zero_qkv = jnp.zeros((3, TP, part), F32)
    full_b_qkv = lax.dynamic_update_index_in_dim(
        zero_qkv, grad_qkv_bias.reshape(3, 1, part), t, 1
    ).reshape(width, 3)
    zero_up = jnp.zeros((TP, hidden), F32)
    full_b_up = lax.dynamic_update_index_in_dim(zero_up, grad_up_bias[None], t, 0).reshape(width, 4)
    lanes = jnp.stack(
        [
            jnp.sum(d_h1 * xhat, axis=0),
            jnp.sum(d_h1, axis=0),
            jnp.sum(d_h2 * xhat, axis=0),
            jnp.sum(d_h2, axis=0),
            jnp.sum(own_upstream, axis=0),
        ],
        axis=1,
    )
    vec_grads = jnp.concatenate([lanes, full_b_qkv, full_b_up], axis=1)

    tail_grads = jnp.concatenate(
        [grad_down.reshape(qs, units, width), grad_out.reshape(qs, shard, width)], axis=1
    )
    tail_sum = scatter_q(tail_grads, q, sizes)
    shard_down, shard_out = tail_sum[:units], tail_sum[units:]
    column_grads = jnp.concatenate([grad_qkv, vec_grads, grad_up], axis=1)
    column_grads = column_grads.reshape(TP, qs, shard, -1).transpose(1, 0, 2, 3)
    column_sum = scatter_q(column_grads, q, sizes)
    low_sum = column_sum.astype(BF)
    got = exchange_t([pick(low_sum, t ^ k) for k in range(TP)])
    got = [pick(column_sum, t)] + [item.astype(F32) for item in got[1:]]
    vec_sum = sum(item[:, at : at + 12] for item in got)
    got = jnp.stack(unxor(got, t))
    shard_qkv = (
        got[:, :, : 3 * part].reshape(TP, shard, 3, part).transpose(1, 2, 0, 3).reshape(shard, -1)
    )
    shard_up = got[:, :, at + 12 :].transpose(1, 0, 2).reshape(shard, -1)
    shard_branch_bias = vec_sum[:, 4]
    return (
        output.astype(BF),
        grad_tokens,
        vec_sum[:, 0],
        vec_sum[:, 1],
        vec_sum[:, 2],
        vec_sum[:, 3],
        shard_qkv,
        vec_sum[:, 5:8].reshape(-1),
        shard_out,
        shard_branch_bias,
        shard_up,
        vec_sum[:, 8:12].reshape(-1),
        shard_down,
        shard_branch_bias,
    )


def solution(mesh):
    nd, nf = mesh.shape["dp"], mesh.shape["fsdp"]
    sizes = (nd // TP, nf)
    inner = Mesh(mesh.devices.reshape((TP,) + sizes), ("t", "dq", "fsdp"))
    axes = ("t", "dq", "fsdp")
    matrix, vector = P(axes, None), P(axes)
    return jax.shard_map(
        lambda *args: local(sizes, *args),
        mesh=inner,
        in_specs=(
            matrix, matrix, vector, vector, vector, vector, matrix, vector,
            matrix, vector, matrix, vector, matrix, vector, matrix,
        ),
        out_specs=(
            matrix, matrix, vector, vector, vector, vector, matrix, vector,
            matrix, vector, matrix, vector, matrix, vector,
        ),
        check_vma=False,
    )
```

```python
import math

import jax
import jax.numpy as jnp
from jax import lax
from jax.experimental import pallas as pl
from jax.experimental.pallas import tpu as pltpu
from jax.sharding import Mesh
from jax.sharding import PartitionSpec as P

HEADS = 12
HEAD = 64
ROT = 16
TP = 4
BF = jnp.bfloat16
F32 = jnp.float32

epsilon = 1e-05
neg_large = -1e30
inv_sqrt_two = 1.0 / math.sqrt(2.0)
inv_sqrt_tau = 1.0 / math.sqrt(2.0 * math.pi)


def xor_pairs(count, bit):
    return [(i, i ^ bit) for i in range(count)]


def pick(array, index, axis=0):
    return lax.dynamic_index_in_dim(array, index, axis, keepdims=False)


def unxor(slots, rank):
    bit = 1
    while bit < len(slots):
        flip = (rank & bit) != 0
        slots = [jnp.where(flip, slots[k ^ bit], slots[k]) for k in range(len(slots))]
        bit *= 2
    return slots


def gather_t(block, rank):
    one = lax.ppermute(block, "t", xor_pairs(TP, 1))
    two = lax.ppermute(block, "t", xor_pairs(TP, 2))
    near = lax.ppermute(block, "t", [(1, 2), (2, 1)])
    far = lax.ppermute(two, "t", [(2, 3), (1, 0)])
    middle = (rank == 1) | (rank == 2)
    return [block, one, two, jnp.where(middle, near, far)]


def scatter_t(slots):
    low = [slot.astype(BF) for slot in slots]
    one = lax.ppermute(low[1], "t", xor_pairs(TP, 1))
    near = lax.ppermute(low[3], "t", [(1, 2), (2, 1)])
    relay = lax.ppermute(low[3], "t", [(0, 1), (3, 2)])
    two = lax.ppermute((slots[2] + relay.astype(F32)).astype(BF), "t", xor_pairs(TP, 2))
    return slots[0] + one.astype(F32) + near.astype(F32) + two.astype(F32)


def exchange_t(pieces):
    return [pieces[0]] + [
        lax.ppermute(pieces[k], "t", xor_pairs(TP, k)) for k in range(1, TP)
    ]


def gather_q(block, rank, sizes):
    if sizes != (2, 4):
        return lax.all_gather(block, ("dq", "fsdp"), axis=0, tiled=False)
    half = block.shape[0] // 2
    one = lax.ppermute(block, "fsdp", xor_pairs(4, 1))
    two = lax.ppermute(block, "fsdp", xor_pairs(4, 2))
    upper = lax.ppermute(one[:half], "fsdp", xor_pairs(4, 2))
    lower = lax.ppermute(two[half:], "fsdp", xor_pairs(4, 1))
    three = jnp.concatenate([upper, lower], axis=0)
    mine = [block, one, two, three]
    other = [lax.ppermute(part, "dq", xor_pairs(2, 1)) for part in mine]
    return jnp.stack(unxor(mine + other, rank))


def scatter_q(blocks, rank, sizes):
    if sizes != (2, 4):
        return lax.psum_scatter(
            blocks.astype(BF), ("dq", "fsdp"), scatter_dimension=0, tiled=False
        ).astype(F32)
    core, spot = rank // 4, rank % 4
    halves = blocks.reshape((2, 4) + blocks.shape[1:])
    keep = pick(halves, core)
    send = pick(halves, 1 - core).astype(BF)
    pair = keep + lax.ppermute(send, "dq", xor_pairs(2, 1)).astype(F32)
    mine, one, two, three = [pick(pair, spot ^ k) for k in range(4)]
    half = mine.shape[0] // 2
    three = three.astype(BF)
    upper = lax.ppermute(three[:half], "fsdp", xor_pairs(4, 1))
    lower = lax.ppermute(three[half:], "fsdp", xor_pairs(4, 2))
    two = jnp.concatenate([two[:half] + upper.astype(F32), two[half:]], axis=0)
    one = jnp.concatenate([one[:half], one[half:] + lower.astype(F32)], axis=0)
    one = lax.ppermute(one.astype(BF), "fsdp", xor_pairs(4, 1))
    two = lax.ppermute(two.astype(BF), "fsdp", xor_pairs(4, 2))
    return mine + one.astype(F32) + two.astype(F32)


def layout(seq_lengths, row_count):
    row_index = jnp.arange(row_count, dtype=jnp.int32)
    slot_count = seq_lengths.shape[0]
    ends = jnp.cumsum(seq_lengths)
    starts = ends - seq_lengths
    segment = jnp.sum((row_index[:, None] >= ends[None, :]).astype(jnp.int32), axis=1)
    live_rows = row_index < ends[-1]
    unique_seg = jnp.where(live_rows, segment, slot_count + row_index)
    slot_index = jnp.arange(slot_count, dtype=jnp.int32)
    first_row = jnp.sum(
        jnp.where(segment[:, None] == slot_index[None, :], starts[None, :], 0), axis=1
    )
    position = jnp.where(live_rows, row_index - first_row, 0)
    attn_mask = (unique_seg[:, None] == unique_seg[None, :]) & (
        row_index[None, :] <= row_index[:, None]
    )
    half_rot = ROT // 2
    inverse_freq = 10000.0 ** (-(2.0 * jnp.arange(half_rot, dtype=jnp.float32)) / ROT)
    angle = position.astype(jnp.float32)[:, None] * inverse_freq[None, :]
    return (
        live_rows.astype(jnp.float32),
        attn_mask,
        jnp.cos(angle)[:, None, :],
        jnp.sin(angle)[:, None, :],
    )


def rotate(part, cosine, sine):
    half_rot = ROT // 2
    first = part[..., :half_rot]
    second = part[..., half_rot:ROT]
    return jnp.concatenate(
        [first * cosine - second * sine, second * cosine + first * sine, part[..., ROT:]], axis=-1
    )


def contract(left, right, left_dim, right_dim):
    return lax.dot_general(
        left, right, (((left_dim,), (right_dim,)), ((), ())), preferred_element_type=F32
    )


ROWS = 128
COUNT = TP * ROWS
WIDTH = 768
SHARD = 24
VEC_AT = 576
NARROW = 640
G_HEADS = HEADS // TP
QUARTER = WIDTH // TP


def iota(shape, axis):
    return lax.broadcasted_iota(jnp.int32, shape, axis)


def split(number, by):
    quotient = jnp.floor((number.astype(F32) + 0.5) * (1.0 / by)).astype(jnp.int32)
    return quotient, number - quotient * by


def hot(condition):
    return jnp.where(condition, 1.0, 0.0).astype(BF)


def owner_of_block(block, t, q):
    return ((block & 3) ^ t) * 8 + ((block >> 2) ^ q)


def feature_order(t, q):
    block, row = split(iota((1, WIDTH), 1), SHARD)
    return hot(iota((WIDTH, 1), 0) == owner_of_block(block, t, q) * SHARD + row)


def head_order(q):
    lane = iota((1, 256), 1)
    row = lane & 31
    place = ((lane >> 5) ^ q) * SHARD + row
    place = jnp.where(row < SHARD, place, -1)
    return hot(iota((QUARTER, 1), 0) == place)


def vector_rows():
    at = iota((160, 1), 0)
    return hot(iota((1, WIDTH), 1) == (at & 31) * SHARD + (at >> 5))


def dot(left, right, left_dim=1, right_dim=0):
    return lax.dot_general(
        left, right, (((left_dim,), (right_dim,)), ((), ())), preferred_element_type=F32
    )


def placing(number, length, owners):
    owner, element = split(number, length)
    return jnp.where(owners == owner, 1.0, 0.0), hot(iota((length, 1), 0) == element)


def all_places(t, q):
    block = iota((32, 1), 0)
    owners = owner_of_block(block, t, q)
    lane = iota((1, WIDTH), 1)
    third, rest = split(iota((1, 3 * QUARTER), 1), QUARTER)
    return (
        placing(lane, SHARD, block),
        placing(lane, SHARD, owners),
        placing(third * WIDTH + t * QUARTER + rest, 3 * SHARD, owners),
        placing(lane + t * WIDTH, 4 * SHARD, owners),
    )


def spread(values, places):
    mask, element = places
    return jnp.sum(dot(values.astype(BF), element) * mask, axis=0, keepdims=True)


def collect(row, places):
    mask, element = places
    return dot((mask * row).astype(BF), element, 1, 1)


def prepare_kernel(place, weights, vector, tokens, *pieces):
    w_fc1, w_qkv = weights.at[:, : 4 * WIDTH], weights.at[:, 4 * WIDTH :]
    t = place[0]
    row = iota((SHARD, 64), 0)
    packed = jnp.zeros((SHARD, 64), F32)
    for i in range(5):
        packed = jnp.where(row == i, vector[:, 64 * i : 64 * i + 64], packed)
    packed = jnp.concatenate([packed.astype(BF), jnp.zeros((SHARD, 128), BF)], axis=1)
    for item in pieces:
        if item.shape[0] > 48:
            item[48:, :] = tokens[:, :]
    for rank in range(TP):

        @pl.when(t == rank)
        def _(rank=rank):
            for k in range(TP):
                r = rank ^ k
                at = QUARTER * r
                lower = jnp.concatenate(
                    [
                        w_qkv[:, at : at + QUARTER],
                        w_qkv[:, WIDTH + at : WIDTH + at + QUARTER],
                        w_qkv[:, 2 * WIDTH + at : 2 * WIDTH + at + QUARTER],
                        packed,
                    ],
                    axis=1,
                )
                pieces[k][:48, :] = jnp.concatenate(
                    [w_fc1[:, WIDTH * r : WIDTH * (r + 1)], lower], axis=0
                )


def merge_kernel(zero, one, two, three, columns):
    parts = [ref[:48, :] for ref in (zero, one, two, three)]
    columns[:, :] = jnp.concatenate(
        [part[:SHARD] for part in parts] + [part[SHARD:] for part in parts], axis=0
    )


def frequency_lanes():
    member = iota((1, 128), 1) & 7
    lanes = jnp.zeros((1, 128), F32)
    for i in range(ROT // 2):
        lanes = jnp.where(member == i, 10000.0 ** (-2.0 * i / ROT), lanes)
    return lanes


def normalized(rows):
    removed = rows - jnp.mean(rows, axis=-1, keepdims=True)
    return removed * lax.rsqrt(jnp.mean(removed * removed, axis=-1, keepdims=True) + epsilon)


def early_kernel(place, zero, one, two, three, tokens, xhat, order, masks, cosine, sine, live):
    order[:, :] = feature_order(place[0], place[1])
    column = iota((1, ROWS), 1).astype(F32)
    line = iota((ROWS, 1), 0).astype(F32)
    member = iota((1, 128), 1) & 63
    for k, piece in enumerate((zero, one, two, three)):
        at = slice(ROWS * k, ROWS * (k + 1))
        if k < 3:
            rows = tokens[:, :] if k == 0 else piece[48:, :]
            xhat[at, :] = normalized(dot(rows, order[:, :]))
        sizes = piece[16:32, 512:640].astype(F32)[12:13, 120:124]
        end = jnp.zeros((1, 1), F32)
        segment_line, segment_column = jnp.zeros((ROWS, 1), F32), jnp.zeros((1, ROWS), F32)
        first_line = jnp.zeros((ROWS, 1), F32)
        for s in range(4):
            size = sizes[:, s : s + 1]
            end = end + size
            first_line = first_line + jnp.where(line >= end, size, 0.0)
            segment_line = segment_line + jnp.where(line >= end, 1.0, 0.0)
            segment_column = segment_column + jnp.where(column >= end, 1.0, 0.0)
        lives = line < end
        mask = (line == column) | (lives & (segment_line == segment_column) & (column <= line))
        masks[at, :] = jnp.where(mask, 1.0, 0.0)
        angle = jnp.where(lives, line - first_line, 0.0) * frequency_lanes()
        cosine[at, :] = jnp.where(member < ROT, jnp.cos(angle), 1.0)
        sine[at, :] = jnp.where(member < ROT, jnp.sin(angle), 0.0) * jnp.where(
            member < ROT // 2, -1.0, 1.0
        )
        live[at, :] = jnp.where(lives, 1.0, 0.0)


def last_kernel(rows, order, xhat):
    xhat[:, :] = normalized(dot(rows[:ROWS, :], order[:, :]))


def turn(values, cosine, sine):
    member = iota((1, 384), 1) & 63
    ahead = pltpu.roll(values, 384 - ROT // 2, 1)
    behind = pltpu.roll(values, ROT // 2, 1)
    partner = jnp.where(member < ROT // 2, ahead, behind)
    return values * jnp.concatenate([cosine] * 3, axis=1) + partner * jnp.concatenate(
        [sine] * 3, axis=1
    )


def forward_kernel(place, xhat, xhat_last, masks, cosine, sine, *refs):
    columns = refs[:2]
    (
        mat_up, mat_qkv, h_one, h_two, act, slope, q_low, k_low, v_low, probs, mixed_slots, gains,
        mixed,
    ) = refs[2:]
    t, q = place[0], place[1]
    for kq in range(8):
        ref, at = columns[kq // 4], 192 * (kq % 4)
        mat_up[96 * kq : 96 * kq + 96, :] = ref[at : at + 96, :]
        mat_qkv[96 * kq : 96 * kq + 96, :] = ref[at + 96 : at + 192, :NARROW]

    slots, plain, of_qkv, of_up = all_places(t, q)
    packed = dot(vector_rows(), mat_qkv[:, VEC_AT:])
    vectors = jnp.concatenate([packed[32 * i : 32 * i + 32] for i in range(5)], axis=1)
    gain_one, bias_one, gain_two, bias_two = [
        spread(vectors[:, SHARD * i : SHARD * i + SHARD], slots) for i in range(4)
    ]
    vec_qkv = spread(vectors[:, 96:168], of_qkv)
    vec_up = spread(vectors[:, 192:288], of_up)
    vec_out = spread(vectors[:, 168:192], plain) + spread(vectors[:, 288:312], plain)
    gains[:, :] = jnp.concatenate([gain_one, gain_two, vec_out, jnp.zeros((5, WIDTH), F32)], axis=0)

    h_two[: 3 * ROWS, :] = (xhat[:, :] * gain_two + bias_two).astype(BF)
    h_two[3 * ROWS :, :] = (xhat_last[:, :] * gain_two + bias_two).astype(BF)
    up = dot(h_two[:, :], mat_up[:, :]) + vec_up
    phi = 0.5 * (1.0 + lax.erf(up * inv_sqrt_two))
    act[:, :] = (up * phi).astype(BF)
    slope[:, :] = phi + up * jnp.exp(-0.5 * up * up) * inv_sqrt_tau

    h_one[: 3 * ROWS, :] = (xhat[:, :] * gain_one + bias_one).astype(BF)
    h_one[3 * ROWS :, :] = (xhat_last[:, :] * gain_one + bias_one).astype(BF)
    qkv = dot(h_one[:, :], mat_qkv[:, :VEC_AT]) + vec_qkv
    turned = turn(qkv[:, : 2 * QUARTER], cosine[:, :], sine[:, :])
    q_low[:, :] = turned[:, :QUARTER].astype(BF)
    k_low[:, :] = turned[:, QUARTER:].astype(BF)
    v_low[:, :] = qkv[:, 2 * QUARTER :].astype(BF)
    for k in range(TP):
        at = slice(ROWS * k, ROWS * (k + 1))
        for head in range(G_HEADS):
            lanes = slice(HEAD * head, HEAD * (head + 1))
            scores = dot(q_low[at, lanes], k_low[at, lanes], 1, 1) * 0.125
            scores = jnp.where(masks[at, :] > 0.0, scores, neg_large)
            exponent = jnp.exp(scores - jnp.max(scores, axis=-1, keepdims=True))
            chances = exponent / jnp.sum(exponent, axis=-1, keepdims=True)
            probs[G_HEADS * k + head] = chances
            mixed[at, lanes] = dot(chances.astype(BF), v_low[at, lanes]).astype(BF)
    mixed_slots[:, :] = dot(mixed[:, :], head_order(q)).astype(BF)


def share_kernel(place, act, mixed_slots, *refs):
    tails, down, out_mat, shares = refs[:2], refs[2], refs[3], refs[4:]
    q = place[1]
    for kq in range(8):
        ref, at = tails[kq // 4], 128 * (kq % 4)
        first = pl.multiple_of((q ^ kq) * 96, 32)
        down[pl.ds(first, 96), :] = ref[at : at + 96, :]
        out_mat[32 * kq : 32 * kq + 32, :] = ref[at + 96 : at + 128, :]
    total = dot(act[:, :], down[:, :]) + dot(mixed_slots[:, :], out_mat[:, :])
    for k in range(TP):
        shares[k][:, :] = total[ROWS * k : ROWS * (k + 1)].astype(shares[k].dtype)


def upstream_kernel(place, *refs):
    cots = refs[:4]
    (
        live, h_two, act, slope, mixed_slots, down, out_mat, d_up, d_mixed, keep, send,
        upstream, grad_down,
    ) = refs[4:]
    q = place[1]
    for k in range(TP):
        at = slice(ROWS * k, ROWS * (k + 1))
        last = cots[k].shape[0]
        upstream[at, :] = (cots[k][last - ROWS :, :].astype(F32) * live[at, :]).astype(BF)
    d_up[:, :] = (dot(upstream[:, :], down[:, :], 1, 1) * slope[:, :]).astype(BF)
    grad_up = dot(h_two[:, :], d_up[:, :], 0, 0)
    grad_down[:, :] = dot(act[:, :], upstream[:, :], 0, 0)
    grad_out = dot(mixed_slots[:, :], upstream[:, :], 0, 0)
    for kq in range(8):
        target = keep if kq < 4 else send
        at = 224 * (kq % 4)
        first = pl.multiple_of((q ^ kq) * 96, 32)
        target[at : at + 96, :] = grad_down[pl.ds(first, 96), :].astype(target.dtype)
        target[at + 96 : at + 128, :] = grad_out[32 * kq : 32 * kq + 32].astype(target.dtype)
        target[at + 128 : at + 224, :] = grad_up[96 * kq : 96 * kq + 96].astype(target.dtype)
    d_slots = dot(upstream[:, :], out_mat[:, :], 1, 1).astype(BF)
    d_mixed[:, :] = dot(d_slots, head_order(q), 1, 1).astype(BF)


def attention_kernel(
    q_low, k_low, v_low, probs, d_mixed, cosine, sine, d_qkv, d_turned
):
    for k in range(TP):
        at = slice(ROWS * k, ROWS * (k + 1))
        for head in range(G_HEADS):
            lanes = slice(HEAD * head, HEAD * (head + 1))
            chances = probs[G_HEADS * k + head]
            d_out = d_mixed[at, lanes]
            d_probs = dot(d_out, v_low[at, lanes], 1, 1)
            delta = jnp.sum(chances * d_probs, axis=-1, keepdims=True)
            d_scores = (chances * (d_probs - delta)).astype(BF)
            d_turned[at, lanes] = dot(d_scores, k_low[at, lanes]) * 0.125
            d_turned[at, QUARTER + HEAD * head : QUARTER + HEAD * (head + 1)] = (
                dot(d_scores, q_low[at, lanes], 0, 0) * 0.125
            )
            d_qkv[at, 2 * QUARTER + HEAD * head : 2 * QUARTER + HEAD * (head + 1)] = dot(
                chances.astype(BF), d_out, 0, 0
            ).astype(BF)
    d_qkv[:, : 2 * QUARTER] = turn(d_turned[:, :], cosine[:, :], -sine[:, :]).astype(BF)


def backward_kernel(
    place, xhat, xhat_last, order, mat_up, mat_qkv, h_one, d_up, d_qkv, gains, cot, live, *refs
):
    shares, (keep, send) = refs[:4], refs[4:]
    t, q = place[0], place[1]
    d_one = dot(d_qkv[:, :], mat_qkv[:, :VEC_AT], 1, 1)
    d_two = dot(d_up[:, :], mat_up[:, :], 1, 1)
    share = (d_one * gains[0:1, :] + d_two * gains[1:2, :]).astype(BF)
    share = dot(share, order[:, :], 1, 1)
    for k in range(TP):
        shares[k][:, :] = share[ROWS * k : ROWS * (k + 1)].astype(shares[k].dtype)

    slots, plain, of_qkv, of_up = all_places(t, q)

    def total(rows):
        return jnp.sum(rows, axis=0, keepdims=True)

    def with_xhat(rows):
        return total(rows[: 3 * ROWS] * xhat[:, :]) + total(rows[3 * ROWS :] * xhat_last[:, :])

    vectors = jnp.concatenate(
        [
            collect(with_xhat(d_one), slots),
            collect(total(d_one), slots),
            collect(with_xhat(d_two), slots),
            collect(total(d_two), slots),
            collect(total(cot[:, :].astype(F32) * live[:ROWS, :]), plain),
            collect(total(d_qkv[:, :].astype(F32)), of_qkv),
            collect(total(d_up[:, :].astype(F32)), of_up),
            jnp.zeros((32, 32), F32),
        ],
        axis=1,
    ).astype(BF)
    packed = jnp.concatenate([vectors[:, 64 * i : 64 * i + 64] for i in range(5)], axis=0)
    grads = jnp.concatenate(
        [dot(h_one[:, :], d_qkv[:, :], 0, 0), dot(vector_rows(), packed, 0, 0)], axis=1
    )
    keep[:, :] = grads[:384]
    send[:, :] = grads[384:].astype(BF)


def columns_kernel(place, zero, one, two, three, qkv, up, *vectors):
    t = place[0]
    parts = [zero[:, :]] + [ref[:, :].astype(F32) for ref in (one, two, three)]
    for rank in range(TP):

        @pl.when(t == rank)
        def _(rank=rank):
            by_rank = [parts[rank ^ s] for s in range(TP)]
            up[:, :] = jnp.concatenate([item[:, :WIDTH] for item in by_rank], axis=1)
            qkv[:, :] = jnp.concatenate(
                [
                    item[:, WIDTH + QUARTER * i : WIDTH + QUARTER * (i + 1)]
                    for i in range(3)
                    for item in by_rank
                ],
                axis=1,
            )

    packed = sum(item[:8, WIDTH + VEC_AT :] for item in parts)
    row = jnp.concatenate([packed[i : i + 1] for i in range(5)], axis=1)
    at = 0
    for ref in vectors[:-1]:
        size = ref.shape[1]
        ref[:, :] = row[:, at : at + size]
        at += size
    vectors[-1][:, :] = row[:, 4 * SHARD : 5 * SHARD]


def output_kernel(zero, one, two, three, tokens, live, gains, output):
    share = zero[:, :] + one[:, :].astype(F32) + two[:, :].astype(F32) + three[:, :].astype(F32)
    output[:, :] = (live[:ROWS, :] * (tokens[:, :].astype(F32) + share + gains[2:3, :])).astype(BF)


def input_kernel(zero, one, two, three, tokens, cot, live, grad):
    e = zero[:, :] + one[:, :].astype(F32) + two[:, :].astype(F32) + three[:, :].astype(F32)
    rows = tokens[:, :].astype(F32)
    removed = rows - jnp.mean(rows, axis=-1, keepdims=True)
    rstd = lax.rsqrt(jnp.mean(removed * removed, axis=-1, keepdims=True) + epsilon)
    xhat = removed * rstd
    dx = rstd * (
        e - jnp.mean(e, axis=-1, keepdims=True) - xhat * jnp.mean(e * xhat, axis=-1, keepdims=True)
    )
    grad[:, :] = cot[:, :].astype(F32) * live[:ROWS, :] + dx


def call(kernel, name, outs, *args, scratch=(), mib=16, weight=1):
    space = [pl.BlockSpec(memory_space=pltpu.VMEM)] * len(args)
    if args[0].dtype == jnp.int32:
        space[0] = pl.BlockSpec(memory_space=pltpu.SMEM)
    shapes = [jax.ShapeDtypeStruct(shape, kind) for shape, kind in outs]
    return pl.pallas_call(
        kernel,
        name=name,
        out_shape=shapes,
        in_specs=space,
        out_specs=[pl.BlockSpec(memory_space=pltpu.VMEM)] * len(shapes),
        scratch_shapes=[pltpu.VMEM(shape, kind) for shape, kind in scratch],
        cost_estimate=pl.CostEstimate(flops=weight * 10**9, transcendentals=0, bytes_accessed=weight * 10**6),
        compiler_params=pltpu.CompilerParams(vmem_limit_bytes=mib * 1024 * 1024),
    )(*args)


def after(array, *others):
    return lax.optimization_barrier((array, others))[0]


def xor_permutes(block, axis, count):
    return [lax.ppermute(block, axis, xor_pairs(count, k)) for k in range(1, 4)]


def plane_pair(keep, send):
    return keep + lax.ppermute(send, "dq", xor_pairs(2, 1)).astype(F32)


def plane_relay(pair):
    rows = pair.shape[0] // 4
    three = pair[3 * rows :].astype(BF)
    upper = lax.ppermute(three[: rows // 2], "fsdp", xor_pairs(4, 1))
    lower = lax.ppermute(three[rows // 2 :], "fsdp", xor_pairs(4, 2))
    return upper, lower


def plane_last(pair, upper, lower):
    rows = pair.shape[0] // 4
    half = rows // 2
    mine, one, two = [pair[rows * k : rows * (k + 1)] for k in range(3)]
    two = jnp.concatenate([two[:half] + upper.astype(F32), two[half:]], axis=0)
    one = jnp.concatenate([one[:half], one[half:] + lower.astype(F32)], axis=0)
    one = lax.ppermute(one.astype(BF), "fsdp", xor_pairs(4, 1))
    two = lax.ppermute(two.astype(BF), "fsdp", xor_pairs(4, 2))
    return mine + one.astype(F32) + two.astype(F32)


def plane_local(
    tokens, lengths, ln_attn_gain, ln_attn_bias, ln_mlp_gain, ln_mlp_bias, w_qkv, b_qkv,
    w_out, b_out, w_fc1, b_fc1, w_fc2, b_fc2, cotangent,
):
    t = lax.axis_index("t")
    q = lax.axis_index("dq") * 4 + lax.axis_index("fsdp")
    place = jnp.stack([t, q]).astype(jnp.int32)
    vector = jnp.concatenate(
        [
            ln_attn_gain, ln_attn_bias, ln_mlp_gain, ln_mlp_bias, b_qkv, b_out, b_fc1, b_fc2,
            lengths[0].astype(BF), jnp.zeros((68,), BF),
        ]
    )
    block = (ROWS, WIDTH)
    piece = ((48, WIDTH), BF)
    piece_rows = ((48 + ROWS, WIDTH), BF)
    tail = jnp.concatenate([w_fc2, w_out, jnp.zeros((8, WIDTH), BF)], axis=0)
    weights = jnp.concatenate([w_fc1, w_qkv], axis=1)
    pieces = call(
        prepare_kernel, "prepare", [piece, piece_rows, piece_rows, piece],
        place, weights, vector.astype(F32)[None], tokens,
        weight=10,
    )
    prepared = pieces
    pieces = exchange_t(pieces)
    token_one = pieces[1]
    both = after(jnp.concatenate([tokens, cotangent], axis=0), token_one)
    rows_three = lax.ppermute(both, "t", xor_pairs(TP, 3))
    tail = after(tail, prepared)
    tail_one = lax.ppermute(tail, "fsdp", xor_pairs(4, 1))
    tail_two = lax.ppermute(tail, "fsdp", xor_pairs(4, 2))
    tail_three = lax.ppermute(after(tail, tail_one), "fsdp", xor_pairs(4, 3))
    (columns,) = call(merge_kernel, "merge", [((192, WIDTH), BF)], *pieces, weight=10)
    columns = after(columns, tail_one, tail_two, tail_three)
    arrived = xor_permutes(columns, "fsdp", 4)
    columns = jnp.concatenate([columns] + arrived, axis=0)
    columns = [columns, lax.ppermute(columns, "dq", xor_pairs(2, 1))]
    wide = (COUNT, WIDTH)
    square = ((COUNT, 128), F32)
    xhat, order, masks, cosine, sine, lives = call(
        early_kernel,
        "early",
        [((3 * ROWS, WIDTH), F32), ((WIDTH, WIDTH), BF), square, square, square, ((COUNT, 1), F32)],
        place, *pieces, tokens,
        weight=10,
    )
    (xhat_last,) = call(
        last_kernel, "last", [(block, F32)], rows_three, order, weight=5
    )
    cot_one = lax.ppermute(after(cotangent, xhat_last), "t", xor_pairs(TP, 1))
    cot_two = lax.ppermute(after(cotangent, xhat_last), "t", xor_pairs(TP, 2))
    cot_slots = [cot_one, cot_two, rows_three]
    third = (COUNT, QUARTER)
    (
        mat_up, mat_qkv, h_one, h_two, act, slope, q_low, k_low, v_low, probs, mixed_slots, gains,
    ) = call(
        forward_kernel,
        "forward",
        [
            ((WIDTH, WIDTH), BF), ((WIDTH, NARROW), BF),
            (wide, BF), (wide, BF), (wide, BF), (wide, F32), (third, BF), (third, BF),
            (third, BF), ((HEADS, ROWS, ROWS), F32), ((COUNT, 256), BF), ((8, WIDTH), F32),
        ],
        place, xhat, xhat_last, masks, cosine, sine, *columns,
        scratch=[(third, BF)],
        weight=100,
    )
    tail = jnp.concatenate([tail, tail_one, tail_two, tail_three], axis=0)
    tail = [tail, lax.ppermute(tail, "dq", xor_pairs(2, 1))]
    shares = [(block, F32)] + [(block, BF)] * 3
    down, out_mat, *out = call(
        share_kernel, "share", [((WIDTH, WIDTH), BF), ((256, WIDTH), BF)] + shares,
        place, act, mixed_slots, *tail,
        weight=10,
    )
    out = exchange_t(out)
    d_up, d_mixed, tail_keep, tail_send = call(
        upstream_kernel,
        "upstream",
        [(wide, BF), (third, BF), ((896, WIDTH), F32), ((896, WIDTH), BF)],
        place, cotangent, *cot_slots, lives, h_two, act, slope, mixed_slots, down, out_mat,
        scratch=[(wide, BF), ((WIDTH, WIDTH), F32)],
        weight=40,
    )
    tail_pair = plane_pair(tail_keep, tail_send)
    (d_qkv,) = call(
        attention_kernel, "attention", [((COUNT, 3 * QUARTER), BF)],
        q_low, k_low, v_low, probs, d_mixed, cosine, sine,
        scratch=[((COUNT, 2 * QUARTER), F32)],
        weight=50,
    )
    tail_got = plane_relay(tail_pair)
    d_qkv = after(d_qkv, tail_pair, out[1])
    *e, col_keep, col_send = call(
        backward_kernel,
        "backward",
        shares + [((384, NARROW), F32), ((384, NARROW), BF)],
        place, xhat, xhat_last, order, mat_up, mat_qkv, h_one, d_up, d_qkv, gains, cotangent, lives,
        weight=40,
    )
    col_pair = plane_pair(col_keep, after(col_send, tail_got, out[2:]))
    col_got = plane_relay(col_pair)
    e = [after(item, out) for item in e]
    e[3] = after(e[3], col_pair)
    e = exchange_t(e)
    col_sum = plane_last(col_pair, *col_got)
    tail_sum = plane_last(after(tail_pair, col_got), *tail_got)
    col_sum = jnp.concatenate([tail_sum[128:], col_sum], axis=1)
    low_sum = col_sum.astype(BF)
    back = [low_sum[SHARD * k : SHARD * (k + 1)] for k in range(TP)]
    arrived = exchange_t(back)
    tail_sum = after(tail_sum, low_sum)
    (output,) = call(
        output_kernel, "output", [(block, BF)], *out, tokens, after(lives, col_keep), gains,
        weight=10,
    )
    (grad_tokens,) = call(
        input_kernel, "input_gradient", [(block, F32)], *e, tokens, cotangent, lives,
        weight=10,
    )
    sizes = [SHARD] * 5 + [3 * SHARD, 4 * SHARD, SHARD]
    shard_qkv, shard_up, *vectors = call(
        columns_kernel, "columns",
        [((SHARD, 3 * WIDTH), F32), ((SHARD, 4 * WIDTH), F32)] + [((1, n), F32) for n in sizes],
        place, col_sum[:SHARD], *arrived[1:],
    )
    g_one, b_one, g_two, b_two, branch, qkv_bias, up_bias, again = [item[0] for item in vectors]
    return (
        output, grad_tokens, g_one, b_one, g_two, b_two, shard_qkv, qkv_bias,
        tail_sum[96 : 96 + SHARD], branch, shard_up, up_bias, tail_sum[:96], again,
    )


def local(
    sizes,
    tokens,
    lengths,
    ln_attn_gain,
    ln_attn_bias,
    ln_mlp_gain,
    ln_mlp_bias,
    w_qkv,
    b_qkv,
    w_out,
    b_out,
    w_fc1,
    b_fc1,
    w_fc2,
    b_fc2,
    cotangent,
):
    if sizes == (2, 4) and w_qkv.shape == (SHARD, 3 * WIDTH) and tokens.shape == (ROWS, WIDTH):
        return plane_local(
            tokens, lengths, ln_attn_gain, ln_attn_bias, ln_mlp_gain, ln_mlp_bias, w_qkv, b_qkv,
            w_out, b_out, w_fc1, b_fc1, w_fc2, b_fc2, cotangent,
        )
    t = lax.axis_index("t")
    q = lax.axis_index("dq") * sizes[1] + lax.axis_index("fsdp")
    qs = sizes[0] * sizes[1]
    rows, width = tokens.shape
    shard = w_qkv.shape[0]
    part = width // TP
    hidden = w_fc1.shape[1] // TP
    units = w_fc2.shape[0]
    heads = HEADS // TP

    vectors = jnp.concatenate(
        [
            item.reshape(shard, -1)
            for item in (
                ln_attn_gain, ln_attn_bias, ln_mlp_gain, ln_mlp_bias, b_qkv, b_out, b_fc1, b_fc2
            )
        ],
        axis=1,
    )
    n_vec = vectors.shape[1]
    low_lengths = jnp.broadcast_to(lengths.astype(BF), (shard, lengths.shape[1]))
    small = jnp.concatenate([vectors, low_lengths], axis=1)
    qkv_parts = w_qkv.reshape(shard, 3, TP, part)
    fc1_parts = w_fc1.reshape(shard, TP, hidden)
    pieces = [
        jnp.concatenate(
            [
                pick(qkv_parts, t ^ k, 2).reshape(shard, 3 * part),
                small,
                pick(fc1_parts, t ^ k, 1),
            ],
            axis=1,
        )
        for k in range(TP)
    ]
    pieces = exchange_t(pieces)
    at = 3 * part
    group_lengths = [piece[0, at + n_vec : at + n_vec + 4].astype(jnp.int32) for piece in pieces]
    mine = jnp.stack(unxor(pieces, t))
    columns = gather_q(mine, q, sizes)
    columns = columns.transpose(1, 0, 2, 3).reshape(width, -1)
    mat_qkv = columns[:, : 3 * part]
    vecs = columns[:, at : at + n_vec].astype(F32)
    mat_up = columns[:, at + small.shape[1] :]
    tail = gather_q(jnp.concatenate([w_fc2, w_out], axis=0), q, sizes)
    mat_down = tail[:, :units].reshape(qs * units, width)
    mat_out = tail[:, units:].reshape(part, width)

    vecs_t = vecs.T
    gain_one, bias_one, gain_two, bias_two = vecs_t[0], vecs_t[1], vecs_t[2], vecs_t[3]
    all_b_qkv = vecs[:, 4:7].reshape(3, TP, part)
    vec_qkv = pick(all_b_qkv, t, 1).reshape(3 * part)
    vec_out = vecs_t[7]
    vec_up = pick(vecs[:, 8:12].reshape(TP, hidden), t)
    vec_down = vecs_t[12]

    token_slots = gather_t(tokens, t)
    upstream_slots = gather_t(cotangent, t)
    layouts = [layout(item, rows) for item in group_lengths]
    live = jnp.concatenate([item[0] for item in layouts])[:, None]
    attn_mask = jnp.stack([item[1] for item in layouts])[:, None]
    cosine = jnp.concatenate([item[2] for item in layouts])
    sine = jnp.concatenate([item[3] for item in layouts])
    resid = jnp.concatenate(token_slots).astype(F32)
    upstream_low = jnp.concatenate(upstream_slots) * live.astype(BF)

    center = jnp.mean(resid, axis=-1, keepdims=True)
    removed = resid - center
    rstd = lax.rsqrt(jnp.mean(removed * removed, axis=-1, keepdims=True) + epsilon)
    xhat = removed * rstd
    low_one = (xhat * gain_one + bias_one).astype(BF)
    low_two = (xhat * gain_two + bias_two).astype(BF)

    up_rows = contract(low_two, mat_up, 1, 0) + vec_up
    phi = 0.5 * (1.0 + lax.erf(up_rows * inv_sqrt_two))
    act_low = (up_rows * phi).astype(BF)
    slope = phi + up_rows * jnp.exp(-0.5 * up_rows * up_rows) * inv_sqrt_tau
    mlp_share = contract(act_low, mat_down, 1, 0)
    grad_down = contract(act_low, upstream_low, 0, 0)
    d_up_low = (contract(upstream_low, mat_down, 1, 1) * slope).astype(BF)
    grad_up = contract(low_two, d_up_low, 0, 0)
    grad_up_bias = jnp.sum(d_up_low.astype(F32), axis=0)
    d_h2 = contract(d_up_low, mat_up, 1, 1)

    count = TP * rows
    qkv = (contract(low_one, mat_qkv, 1, 0) + vec_qkv).reshape(count, 3, heads, HEAD)
    q_low = rotate(qkv[:, 0], cosine, sine).astype(BF).reshape(TP, rows, heads, HEAD)
    k_low = rotate(qkv[:, 1], cosine, sine).astype(BF).reshape(TP, rows, heads, HEAD)
    v_low = qkv[:, 2].astype(BF).reshape(TP, rows, heads, HEAD)
    scores = jnp.einsum("gqhd,gkhd->ghqk", q_low, k_low, preferred_element_type=F32) * 0.125
    scores = jnp.where(attn_mask, scores, neg_large)
    exponent = jnp.exp(scores - jnp.max(scores, axis=-1, keepdims=True))
    probs = exponent / jnp.sum(exponent, axis=-1, keepdims=True)
    probs_low = probs.astype(BF)
    mixed = jnp.einsum("ghqk,gkhd->gqhd", probs_low, v_low, preferred_element_type=F32)
    mixed_low = mixed.reshape(count, part).astype(BF)
    out_share = (mlp_share + contract(mixed_low, mat_out, 1, 0)).reshape(TP, rows, width)
    out_sum = scatter_t([out_share[k] for k in range(TP)])
    output = live[:rows] * (resid[:rows] + out_sum + vec_out + vec_down)

    grad_out = contract(mixed_low, upstream_low, 0, 0)
    d_mixed = contract(upstream_low, mat_out, 1, 1).astype(BF).reshape(TP, rows, heads, HEAD)
    d_probs = jnp.einsum("gqhd,gkhd->ghqk", d_mixed, v_low, preferred_element_type=F32)
    d_values = jnp.einsum("ghqk,gqhd->gkhd", probs_low, d_mixed, preferred_element_type=F32)
    delta = jnp.sum(probs * d_probs, axis=-1, keepdims=True)
    d_scores = (probs * (d_probs - delta)).astype(BF)
    d_query = jnp.einsum("ghqk,gkhd->gqhd", d_scores, k_low, preferred_element_type=F32) * 0.125
    d_keys = jnp.einsum("ghqk,gqhd->gkhd", d_scores, q_low, preferred_element_type=F32) * 0.125
    d_query = rotate(d_query.reshape(count, heads, HEAD), cosine, -sine).reshape(count, part)
    d_keys = rotate(d_keys.reshape(count, heads, HEAD), cosine, -sine).reshape(count, part)
    d_qkv = jnp.concatenate([d_query, d_keys, d_values.reshape(count, part)], axis=1).astype(BF)
    grad_qkv = contract(low_one, d_qkv, 0, 0)
    grad_qkv_bias = jnp.sum(d_qkv.astype(F32), axis=0)
    d_h1 = contract(d_qkv, mat_qkv, 1, 1)

    e_share = (d_h1 * gain_one + d_h2 * gain_two).reshape(TP, rows, width)
    e_sum = scatter_t([e_share[k] for k in range(TP)])
    own_xhat = xhat[:rows]
    dx = rstd[:rows] * (
        e_sum
        - jnp.mean(e_sum, axis=-1, keepdims=True)
        - own_xhat * jnp.mean(e_sum * own_xhat, axis=-1, keepdims=True)
    )
    own_upstream = upstream_low[:rows].astype(F32)
    grad_tokens = own_upstream + dx

    zero_qkv = jnp.zeros((3, TP, part), F32)
    full_b_qkv = lax.dynamic_update_index_in_dim(
        zero_qkv, grad_qkv_bias.reshape(3, 1, part), t, 1
    ).reshape(width, 3)
    zero_up = jnp.zeros((TP, hidden), F32)
    full_b_up = lax.dynamic_update_index_in_dim(zero_up, grad_up_bias[None], t, 0).reshape(width, 4)
    lanes = jnp.stack(
        [
            jnp.sum(d_h1 * xhat, axis=0),
            jnp.sum(d_h1, axis=0),
            jnp.sum(d_h2 * xhat, axis=0),
            jnp.sum(d_h2, axis=0),
            jnp.sum(own_upstream, axis=0),
        ],
        axis=1,
    )
    vec_grads = jnp.concatenate([lanes, full_b_qkv, full_b_up], axis=1)

    tail_grads = jnp.concatenate(
        [grad_down.reshape(qs, units, width), grad_out.reshape(qs, shard, width)], axis=1
    )
    tail_sum = scatter_q(tail_grads, q, sizes)
    shard_down, shard_out = tail_sum[:units], tail_sum[units:]
    column_grads = jnp.concatenate([grad_qkv, vec_grads, grad_up], axis=1)
    column_grads = column_grads.reshape(TP, qs, shard, -1).transpose(1, 0, 2, 3)
    column_sum = scatter_q(column_grads, q, sizes)
    low_sum = column_sum.astype(BF)
    got = exchange_t([pick(low_sum, t ^ k) for k in range(TP)])
    got = [pick(column_sum, t)] + [item.astype(F32) for item in got[1:]]
    vec_sum = sum(item[:, at : at + 12] for item in got)
    got = jnp.stack(unxor(got, t))
    shard_qkv = (
        got[:, :, : 3 * part].reshape(TP, shard, 3, part).transpose(1, 2, 0, 3).reshape(shard, -1)
    )
    shard_up = got[:, :, at + 12 :].transpose(1, 0, 2).reshape(shard, -1)
    shard_branch_bias = vec_sum[:, 4]
    return (
        output.astype(BF),
        grad_tokens,
        vec_sum[:, 0],
        vec_sum[:, 1],
        vec_sum[:, 2],
        vec_sum[:, 3],
        shard_qkv,
        vec_sum[:, 5:8].reshape(-1),
        shard_out,
        shard_branch_bias,
        shard_up,
        vec_sum[:, 8:12].reshape(-1),
        shard_down,
        shard_branch_bias,
    )


def solution(mesh):
    nd, nf = mesh.shape["dp"], mesh.shape["fsdp"]
    sizes = (nd // TP, nf)
    inner = Mesh(mesh.devices.reshape((TP,) + sizes), ("t", "dq", "fsdp"))
    axes = ("t", "dq", "fsdp")
    matrix, vector = P(axes, None), P(axes)
    return jax.shard_map(
        lambda *args: local(sizes, *args),
        mesh=inner,
        in_specs=(
            matrix, matrix, vector, vector, vector, vector, matrix, vector,
            matrix, vector, matrix, vector, matrix, vector, matrix,
        ),
        out_specs=(
            matrix, matrix, vector, vector, vector, vector, matrix, vector,
            matrix, vector, matrix, vector, matrix, vector,
        ),
        check_vma=False,
    )
```

```python
import math

import jax
import jax.numpy as jnp
from jax import lax
from jax.experimental import pallas as pl
from jax.experimental.pallas import tpu as pltpu
from jax.sharding import Mesh
from jax.sharding import PartitionSpec as P

HEADS = 12
HEAD = 64
ROT = 16
TP = 4
BF = jnp.bfloat16
F32 = jnp.float32

epsilon = 1e-05
neg_large = -1e30
inv_sqrt_two = 1.0 / math.sqrt(2.0)
inv_sqrt_tau = 1.0 / math.sqrt(2.0 * math.pi)


def xor_pairs(count, bit):
    return [(i, i ^ bit) for i in range(count)]


def pick(array, index, axis=0):
    return lax.dynamic_index_in_dim(array, index, axis, keepdims=False)


def unxor(slots, rank):
    bit = 1
    while bit < len(slots):
        flip = (rank & bit) != 0
        slots = [jnp.where(flip, slots[k ^ bit], slots[k]) for k in range(len(slots))]
        bit *= 2
    return slots


def gather_t(block, rank):
    one = lax.ppermute(block, "t", xor_pairs(TP, 1))
    two = lax.ppermute(block, "t", xor_pairs(TP, 2))
    near = lax.ppermute(block, "t", [(1, 2), (2, 1)])
    far = lax.ppermute(two, "t", [(2, 3), (1, 0)])
    middle = (rank == 1) | (rank == 2)
    return [block, one, two, jnp.where(middle, near, far)]


def scatter_t(slots):
    low = [slot.astype(BF) for slot in slots]
    one = lax.ppermute(low[1], "t", xor_pairs(TP, 1))
    near = lax.ppermute(low[3], "t", [(1, 2), (2, 1)])
    relay = lax.ppermute(low[3], "t", [(0, 1), (3, 2)])
    two = lax.ppermute((slots[2] + relay.astype(F32)).astype(BF), "t", xor_pairs(TP, 2))
    return slots[0] + one.astype(F32) + near.astype(F32) + two.astype(F32)


def exchange_t(pieces):
    return [pieces[0]] + [
        lax.ppermute(pieces[k], "t", xor_pairs(TP, k)) for k in range(1, TP)
    ]


def gather_q(block, rank, sizes):
    if sizes != (2, 4):
        return lax.all_gather(block, ("dq", "fsdp"), axis=0, tiled=False)
    half = block.shape[0] // 2
    one = lax.ppermute(block, "fsdp", xor_pairs(4, 1))
    two = lax.ppermute(block, "fsdp", xor_pairs(4, 2))
    upper = lax.ppermute(one[:half], "fsdp", xor_pairs(4, 2))
    lower = lax.ppermute(two[half:], "fsdp", xor_pairs(4, 1))
    three = jnp.concatenate([upper, lower], axis=0)
    mine = [block, one, two, three]
    other = [lax.ppermute(part, "dq", xor_pairs(2, 1)) for part in mine]
    return jnp.stack(unxor(mine + other, rank))


def scatter_q(blocks, rank, sizes):
    if sizes != (2, 4):
        return lax.psum_scatter(
            blocks.astype(BF), ("dq", "fsdp"), scatter_dimension=0, tiled=False
        ).astype(F32)
    core, spot = rank // 4, rank % 4
    halves = blocks.reshape((2, 4) + blocks.shape[1:])
    keep = pick(halves, core)
    send = pick(halves, 1 - core).astype(BF)
    pair = keep + lax.ppermute(send, "dq", xor_pairs(2, 1)).astype(F32)
    mine, one, two, three = [pick(pair, spot ^ k) for k in range(4)]
    half = mine.shape[0] // 2
    three = three.astype(BF)
    upper = lax.ppermute(three[:half], "fsdp", xor_pairs(4, 1))
    lower = lax.ppermute(three[half:], "fsdp", xor_pairs(4, 2))
    two = jnp.concatenate([two[:half] + upper.astype(F32), two[half:]], axis=0)
    one = jnp.concatenate([one[:half], one[half:] + lower.astype(F32)], axis=0)
    one = lax.ppermute(one.astype(BF), "fsdp", xor_pairs(4, 1))
    two = lax.ppermute(two.astype(BF), "fsdp", xor_pairs(4, 2))
    return mine + one.astype(F32) + two.astype(F32)


def layout(seq_lengths, row_count):
    row_index = jnp.arange(row_count, dtype=jnp.int32)
    slot_count = seq_lengths.shape[0]
    ends = jnp.cumsum(seq_lengths)
    starts = ends - seq_lengths
    segment = jnp.sum((row_index[:, None] >= ends[None, :]).astype(jnp.int32), axis=1)
    live_rows = row_index < ends[-1]
    unique_seg = jnp.where(live_rows, segment, slot_count + row_index)
    slot_index = jnp.arange(slot_count, dtype=jnp.int32)
    first_row = jnp.sum(
        jnp.where(segment[:, None] == slot_index[None, :], starts[None, :], 0), axis=1
    )
    position = jnp.where(live_rows, row_index - first_row, 0)
    attn_mask = (unique_seg[:, None] == unique_seg[None, :]) & (
        row_index[None, :] <= row_index[:, None]
    )
    half_rot = ROT // 2
    inverse_freq = 10000.0 ** (-(2.0 * jnp.arange(half_rot, dtype=jnp.float32)) / ROT)
    angle = position.astype(jnp.float32)[:, None] * inverse_freq[None, :]
    return (
        live_rows.astype(jnp.float32),
        attn_mask,
        jnp.cos(angle)[:, None, :],
        jnp.sin(angle)[:, None, :],
    )


def rotate(part, cosine, sine):
    half_rot = ROT // 2
    first = part[..., :half_rot]
    second = part[..., half_rot:ROT]
    return jnp.concatenate(
        [first * cosine - second * sine, second * cosine + first * sine, part[..., ROT:]], axis=-1
    )


def contract(left, right, left_dim, right_dim):
    return lax.dot_general(
        left, right, (((left_dim,), (right_dim,)), ((), ())), preferred_element_type=F32
    )


ROWS = 128
COUNT = TP * ROWS
WIDTH = 768
SHARD = 24
VEC_AT = 576
NARROW = 640
G_HEADS = HEADS // TP
QUARTER = WIDTH // TP


def iota(shape, axis):
    return lax.broadcasted_iota(jnp.int32, shape, axis)


def split(number, by):
    quotient = jnp.floor((number.astype(F32) + 0.5) * (1.0 / by)).astype(jnp.int32)
    return quotient, number - quotient * by


def hot(condition):
    return jnp.where(condition, 1.0, 0.0).astype(BF)


def owner_of_block(block, t, q):
    return ((block & 3) ^ t) * 8 + ((block >> 2) ^ q)


def feature_order(t, q):
    block, row = split(iota((1, WIDTH), 1), SHARD)
    return hot(iota((WIDTH, 1), 0) == owner_of_block(block, t, q) * SHARD + row)


def head_order(q):
    lane = iota((1, 256), 1)
    row = lane & 31
    place = ((lane >> 5) ^ q) * SHARD + row
    place = jnp.where(row < SHARD, place, -1)
    return hot(iota((QUARTER, 1), 0) == place)


def vector_rows():
    at = iota((160, 1), 0)
    return hot(iota((1, WIDTH), 1) == (at & 31) * SHARD + (at >> 5))


def dot(left, right, left_dim=1, right_dim=0):
    return lax.dot_general(
        left, right, (((left_dim,), (right_dim,)), ((), ())), preferred_element_type=F32
    )


def placing(number, length, owners):
    owner, element = split(number, length)
    return jnp.where(owners == owner, 1.0, 0.0), hot(iota((length, 1), 0) == element)


def all_places(t, q):
    block = iota((32, 1), 0)
    owners = owner_of_block(block, t, q)
    lane = iota((1, WIDTH), 1)
    third, rest = split(iota((1, 3 * QUARTER), 1), QUARTER)
    return (
        placing(lane, SHARD, block),
        placing(lane, SHARD, owners),
        placing(third * WIDTH + t * QUARTER + rest, 3 * SHARD, owners),
        placing(lane + t * WIDTH, 4 * SHARD, owners),
    )


def spread(values, places):
    mask, element = places
    return jnp.sum(dot(values.astype(BF), element) * mask, axis=0, keepdims=True)


def collect(row, places):
    mask, element = places
    return dot((mask * row).astype(BF), element, 1, 1)


def prepare_kernel(place, weights, vector, tokens, *pieces):
    w_fc1, w_qkv = weights.at[:, : 4 * WIDTH], weights.at[:, 4 * WIDTH :]
    t = place[0]
    row = iota((SHARD, 64), 0)
    packed = jnp.zeros((SHARD, 64), F32)
    for i in range(5):
        packed = jnp.where(row == i, vector[:, 64 * i : 64 * i + 64], packed)
    packed = jnp.concatenate([packed.astype(BF), jnp.zeros((SHARD, 128), BF)], axis=1)
    for item in pieces:
        if item.shape[0] > 48:
            item[48:, :] = tokens[:, :]
    for rank in range(TP):

        @pl.when(t == rank)
        def _(rank=rank):
            for k in range(TP):
                r = rank ^ k
                at = QUARTER * r
                lower = jnp.concatenate(
                    [
                        w_qkv[:, at : at + QUARTER],
                        w_qkv[:, WIDTH + at : WIDTH + at + QUARTER],
                        w_qkv[:, 2 * WIDTH + at : 2 * WIDTH + at + QUARTER],
                        packed,
                    ],
                    axis=1,
                )
                pieces[k][:48, :] = jnp.concatenate(
                    [w_fc1[:, WIDTH * r : WIDTH * (r + 1)], lower], axis=0
                )


def merge_kernel(zero, one, two, three, columns):
    parts = [ref[:48, :] for ref in (zero, one, two, three)]
    columns[:, :] = jnp.concatenate(
        [part[:SHARD] for part in parts] + [part[SHARD:] for part in parts], axis=0
    )


def frequency_lanes():
    member = iota((1, 128), 1) & 7
    lanes = jnp.zeros((1, 128), F32)
    for i in range(ROT // 2):
        lanes = jnp.where(member == i, 10000.0 ** (-2.0 * i / ROT), lanes)
    return lanes


def normalized(rows):
    removed = rows - jnp.mean(rows, axis=-1, keepdims=True)
    return removed * lax.rsqrt(jnp.mean(removed * removed, axis=-1, keepdims=True) + epsilon)


def early_kernel(place, zero, one, two, three, tokens, xhat, order, masks, cosine, sine, live):
    order[:, :] = feature_order(place[0], place[1])
    column = iota((1, ROWS), 1).astype(F32)
    line = iota((ROWS, 1), 0).astype(F32)
    member = iota((1, 128), 1) & 63
    for k, piece in enumerate((zero, one, two, three)):
        at = slice(ROWS * k, ROWS * (k + 1))
        if k < 3:
            rows = tokens[:, :] if k == 0 else piece[48:, :]
            xhat[at, :] = normalized(dot(rows, order[:, :]))
        sizes = piece[16:32, 512:640].astype(F32)[12:13, 120:124]
        end = jnp.zeros((1, 1), F32)
        segment_line, segment_column = jnp.zeros((ROWS, 1), F32), jnp.zeros((1, ROWS), F32)
        first_line = jnp.zeros((ROWS, 1), F32)
        for s in range(4):
            size = sizes[:, s : s + 1]
            end = end + size
            first_line = first_line + jnp.where(line >= end, size, 0.0)
            segment_line = segment_line + jnp.where(line >= end, 1.0, 0.0)
            segment_column = segment_column + jnp.where(column >= end, 1.0, 0.0)
        lives = line < end
        mask = (line == column) | (lives & (segment_line == segment_column) & (column <= line))
        masks[at, :] = jnp.where(mask, 1.0, 0.0)
        angle = jnp.where(lives, line - first_line, 0.0) * frequency_lanes()
        cosine[at, :] = jnp.where(member < ROT, jnp.cos(angle), 1.0)
        sine[at, :] = jnp.where(member < ROT, jnp.sin(angle), 0.0) * jnp.where(
            member < ROT // 2, -1.0, 1.0
        )
        live[at, :] = jnp.where(lives, 1.0, 0.0)


def last_kernel(rows, order, xhat):
    xhat[:, :] = normalized(dot(rows[:ROWS, :], order[:, :]))


def turn(values, cosine, sine):
    member = iota((1, 384), 1) & 63
    ahead = pltpu.roll(values, 384 - ROT // 2, 1)
    behind = pltpu.roll(values, ROT // 2, 1)
    partner = jnp.where(member < ROT // 2, ahead, behind)
    return values * jnp.concatenate([cosine] * 3, axis=1) + partner * jnp.concatenate(
        [sine] * 3, axis=1
    )


def forward_kernel(place, xhat, xhat_last, masks, cosine, sine, *refs):
    columns = refs[:2]
    (
        mat_up, mat_qkv, h_one, h_two, act, slope, q_low, k_low, v_low, probs, mixed_slots, gains,
        mixed,
    ) = refs[2:]
    t, q = place[0], place[1]
    for kq in range(8):
        ref, at = columns[kq // 4], 192 * (kq % 4)
        mat_up[96 * kq : 96 * kq + 96, :] = ref[at : at + 96, :]
        mat_qkv[96 * kq : 96 * kq + 96, :] = ref[at + 96 : at + 192, :NARROW]

    slots, plain, of_qkv, of_up = all_places(t, q)
    packed = dot(vector_rows(), mat_qkv[:, VEC_AT:])
    vectors = jnp.concatenate([packed[32 * i : 32 * i + 32] for i in range(5)], axis=1)
    gain_one, bias_one, gain_two, bias_two = [
        spread(vectors[:, SHARD * i : SHARD * i + SHARD], slots) for i in range(4)
    ]
    vec_qkv = spread(vectors[:, 96:168], of_qkv)
    vec_up = spread(vectors[:, 192:288], of_up)
    vec_out = spread(vectors[:, 168:192], plain) + spread(vectors[:, 288:312], plain)
    gains[:, :] = jnp.concatenate([gain_one, gain_two, vec_out, jnp.zeros((5, WIDTH), F32)], axis=0)

    h_two[: 3 * ROWS, :] = (xhat[:, :] * gain_two + bias_two).astype(BF)
    h_two[3 * ROWS :, :] = (xhat_last[:, :] * gain_two + bias_two).astype(BF)
    up = dot(h_two[:, :], mat_up[:, :]) + vec_up
    phi = 0.5 * (1.0 + lax.erf(up * inv_sqrt_two))
    act[:, :] = (up * phi).astype(BF)
    slope[:, :] = phi + up * jnp.exp(-0.5 * up * up) * inv_sqrt_tau

    h_one[: 3 * ROWS, :] = (xhat[:, :] * gain_one + bias_one).astype(BF)
    h_one[3 * ROWS :, :] = (xhat_last[:, :] * gain_one + bias_one).astype(BF)
    qkv = dot(h_one[:, :], mat_qkv[:, :VEC_AT]) + vec_qkv
    turned = turn(qkv[:, : 2 * QUARTER], cosine[:, :], sine[:, :])
    q_low[:, :] = turned[:, :QUARTER].astype(BF)
    k_low[:, :] = turned[:, QUARTER:].astype(BF)
    v_low[:, :] = qkv[:, 2 * QUARTER :].astype(BF)
    for k in range(TP):
        at = slice(ROWS * k, ROWS * (k + 1))
        for head in range(G_HEADS):
            lanes = slice(HEAD * head, HEAD * (head + 1))
            scores = dot(q_low[at, lanes], k_low[at, lanes], 1, 1) * 0.125
            scores = jnp.where(masks[at, :] > 0.0, scores, neg_large)
            exponent = jnp.exp(scores - jnp.max(scores, axis=-1, keepdims=True))
            chances = exponent / jnp.sum(exponent, axis=-1, keepdims=True)
            probs[G_HEADS * k + head] = chances
            mixed[at, lanes] = dot(chances.astype(BF), v_low[at, lanes]).astype(BF)
    mixed_slots[:, :] = dot(mixed[:, :], head_order(q)).astype(BF)


def share_kernel(place, act, mixed_slots, *refs):
    tails, down, out_mat, shares = refs[:2], refs[2], refs[3], refs[4:]
    q = place[1]
    for kq in range(8):
        ref, at = tails[kq // 4], 128 * (kq % 4)
        first = pl.multiple_of((q ^ kq) * 96, 32)
        down[pl.ds(first, 96), :] = ref[at : at + 96, :]
        out_mat[32 * kq : 32 * kq + 32, :] = ref[at + 96 : at + 128, :]
    total = dot(act[:, :], down[:, :]) + dot(mixed_slots[:, :], out_mat[:, :])
    for k in range(TP):
        shares[k][:, :] = total[ROWS * k : ROWS * (k + 1)].astype(shares[k].dtype)


def upstream_kernel(place, *refs):
    cots = refs[:4]
    (
        live, h_two, act, slope, mixed_slots, down, out_mat, d_up, d_mixed, keep, send,
        upstream, grad_down,
    ) = refs[4:]
    q = place[1]
    for k in range(TP):
        at = slice(ROWS * k, ROWS * (k + 1))
        last = cots[k].shape[0]
        upstream[at, :] = (cots[k][last - ROWS :, :].astype(F32) * live[at, :]).astype(BF)
    d_up[:, :] = (dot(upstream[:, :], down[:, :], 1, 1) * slope[:, :]).astype(BF)
    grad_up = dot(h_two[:, :], d_up[:, :], 0, 0)
    grad_down[:, :] = dot(act[:, :], upstream[:, :], 0, 0)
    grad_out = dot(mixed_slots[:, :], upstream[:, :], 0, 0)
    for kq in range(8):
        target = keep if kq < 4 else send
        at = 224 * (kq % 4)
        first = pl.multiple_of((q ^ kq) * 96, 32)
        target[at : at + 96, :] = grad_down[pl.ds(first, 96), :].astype(target.dtype)
        target[at + 96 : at + 128, :] = grad_out[32 * kq : 32 * kq + 32].astype(target.dtype)
        target[at + 128 : at + 224, :] = grad_up[96 * kq : 96 * kq + 96].astype(target.dtype)
    d_slots = dot(upstream[:, :], out_mat[:, :], 1, 1).astype(BF)
    d_mixed[:, :] = dot(d_slots, head_order(q), 1, 1).astype(BF)


def attention_kernel(
    q_low, k_low, v_low, probs, d_mixed, cosine, sine, d_qkv, d_turned
):
    for k in range(TP):
        at = slice(ROWS * k, ROWS * (k + 1))
        for head in range(G_HEADS):
            lanes = slice(HEAD * head, HEAD * (head + 1))
            chances = probs[G_HEADS * k + head]
            d_out = d_mixed[at, lanes]
            d_probs = dot(d_out, v_low[at, lanes], 1, 1)
            delta = jnp.sum(chances * d_probs, axis=-1, keepdims=True)
            d_scores = (chances * (d_probs - delta)).astype(BF)
            d_turned[at, lanes] = dot(d_scores, k_low[at, lanes]) * 0.125
            d_turned[at, QUARTER + HEAD * head : QUARTER + HEAD * (head + 1)] = (
                dot(d_scores, q_low[at, lanes], 0, 0) * 0.125
            )
            d_qkv[at, 2 * QUARTER + HEAD * head : 2 * QUARTER + HEAD * (head + 1)] = dot(
                chances.astype(BF), d_out, 0, 0
            ).astype(BF)
    d_qkv[:, : 2 * QUARTER] = turn(d_turned[:, :], cosine[:, :], -sine[:, :]).astype(BF)


def backward_kernel(
    place, xhat, xhat_last, order, mat_up, mat_qkv, h_one, d_up, d_qkv, gains, cot, live, *refs
):
    shares, (keep, send) = refs[:4], refs[4:]
    t, q = place[0], place[1]
    d_one = dot(d_qkv[:, :], mat_qkv[:, :VEC_AT], 1, 1)
    d_two = dot(d_up[:, :], mat_up[:, :], 1, 1)
    share = (d_one * gains[0:1, :] + d_two * gains[1:2, :]).astype(BF)
    share = dot(share, order[:, :], 1, 1)
    for k in range(TP):
        shares[k][:, :] = share[ROWS * k : ROWS * (k + 1)].astype(shares[k].dtype)

    slots, plain, of_qkv, of_up = all_places(t, q)

    def total(rows):
        return jnp.sum(rows, axis=0, keepdims=True)

    def with_xhat(rows):
        return total(rows[: 3 * ROWS] * xhat[:, :]) + total(rows[3 * ROWS :] * xhat_last[:, :])

    vectors = jnp.concatenate(
        [
            collect(with_xhat(d_one), slots),
            collect(total(d_one), slots),
            collect(with_xhat(d_two), slots),
            collect(total(d_two), slots),
            collect(total(cot[:, :].astype(F32) * live[:ROWS, :]), plain),
            collect(total(d_qkv[:, :].astype(F32)), of_qkv),
            collect(total(d_up[:, :].astype(F32)), of_up),
            jnp.zeros((32, 32), F32),
        ],
        axis=1,
    ).astype(BF)
    packed = jnp.concatenate([vectors[:, 64 * i : 64 * i + 64] for i in range(5)], axis=0)
    grads = jnp.concatenate(
        [dot(h_one[:, :], d_qkv[:, :], 0, 0), dot(vector_rows(), packed, 0, 0)], axis=1
    )
    keep[:, :] = grads[:384]
    send[:, :] = grads[384:].astype(BF)


def columns_kernel(place, zero, one, two, three, qkv, up, *vectors):
    t = place[0]
    parts = [zero[:, :]] + [ref[:, :].astype(F32) for ref in (one, two, three)]
    for rank in range(TP):

        @pl.when(t == rank)
        def _(rank=rank):
            by_rank = [parts[rank ^ s] for s in range(TP)]
            up[:, :] = jnp.concatenate([item[:, :WIDTH] for item in by_rank], axis=1)
            qkv[:, :] = jnp.concatenate(
                [
                    item[:, WIDTH + QUARTER * i : WIDTH + QUARTER * (i + 1)]
                    for i in range(3)
                    for item in by_rank
                ],
                axis=1,
            )

    packed = sum(item[:8, WIDTH + VEC_AT :] for item in parts)
    row = jnp.concatenate([packed[i : i + 1] for i in range(5)], axis=1)
    at = 0
    for ref in vectors[:-1]:
        size = ref.shape[1]
        ref[:, :] = row[:, at : at + size]
        at += size
    vectors[-1][:, :] = row[:, 4 * SHARD : 5 * SHARD]


def output_kernel(zero, one, two, three, tokens, live, gains, output):
    share = zero[:, :] + one[:, :].astype(F32) + two[:, :].astype(F32) + three[:, :].astype(F32)
    output[:, :] = (live[:ROWS, :] * (tokens[:, :].astype(F32) + share + gains[2:3, :])).astype(BF)


def input_kernel(zero, one, two, three, tokens, cot, live, grad):
    e = zero[:, :] + one[:, :].astype(F32) + two[:, :].astype(F32) + three[:, :].astype(F32)
    rows = tokens[:, :].astype(F32)
    removed = rows - jnp.mean(rows, axis=-1, keepdims=True)
    rstd = lax.rsqrt(jnp.mean(removed * removed, axis=-1, keepdims=True) + epsilon)
    xhat = removed * rstd
    dx = rstd * (
        e - jnp.mean(e, axis=-1, keepdims=True) - xhat * jnp.mean(e * xhat, axis=-1, keepdims=True)
    )
    grad[:, :] = cot[:, :].astype(F32) * live[:ROWS, :] + dx


def call(kernel, name, outs, *args, scratch=(), mib=16, weight=1):
    space = [pl.BlockSpec(memory_space=pltpu.VMEM)] * len(args)
    if args[0].dtype == jnp.int32:
        space[0] = pl.BlockSpec(memory_space=pltpu.SMEM)
    shapes = [jax.ShapeDtypeStruct(shape, kind) for shape, kind in outs]
    return pl.pallas_call(
        kernel,
        name=name,
        out_shape=shapes,
        in_specs=space,
        out_specs=[pl.BlockSpec(memory_space=pltpu.VMEM)] * len(shapes),
        scratch_shapes=[pltpu.VMEM(shape, kind) for shape, kind in scratch],
        cost_estimate=pl.CostEstimate(flops=weight * 10**9, transcendentals=0, bytes_accessed=weight * 10**6),
        compiler_params=pltpu.CompilerParams(vmem_limit_bytes=mib * 1024 * 1024),
    )(*args)


def after(array, *others):
    return lax.optimization_barrier((array, others))[0]


def xor_permutes(block, axis, count):
    return [lax.ppermute(block, axis, xor_pairs(count, k)) for k in range(1, 4)]


def plane_pair(keep, send):
    return keep + lax.ppermute(send, "dq", xor_pairs(2, 1)).astype(F32)


def plane_relay(pair):
    rows = pair.shape[0] // 4
    three = pair[3 * rows :].astype(BF)
    upper = lax.ppermute(three[: rows // 2], "fsdp", xor_pairs(4, 1))
    lower = lax.ppermute(three[rows // 2 :], "fsdp", xor_pairs(4, 2))
    return upper, lower


def plane_last(pair, upper, lower):
    rows = pair.shape[0] // 4
    half = rows // 2
    mine, one, two = [pair[rows * k : rows * (k + 1)] for k in range(3)]
    two = jnp.concatenate([two[:half] + upper.astype(F32), two[half:]], axis=0)
    one = jnp.concatenate([one[:half], one[half:] + lower.astype(F32)], axis=0)
    one = lax.ppermute(one.astype(BF), "fsdp", xor_pairs(4, 1))
    two = lax.ppermute(two.astype(BF), "fsdp", xor_pairs(4, 2))
    return mine + one.astype(F32) + two.astype(F32)


def plane_local(
    tokens, lengths, ln_attn_gain, ln_attn_bias, ln_mlp_gain, ln_mlp_bias, w_qkv, b_qkv,
    w_out, b_out, w_fc1, b_fc1, w_fc2, b_fc2, cotangent,
):
    t = lax.axis_index("t")
    q = lax.axis_index("dq") * 4 + lax.axis_index("fsdp")
    place = jnp.stack([t, q]).astype(jnp.int32)
    vector = jnp.concatenate(
        [
            ln_attn_gain, ln_attn_bias, ln_mlp_gain, ln_mlp_bias, b_qkv, b_out, b_fc1, b_fc2,
            lengths[0].astype(BF), jnp.zeros((68,), BF),
        ]
    )
    block = (ROWS, WIDTH)
    piece = ((48, WIDTH), BF)
    piece_rows = ((48 + ROWS, WIDTH), BF)
    tail = jnp.concatenate([w_fc2, w_out, jnp.zeros((8, WIDTH), BF)], axis=0)
    weights = jnp.concatenate([w_fc1, w_qkv], axis=1)
    pieces = call(
        prepare_kernel, "prepare", [piece, piece_rows, piece_rows, piece],
        place, weights, vector.astype(F32)[None], tokens,
        weight=10,
    )
    prepared = pieces
    pieces = exchange_t(pieces)
    token_one = pieces[1]
    both = after(jnp.concatenate([tokens, cotangent], axis=0), token_one)
    rows_three = lax.ppermute(both, "t", xor_pairs(TP, 3))
    tail = after(tail, prepared)
    tail_one = lax.ppermute(tail, "fsdp", xor_pairs(4, 1))
    tail_two = lax.ppermute(tail, "fsdp", xor_pairs(4, 2))
    tail_three = lax.ppermute(after(tail, tail_one), "fsdp", xor_pairs(4, 3))
    (columns,) = call(merge_kernel, "merge", [((192, WIDTH), BF)], *pieces, weight=10)
    columns = after(columns, tail_one, tail_two, tail_three)
    arrived = xor_permutes(columns, "fsdp", 4)
    columns = jnp.concatenate([columns] + arrived, axis=0)
    columns = [columns, lax.ppermute(columns, "dq", xor_pairs(2, 1))]
    wide = (COUNT, WIDTH)
    square = ((COUNT, 128), F32)
    xhat, order, masks, cosine, sine, lives = call(
        early_kernel,
        "early",
        [((3 * ROWS, WIDTH), F32), ((WIDTH, WIDTH), BF), square, square, square, ((COUNT, 1), F32)],
        place, *pieces, tokens,
        weight=10,
    )
    (xhat_last,) = call(
        last_kernel, "last", [(block, F32)], rows_three, order, weight=5
    )
    cot_one = lax.ppermute(after(cotangent, xhat_last), "t", xor_pairs(TP, 1))
    cot_two = lax.ppermute(after(cotangent, xhat_last), "t", xor_pairs(TP, 2))
    cot_slots = [cot_one, cot_two, rows_three]
    third = (COUNT, QUARTER)
    (
        mat_up, mat_qkv, h_one, h_two, act, slope, q_low, k_low, v_low, probs, mixed_slots, gains,
    ) = call(
        forward_kernel,
        "forward",
        [
            ((WIDTH, WIDTH), BF), ((WIDTH, NARROW), BF),
            (wide, BF), (wide, BF), (wide, BF), (wide, F32), (third, BF), (third, BF),
            (third, BF), ((HEADS, ROWS, ROWS), F32), ((COUNT, 256), BF), ((8, WIDTH), F32),
        ],
        place, xhat, xhat_last, masks, cosine, sine, *columns,
        scratch=[(third, BF)],
        weight=100,
    )
    tail = jnp.concatenate([tail, tail_one, tail_two, tail_three], axis=0)
    tail = [tail, lax.ppermute(tail, "dq", xor_pairs(2, 1))]
    shares = [(block, F32)] + [(block, BF)] * 3
    down, out_mat, *out = call(
        share_kernel, "share", [((WIDTH, WIDTH), BF), ((256, WIDTH), BF)] + shares,
        place, act, mixed_slots, *tail,
        weight=10,
    )
    out = exchange_t(out)
    d_up, d_mixed, tail_keep, tail_send = call(
        upstream_kernel,
        "upstream",
        [(wide, BF), (third, BF), ((896, WIDTH), F32), ((896, WIDTH), BF)],
        place, cotangent, *cot_slots, lives, h_two, act, slope, mixed_slots, down, out_mat,
        scratch=[(wide, BF), ((WIDTH, WIDTH), F32)],
        weight=40,
    )
    tail_pair = plane_pair(tail_keep, tail_send)
    (d_qkv,) = call(
        attention_kernel, "attention", [((COUNT, 3 * QUARTER), BF)],
        q_low, k_low, v_low, probs, d_mixed, cosine, sine,
        scratch=[((COUNT, 2 * QUARTER), F32)],
        weight=50,
    )
    tail_got = plane_relay(tail_pair)
    d_qkv = after(d_qkv, tail_pair, out[1])
    *e, col_keep, col_send = call(
        backward_kernel,
        "backward",
        shares + [((384, NARROW), F32), ((384, NARROW), BF)],
        place, xhat, xhat_last, order, mat_up, mat_qkv, h_one, d_up, d_qkv, gains, cotangent, lives,
        weight=40,
    )
    col_pair = plane_pair(col_keep, after(col_send, tail_got, out[2:]))
    col_got = plane_relay(col_pair)
    e = [after(item, out) for item in e]
    e[3] = after(e[3], col_pair)
    e = exchange_t(e)
    col_sum = plane_last(col_pair, *col_got)
    tail_sum = plane_last(after(tail_pair, col_got), *tail_got)
    col_sum = jnp.concatenate([tail_sum[128:], col_sum], axis=1)
    low_sum = col_sum.astype(BF)
    back = [low_sum[SHARD * k : SHARD * (k + 1)] for k in range(TP)]
    arrived = exchange_t(back)
    tail_sum = after(tail_sum, low_sum)
    (output,) = call(
        output_kernel, "output", [(block, BF)], *out, tokens, after(lives, low_sum), gains,
        weight=10,
    )
    (grad_tokens,) = call(
        input_kernel, "input_gradient", [(block, F32)], *e, tokens, cotangent, lives,
        weight=10,
    )
    sizes = [SHARD] * 5 + [3 * SHARD, 4 * SHARD, SHARD]
    shard_qkv, shard_up, *vectors = call(
        columns_kernel, "columns",
        [((SHARD, 3 * WIDTH), F32), ((SHARD, 4 * WIDTH), F32)] + [((1, n), F32) for n in sizes],
        place, col_sum[:SHARD], *arrived[1:],
    )
    g_one, b_one, g_two, b_two, branch, qkv_bias, up_bias, again = [item[0] for item in vectors]
    return (
        output, grad_tokens, g_one, b_one, g_two, b_two, shard_qkv, qkv_bias,
        tail_sum[96 : 96 + SHARD], branch, shard_up, up_bias, tail_sum[:96], again,
    )


def local(
    sizes,
    tokens,
    lengths,
    ln_attn_gain,
    ln_attn_bias,
    ln_mlp_gain,
    ln_mlp_bias,
    w_qkv,
    b_qkv,
    w_out,
    b_out,
    w_fc1,
    b_fc1,
    w_fc2,
    b_fc2,
    cotangent,
):
    if sizes == (2, 4) and w_qkv.shape == (SHARD, 3 * WIDTH) and tokens.shape == (ROWS, WIDTH):
        return plane_local(
            tokens, lengths, ln_attn_gain, ln_attn_bias, ln_mlp_gain, ln_mlp_bias, w_qkv, b_qkv,
            w_out, b_out, w_fc1, b_fc1, w_fc2, b_fc2, cotangent,
        )
    t = lax.axis_index("t")
    q = lax.axis_index("dq") * sizes[1] + lax.axis_index("fsdp")
    qs = sizes[0] * sizes[1]
    rows, width = tokens.shape
    shard = w_qkv.shape[0]
    part = width // TP
    hidden = w_fc1.shape[1] // TP
    units = w_fc2.shape[0]
    heads = HEADS // TP

    vectors = jnp.concatenate(
        [
            item.reshape(shard, -1)
            for item in (
                ln_attn_gain, ln_attn_bias, ln_mlp_gain, ln_mlp_bias, b_qkv, b_out, b_fc1, b_fc2
            )
        ],
        axis=1,
    )
    n_vec = vectors.shape[1]
    low_lengths = jnp.broadcast_to(lengths.astype(BF), (shard, lengths.shape[1]))
    small = jnp.concatenate([vectors, low_lengths], axis=1)
    qkv_parts = w_qkv.reshape(shard, 3, TP, part)
    fc1_parts = w_fc1.reshape(shard, TP, hidden)
    pieces = [
        jnp.concatenate(
            [
                pick(qkv_parts, t ^ k, 2).reshape(shard, 3 * part),
                small,
                pick(fc1_parts, t ^ k, 1),
            ],
            axis=1,
        )
        for k in range(TP)
    ]
    pieces = exchange_t(pieces)
    at = 3 * part
    group_lengths = [piece[0, at + n_vec : at + n_vec + 4].astype(jnp.int32) for piece in pieces]
    mine = jnp.stack(unxor(pieces, t))
    columns = gather_q(mine, q, sizes)
    columns = columns.transpose(1, 0, 2, 3).reshape(width, -1)
    mat_qkv = columns[:, : 3 * part]
    vecs = columns[:, at : at + n_vec].astype(F32)
    mat_up = columns[:, at + small.shape[1] :]
    tail = gather_q(jnp.concatenate([w_fc2, w_out], axis=0), q, sizes)
    mat_down = tail[:, :units].reshape(qs * units, width)
    mat_out = tail[:, units:].reshape(part, width)

    vecs_t = vecs.T
    gain_one, bias_one, gain_two, bias_two = vecs_t[0], vecs_t[1], vecs_t[2], vecs_t[3]
    all_b_qkv = vecs[:, 4:7].reshape(3, TP, part)
    vec_qkv = pick(all_b_qkv, t, 1).reshape(3 * part)
    vec_out = vecs_t[7]
    vec_up = pick(vecs[:, 8:12].reshape(TP, hidden), t)
    vec_down = vecs_t[12]

    token_slots = gather_t(tokens, t)
    upstream_slots = gather_t(cotangent, t)
    layouts = [layout(item, rows) for item in group_lengths]
    live = jnp.concatenate([item[0] for item in layouts])[:, None]
    attn_mask = jnp.stack([item[1] for item in layouts])[:, None]
    cosine = jnp.concatenate([item[2] for item in layouts])
    sine = jnp.concatenate([item[3] for item in layouts])
    resid = jnp.concatenate(token_slots).astype(F32)
    upstream_low = jnp.concatenate(upstream_slots) * live.astype(BF)

    center = jnp.mean(resid, axis=-1, keepdims=True)
    removed = resid - center
    rstd = lax.rsqrt(jnp.mean(removed * removed, axis=-1, keepdims=True) + epsilon)
    xhat = removed * rstd
    low_one = (xhat * gain_one + bias_one).astype(BF)
    low_two = (xhat * gain_two + bias_two).astype(BF)

    up_rows = contract(low_two, mat_up, 1, 0) + vec_up
    phi = 0.5 * (1.0 + lax.erf(up_rows * inv_sqrt_two))
    act_low = (up_rows * phi).astype(BF)
    slope = phi + up_rows * jnp.exp(-0.5 * up_rows * up_rows) * inv_sqrt_tau
    mlp_share = contract(act_low, mat_down, 1, 0)
    grad_down = contract(act_low, upstream_low, 0, 0)
    d_up_low = (contract(upstream_low, mat_down, 1, 1) * slope).astype(BF)
    grad_up = contract(low_two, d_up_low, 0, 0)
    grad_up_bias = jnp.sum(d_up_low.astype(F32), axis=0)
    d_h2 = contract(d_up_low, mat_up, 1, 1)

    count = TP * rows
    qkv = (contract(low_one, mat_qkv, 1, 0) + vec_qkv).reshape(count, 3, heads, HEAD)
    q_low = rotate(qkv[:, 0], cosine, sine).astype(BF).reshape(TP, rows, heads, HEAD)
    k_low = rotate(qkv[:, 1], cosine, sine).astype(BF).reshape(TP, rows, heads, HEAD)
    v_low = qkv[:, 2].astype(BF).reshape(TP, rows, heads, HEAD)
    scores = jnp.einsum("gqhd,gkhd->ghqk", q_low, k_low, preferred_element_type=F32) * 0.125
    scores = jnp.where(attn_mask, scores, neg_large)
    exponent = jnp.exp(scores - jnp.max(scores, axis=-1, keepdims=True))
    probs = exponent / jnp.sum(exponent, axis=-1, keepdims=True)
    probs_low = probs.astype(BF)
    mixed = jnp.einsum("ghqk,gkhd->gqhd", probs_low, v_low, preferred_element_type=F32)
    mixed_low = mixed.reshape(count, part).astype(BF)
    out_share = (mlp_share + contract(mixed_low, mat_out, 1, 0)).reshape(TP, rows, width)
    out_sum = scatter_t([out_share[k] for k in range(TP)])
    output = live[:rows] * (resid[:rows] + out_sum + vec_out + vec_down)

    grad_out = contract(mixed_low, upstream_low, 0, 0)
    d_mixed = contract(upstream_low, mat_out, 1, 1).astype(BF).reshape(TP, rows, heads, HEAD)
    d_probs = jnp.einsum("gqhd,gkhd->ghqk", d_mixed, v_low, preferred_element_type=F32)
    d_values = jnp.einsum("ghqk,gqhd->gkhd", probs_low, d_mixed, preferred_element_type=F32)
    delta = jnp.sum(probs * d_probs, axis=-1, keepdims=True)
    d_scores = (probs * (d_probs - delta)).astype(BF)
    d_query = jnp.einsum("ghqk,gkhd->gqhd", d_scores, k_low, preferred_element_type=F32) * 0.125
    d_keys = jnp.einsum("ghqk,gqhd->gkhd", d_scores, q_low, preferred_element_type=F32) * 0.125
    d_query = rotate(d_query.reshape(count, heads, HEAD), cosine, -sine).reshape(count, part)
    d_keys = rotate(d_keys.reshape(count, heads, HEAD), cosine, -sine).reshape(count, part)
    d_qkv = jnp.concatenate([d_query, d_keys, d_values.reshape(count, part)], axis=1).astype(BF)
    grad_qkv = contract(low_one, d_qkv, 0, 0)
    grad_qkv_bias = jnp.sum(d_qkv.astype(F32), axis=0)
    d_h1 = contract(d_qkv, mat_qkv, 1, 1)

    e_share = (d_h1 * gain_one + d_h2 * gain_two).reshape(TP, rows, width)
    e_sum = scatter_t([e_share[k] for k in range(TP)])
    own_xhat = xhat[:rows]
    dx = rstd[:rows] * (
        e_sum
        - jnp.mean(e_sum, axis=-1, keepdims=True)
        - own_xhat * jnp.mean(e_sum * own_xhat, axis=-1, keepdims=True)
    )
    own_upstream = upstream_low[:rows].astype(F32)
    grad_tokens = own_upstream + dx

    zero_qkv = jnp.zeros((3, TP, part), F32)
    full_b_qkv = lax.dynamic_update_index_in_dim(
        zero_qkv, grad_qkv_bias.reshape(3, 1, part), t, 1
    ).reshape(width, 3)
    zero_up = jnp.zeros((TP, hidden), F32)
    full_b_up = lax.dynamic_update_index_in_dim(zero_up, grad_up_bias[None], t, 0).reshape(width, 4)
    lanes = jnp.stack(
        [
            jnp.sum(d_h1 * xhat, axis=0),
            jnp.sum(d_h1, axis=0),
            jnp.sum(d_h2 * xhat, axis=0),
            jnp.sum(d_h2, axis=0),
            jnp.sum(own_upstream, axis=0),
        ],
        axis=1,
    )
    vec_grads = jnp.concatenate([lanes, full_b_qkv, full_b_up], axis=1)

    tail_grads = jnp.concatenate(
        [grad_down.reshape(qs, units, width), grad_out.reshape(qs, shard, width)], axis=1
    )
    tail_sum = scatter_q(tail_grads, q, sizes)
    shard_down, shard_out = tail_sum[:units], tail_sum[units:]
    column_grads = jnp.concatenate([grad_qkv, vec_grads, grad_up], axis=1)
    column_grads = column_grads.reshape(TP, qs, shard, -1).transpose(1, 0, 2, 3)
    column_sum = scatter_q(column_grads, q, sizes)
    low_sum = column_sum.astype(BF)
    got = exchange_t([pick(low_sum, t ^ k) for k in range(TP)])
    got = [pick(column_sum, t)] + [item.astype(F32) for item in got[1:]]
    vec_sum = sum(item[:, at : at + 12] for item in got)
    got = jnp.stack(unxor(got, t))
    shard_qkv = (
        got[:, :, : 3 * part].reshape(TP, shard, 3, part).transpose(1, 2, 0, 3).reshape(shard, -1)
    )
    shard_up = got[:, :, at + 12 :].transpose(1, 0, 2).reshape(shard, -1)
    shard_branch_bias = vec_sum[:, 4]
    return (
        output.astype(BF),
        grad_tokens,
        vec_sum[:, 0],
        vec_sum[:, 1],
        vec_sum[:, 2],
        vec_sum[:, 3],
        shard_qkv,
        vec_sum[:, 5:8].reshape(-1),
        shard_out,
        shard_branch_bias,
        shard_up,
        vec_sum[:, 8:12].reshape(-1),
        shard_down,
        shard_branch_bias,
    )


def solution(mesh):
    nd, nf = mesh.shape["dp"], mesh.shape["fsdp"]
    sizes = (nd // TP, nf)
    inner = Mesh(mesh.devices.reshape((TP,) + sizes), ("t", "dq", "fsdp"))
    axes = ("t", "dq", "fsdp")
    matrix, vector = P(axes, None), P(axes)
    return jax.shard_map(
        lambda *args: local(sizes, *args),
        mesh=inner,
        in_specs=(
            matrix, matrix, vector, vector, vector, vector, matrix, vector,
            matrix, vector, matrix, vector, matrix, vector, matrix,
        ),
        out_specs=(
            matrix, matrix, vector, vector, vector, vector, matrix, vector,
            matrix, vector, matrix, vector, matrix, vector,
        ),
        check_vma=False,
    )
```
